32 devices in a mesh: dom: 8 (over z, x), rep: 4 (over y, core).
Axes of the slice: x: 2, y: 2, z: 4, core: 2. Of those that a mesh axis runs over, the one named last changes fastest.
Arguments:
- entities: bfloat16 [8192, 512], P('dom'), may hold values from -60 to 60
- relations: bfloat16 [4, 512, 512], replicated, may hold values from -2 to 2
- head_local: int32 [16384], P(('dom', 'rep')), may hold values from 0 to 1023
- rel_ids: int32 [16384], P(('dom', 'rep')), may hold values from 0 to 3
- tail_part: int32 [16384, 1], P(('dom', 'rep')), may hold values from 0 to 7; in each aligned block of 512 rows (0 to 511, 512 to 1023, ...) at most 128 rows name the same one
- tail_local: int32 [16384], P(('dom', 'rep')), may hold values from 0 to 1023
- neg_local: int32 [256], P('dom'), may hold values from 0 to 1023
Outputs:
- entity_grad: float32 [8192, 512], P('dom')
- relation_grad: float32 [4, 512, 512], replicated
- edge_loss: float32 [16384], P(('dom', 'rep'))
The draws below stay inside these ranges and needn't reach their ends.
Inputs may be any that keep to these rules, and one draw needn't show every extreme that they name: `tail_part`: in the 512 edges of one device no partition is named by more than 128 edges, a bound that some block reaches.
All inputs are finite; a program needn't handle non-finite values.
Results may differ from the reference program's by a relative error of at most 0.012.
The reference program's roundings to bfloat16 on the way (of `queries`, `prob_neg` and `query_grad`) count: a program that leaves them out, or rounds other values in their place, can miss the bound.
Values may be sent and summed in bfloat16 or wider, within the bound.
No kernel may reach another device: no remote copies, remote signals or barrier semaphores. Data moves between devices by JAX's collectives and lax.ppermute only.
A program may use at most 64 MiB of HBM per device.

```python
import math
import jax
import jax.numpy as jnp
import numpy as np
from jax import lax

D = 512
REL = 4
ENT_DEV = 1024
E_DEV = 512
NEG_DEV = 32
ENT = 8192
EDGES = 16384
NEG = 256
CAP = 128
N_DOM = 8
N_REP = 4


def draw_entities(key, part):
    first = jax.random.fold_in(key, 0)
    values = jnp.clip(jax.random.normal(first, (ENT_DEV * N_DOM, D), jnp.float32), -6.0, 6.0)
    return values.astype(jnp.bfloat16)


def draw_relations(key, part):
    first, second = jax.random.split(key)
    spread = 0.8 / math.sqrt(D)
    noise = jnp.clip(jax.random.normal(first, (REL, D, D), jnp.float32), -4.0, 4.0) * spread
    diagonal = jax.random.uniform(second, (REL, 1, 1), jnp.float32, 0.6, 1.4)
    identity = (jnp.arange(D)[:, None] == jnp.arange(D)[None, :]).astype(jnp.float32)
    return (diagonal * identity + noise).astype(jnp.bfloat16)


def touch_ends(values, own_key, smallest, top_value):
    extent = values.shape
    place = [jax.random.randint(jax.random.fold_in(own_key, axis), (), 0, extent[axis]) for axis in range(len(extent))]
    values = values.at[tuple(place)].set(smallest)
    longest = extent.index(max(extent))
    place[longest] = (place[longest] + 1) % extent[longest]
    return values.at[tuple(place)].set(top_value)


def deal_out(rng, own, number, rows, number_of, top, limit, slope):
    sequence = jax.random.permutation(rng, number_of)
    crowded, common = portions_of(number_of, rows * top, limit, slope, True), portions_of(number_of, rows * top, limit, slope, False)
    places = jnp.arange(number_of)

    def named(sizes, offset_by):
        used = int((sizes > 0).sum())
        fixed = max(1, used // 4)
        moved = fixed + (places - fixed + offset_by * (used - fixed)) % max(1, number_of - fixed)
        return jnp.zeros((number_of,), jnp.int32).at[sequence[jnp.where(places < fixed, places, moved)]].set(jnp.asarray(sizes, jnp.int32))

    sizes = jnp.where(number % 4 == 0, named(crowded, number // 4), named(common, number - number // 4 - 1))
    mixed = jax.random.permutation(jax.random.fold_in(own, 3), number_of)
    giver, sink = mixed[0:number_of // 2 * 2:2], mixed[1:number_of // 2 * 2:2]
    slack = jnp.minimum(sizes[giver] - 1, limit - sizes[sink]) // 2
    slack = jnp.where((giver == sequence[0]) | (sink == sequence[0]) | (sizes[sink] == 0), 0, jnp.maximum(slack, 0))
    moved = jax.random.randint(jax.random.fold_in(own, 4), (number_of // 2,), 0, 1 << 20) % (slack + 1)
    sizes = sizes.at[giver].add(-moved).at[sink].add(moved)
    items = jnp.searchsorted(jnp.cumsum(sizes), jnp.arange(rows * top), side="right").astype(jnp.int32)
    table = items.reshape(top, rows).T
    table = table[jax.random.permutation(jax.random.fold_in(own, 1), rows)]
    offset_by = jax.random.randint(jax.random.fold_in(own, 2), (rows, 1), 0, top)
    return jnp.take_along_axis(table, (jnp.arange(top)[None, :] + offset_by) % top, axis=1)


def portions_of(number_of, total, bound, lean, full):
    portions = [(1 << 20) // math.isqrt(grade ** lean) + 1 for grade in range(1, number_of + 1)]
    largest = bound if full else min(bound, max(-(-total // number_of), total * portions[0] // sum(portions)))
    least = 1 if total - largest >= number_of - 1 else 0
    holding, surplus = [largest] + [least] * (number_of - 1), total - largest - least * (number_of - 1)
    while surplus > 0:
        free = [i for i in range(1, number_of) if holding[i] < largest] or [i for i in range(1, number_of) if holding[i] < bound]
        whole, remaining = sum([portions[i] for i in free]), surplus
        for i in free:
            extra = min(bound - holding[i], max(1, remaining * portions[i] // whole), surplus)
            holding[i] = holding[i] + extra
            surplus = surplus - extra
    return np.array(holding)


def setup_inputs(seed: int = 0) -> dict:
    streams_of = jax.random.split(jax.random.key(seed), 8)
    entities = draw_entities(jax.random.fold_in(streams_of[7], 71), 0)
    relations = draw_relations(jax.random.fold_in(streams_of[7], 71), 0)
    head_local = touch_ends(jax.random.randint(streams_of[2], (EDGES,), 0, ENT_DEV), jax.random.fold_in(streams_of[2], 1), 0, ENT_DEV - 1).astype(jnp.int32)
    rel_ids = touch_ends(jax.random.randint(streams_of[3], (EDGES,), 0, REL), jax.random.fold_in(streams_of[3], 1), 0, REL - 1).astype(jnp.int32)
    tail_part_keys = jax.random.split(jax.random.fold_in(streams_of[4], 1), EDGES // E_DEV)
    tail_part_turns = jax.random.permutation(jax.random.fold_in(streams_of[4], 3), EDGES // E_DEV)
    tail_part = jax.vmap(lambda own, number: deal_out(jax.random.fold_in(streams_of[4], 2), own, number, E_DEV, N_DOM, 1, CAP, 2))(tail_part_keys, tail_part_turns).reshape((EDGES, 1))
    tail_local = touch_ends(jax.random.randint(streams_of[5], (EDGES,), 0, ENT_DEV), jax.random.fold_in(streams_of[5], 1), 0, ENT_DEV - 1).astype(jnp.int32)
    neg_local = touch_ends(jax.random.randint(streams_of[6], (NEG,), 0, ENT_DEV), jax.random.fold_in(streams_of[6], 1), 0, ENT_DEV - 1).astype(jnp.int32)
    return dict(entities=entities, relations=relations, head_local=head_local, rel_ids=rel_ids, tail_part=tail_part, tail_local=tail_local, neg_local=neg_local)


def edge_block(queries, tail_embed, negatives, factor):
    positive = lax.optimization_barrier(jnp.sum(queries.astype(jnp.float32) * tail_embed.astype(jnp.float32), axis=1)) * factor
    scores = lax.dot_general(queries, negatives, (((1,), (1,)), ((), ())), preferred_element_type=jnp.float32) * factor
    row_max = jnp.maximum(positive, lax.optimization_barrier(jnp.max(scores, axis=1)))
    exp_pos = jnp.exp(positive - row_max)
    exp_neg = jnp.exp(scores - row_max[:, None])
    partition_sum = exp_pos + lax.optimization_barrier(jnp.sum(exp_neg, axis=1))
    edge_loss = jnp.log(partition_sum) + row_max - positive
    prob_pos = exp_pos / partition_sum
    prob_neg = (exp_neg / partition_sum[:, None]).astype(jnp.bfloat16)
    mixed = jnp.dot(prob_neg, negatives, preferred_element_type=jnp.float32)
    query_grad = (factor * ((prob_pos - 1.0)[:, None] * tail_embed.astype(jnp.float32) + mixed)).astype(jnp.bfloat16)
    tail_grad = factor * (prob_pos - 1.0)[:, None] * queries.astype(jnp.float32)
    neg_grad = factor * lax.dot_general(prob_neg, queries, (((0,), (0,)), ((), ())), preferred_element_type=jnp.float32)
    return (edge_loss, query_grad, tail_grad, neg_grad)

def reference(entities, relations, head_local, rel_ids, tail_part, tail_local, neg_local):
    factor = 1.0 / math.sqrt(D)
    neg_ids = jnp.arange(NEG, dtype=jnp.int32) // NEG_DEV * ENT_DEV + neg_local
    negatives = jnp.take(entities, neg_ids, axis=0)
    blocks = EDGES // E_DEV

    def one_block(carry, block):
        entity_acc, relation_acc, negative_acc = carry
        start = (block * E_DEV).astype(jnp.int32)
        owner = (block // N_REP).astype(jnp.int32)
        head_ids = owner * ENT_DEV + lax.dynamic_slice_in_dim(head_local, start, E_DEV)
        rel_block = lax.dynamic_slice_in_dim(rel_ids, start, E_DEV)
        tail_ids = lax.dynamic_slice_in_dim(tail_part[:, 0], start, E_DEV) * ENT_DEV + lax.dynamic_slice_in_dim(tail_local, start, E_DEV)
        head_rows = jnp.take(entities, head_ids, axis=0)
        tail_embed = jnp.take(entities, tail_ids, axis=0)
        query_sum = jnp.zeros((E_DEV, D), jnp.float32)
        for relation in range(REL):
            picked = jnp.where((rel_block == relation)[:, None], head_rows, jnp.zeros_like(head_rows))
            query_sum = query_sum + jnp.dot(picked, relations[relation], preferred_element_type=jnp.float32)
        queries = query_sum.astype(jnp.bfloat16)
        edge_loss, query_grad, tail_grad, neg_grad = edge_block(queries, tail_embed, negatives, factor)
        head_grad = jnp.zeros((E_DEV, D), jnp.float32)
        rel_terms = []
        for relation in range(REL):
            selector = (rel_block == relation)[:, None]
            picked_grad = jnp.where(selector, query_grad, jnp.zeros_like(query_grad))
            head_grad = head_grad + lax.dot_general(picked_grad, relations[relation], (((1,), (1,)), ((), ())), preferred_element_type=jnp.float32)
            picked_rows = jnp.where(selector, head_rows, jnp.zeros_like(head_rows))
            rel_terms.append(lax.dot_general(picked_rows, query_grad, (((0,), (0,)), ((), ())), preferred_element_type=jnp.float32))
        entity_acc = entity_acc.at[head_ids].add(head_grad).at[tail_ids].add(tail_grad)
        relation_acc = relation_acc + jnp.stack(rel_terms)
        negative_acc = negative_acc + neg_grad
        return ((entity_acc, relation_acc, negative_acc), edge_loss)
    initial = (jnp.zeros((ENT, D), jnp.float32), jnp.zeros((REL, D, D), jnp.float32), jnp.zeros((NEG, D), jnp.float32))
    (entity_acc, relation_acc, negative_acc), losses = lax.scan(one_block, initial, jnp.arange(blocks, dtype=jnp.int32))
    entity_acc = entity_acc.at[neg_ids].add(negative_acc)
    return (entity_acc, relation_acc, losses.reshape(EDGES))
```

```python
import functools
import math

import jax
import jax.numpy as jnp
from jax import lax
from jax.experimental import pallas as pl
from jax.experimental.pallas import tpu as pltpu
from jax.sharding import PartitionSpec as P

BF = jnp.bfloat16
F32 = jnp.float32
VMEM = pl.BlockSpec(memory_space=pltpu.VMEM)
SMEM = pl.BlockSpec(memory_space=pltpu.SMEM)


def call(body, outs, scalars, *operands):
    return pl.pallas_call(
        body,
        out_shape=[jax.ShapeDtypeStruct(s, d) for s, d in outs],
        in_specs=[SMEM] * len(scalars) + [VMEM] * len(operands),
        out_specs=[VMEM] * len(outs),
        compiler_params=pltpu.CompilerParams(vmem_limit_bytes=40 * 1024 * 1024),
    )(*scalars, *operands)


def iota(shape, axis):
    return lax.broadcasted_iota(jnp.int32, shape, axis)


def as_column(row):
    size = row.shape[1]
    step = min(128, size)
    eye = iota((step, step), 0) == iota((step, step), 1)
    pieces = [
        jnp.sum(jnp.where(eye, row[:, at : at + step], 0), axis=1, keepdims=True)
        for at in range(0, size, step)
    ]
    return jnp.concatenate(pieces, axis=0)


def as_row(column):
    size = column.shape[0]
    step = min(128, size)
    eye = iota((step, step), 0) == iota((step, step), 1)
    pieces = [
        jnp.sum(jnp.where(eye, column[at : at + step, :], 0.0), axis=0, keepdims=True)
        for at in range(0, size, step)
    ]
    return jnp.concatenate(pieces, axis=1)


def hot_rows(row, count):
    return (as_column(row) == iota((row.shape[1], count), 1)).astype(F32).astype(BF)


def dot(a, b):
    return jnp.dot(a, b, preferred_element_type=F32)


def dot_t0(a, b):
    return lax.dot_general(a, b, (((0,), (0,)), ((), ())), preferred_element_type=F32)


def dot_t1(a, b):
    return lax.dot_general(a, b, (((1,), (1,)), ((), ())), preferred_element_type=F32)


def split(x):
    high = x.astype(BF)
    return high, (x - high.astype(F32)).astype(BF)


def slots_kernel(parts, cap, part_ref, tail_ref, neg_ref, ent_ref, ids_ref, slot_ref, negs_ref):
    edges = part_ref.shape[1]
    slots = parts * cap
    part = part_ref[...]
    tail = tail_ref[...]
    named = (iota((parts, edges), 0) == part).astype(F32)
    before = (iota((edges, edges), 0) < iota((edges, edges), 1)).astype(F32).astype(BF)
    earlier = dot(named.astype(BF), before)
    position = jnp.sum(earlier * named, axis=0, keepdims=True).astype(jnp.int32)
    slot = part * cap + position
    slot_ref[...] = slot
    placed = (iota((slots, edges), 0) == slot).astype(F32).astype(BF)
    which = iota((8, edges), 0)
    digits = jnp.where(which == 0, tail >> 7, jnp.where(which == 1, tail & 127, 0))
    found = dot_t1(digits.astype(F32).astype(BF), placed)
    ids_ref[...] = (found[0:1, :] * 128.0 + found[1:2, :]).astype(jnp.int32)
    negs_ref[...] = dot(hot_rows(neg_ref[...], ent_ref.shape[0]), ent_ref[...]).astype(BF)


def query_kernel(head_ref, rel_ref, slot_ref, ent_ref, op_ref, rows_ref, query_ref, sent_ref):
    rows = dot(hot_rows(head_ref[...], ent_ref.shape[0]), ent_ref[...]).astype(BF)
    rows_ref[...] = rows
    rel = as_column(rel_ref[...])
    total = jnp.zeros(rows.shape, F32)
    for relation in range(op_ref.shape[0]):
        picked = jnp.where(rel == relation, rows, jnp.zeros_like(rows))
        total = total + dot(picked, op_ref[relation])
    queries = total.astype(BF)
    query_ref[...] = queries
    slot = slot_ref[...]
    slots, edges = sent_ref.shape[0], slot.shape[1]
    placed = (iota((slots, edges), 0) == slot).astype(F32).astype(BF)
    sent_ref[...] = dot(placed, queries).astype(BF)


def lookup_kernel(ids_ref, ent_ref, rows_ref):
    rows_ref[...] = dot(hot_rows(ids_ref[...], ent_ref.shape[0]), ent_ref[...]).astype(BF)


def edge_kernel(
    factor,
    picks_ref,
    blocks_ref,
    query_ref,
    got_ref,
    slot_ref,
    negs_ref,
    rows_ref,
    rel_ref,
    loss_ref,
    weight_ref,
    grad_ref,
    prob_ref,
    rel_grad_ref,
):
    queries = query_ref[...]
    negatives = negs_ref[...]
    slots = got_ref.shape[0]
    edges, columns = queries.shape
    placed = as_column(slot_ref[...]) == iota((edges, slots), 1)
    tails = dot(placed.astype(F32).astype(BF), got_ref[...])
    positive = jnp.sum(queries.astype(F32) * tails, axis=1, keepdims=True) * factor
    scores = dot_t1(queries, negatives) * factor
    row_max = jnp.maximum(positive, jnp.max(scores, axis=1, keepdims=True))
    exp_pos = jnp.exp(positive - row_max)
    exp_neg = jnp.exp(scores - row_max)
    total = exp_pos + jnp.sum(exp_neg, axis=1, keepdims=True)
    loss_ref[...] = as_row(jnp.log(total) + row_max - positive)
    pull = exp_pos / total - 1.0
    prob = (exp_neg / total).astype(BF)
    prob_ref[...] = prob
    grad = (factor * (pull * tails + dot(prob, negatives))).astype(BF)
    grad_ref[...] = grad
    weight_ref[...] = jnp.sum(jnp.where(placed, factor * pull, 0.0), axis=0, keepdims=True)
    rel = as_column(rel_ref[...])
    relation_count, blocks = blocks_ref.shape[0] // 4, 4
    width = columns // blocks
    for place in range(relation_count):
        picked_grad = jnp.where(rel == picks_ref[place], grad, jnp.zeros_like(grad))
        for block in range(blocks):
            at = pl.multiple_of(blocks_ref[place * blocks + block] * width, width)
            rel_grad_ref[place, pl.ds(block * width, width), :] = dot_t0(
                rows_ref[:, pl.ds(at, width)], picked_grad
            ).astype(rel_grad_ref.dtype)


def back_kernel(factor, query_ref, prob_ref, grad_ref, rel_ref, op_ref, neg_ref, high_ref, low_ref):
    neg_ref[...] = (factor * dot_t0(prob_ref[...], query_ref[...])).astype(BF)
    rel = as_column(rel_ref[...])
    grad = grad_ref[...]
    total = jnp.zeros(grad.shape, F32)
    for relation in range(op_ref.shape[0]):
        picked = jnp.where(rel == relation, grad, jnp.zeros_like(grad))
        total = total + dot_t1(picked, op_ref[relation])
    high_ref[...], low_ref[...] = split(total)


def add_kernel(
    base_ref,
    ids_ref,
    weight_ref,
    query_ref,
    head_ref,
    high_ref,
    low_ref,
    neg_ref,
    neg_sum_ref,
    out_ref,
):
    count = out_ref.shape[0]
    base = base_ref[0]

    def hot(row):
        return (iota((count, row.shape[1]), 0) + base) == row

    tails = jnp.where(hot(ids_ref[...]), weight_ref[...], 0.0).astype(BF)
    total = dot(tails, query_ref[...])
    heads = hot(head_ref[...]).astype(F32).astype(BF)
    total = total + dot(heads, high_ref[...]) + dot(heads, low_ref[...])
    own = hot(neg_ref[...]).astype(F32).astype(BF)
    high, low = split(neg_sum_ref[...])
    out_ref[...] = (total + (dot(own, high) + dot(own, low))).astype(out_ref.dtype)


def join_kernel(core_ref, mine_ref, other_ref, out_ref):
    half = mine_ref.shape[0]
    at = pl.multiple_of(core_ref[0] * half, half)
    out_ref[pl.ds(at, half), :] = mine_ref[...]
    at = pl.multiple_of((1 - core_ref[0]) * half, half)
    out_ref[pl.ds(at, half), :] = other_ref[...]


def operator_kernel(picks_ref, blocks_ref, mine_ref, other_ref, out_ref):
    width = out_ref.shape[1] // 4
    for place in range(4):
        source = mine_ref if place < 2 else other_ref
        for block in range(4):
            at = pl.multiple_of(blocks_ref[place * 4 + block] * width, width)
            out_ref[picks_ref[place], pl.ds(at, width), :] = source[
                (place % 2) * 4 + block
            ].astype(F32)


def flip(x, axis, size, bit):
    return lax.ppermute(x, axis, [(i, i ^ bit) for i in range(size)])


def exchange(x):
    return lax.all_to_all(x, "dom", split_axis=0, concat_axis=0, tiled=True)


def local(special, entities, relations, head_local, rel_ids, tail_part, tail_local, neg_local):
    columns = entities.shape[1]
    factor = 1.0 / math.sqrt(columns)
    ent_dev = entities.shape[0]
    edges = head_local.shape[0]
    parts = lax.axis_size("dom")
    cap = 2 * edges // parts
    slots = parts * cap
    neg_dev = neg_local.shape[0]
    negs = parts * neg_dev
    count = relations.shape[0]
    head = head_local.reshape(1, edges)
    rel = rel_ids.reshape(1, edges)
    neg_own = neg_local.reshape(1, neg_dev)

    ids, slot, own_negs = call(
        functools.partial(slots_kernel, parts, cap),
        [((1, slots), jnp.int32), ((1, edges), jnp.int32), ((neg_dev, columns), BF)],
        (),
        tail_part.reshape(1, edges),
        tail_local.reshape(1, edges),
        neg_own,
        entities,
    )
    asked = exchange(ids.reshape(parts, cap)).reshape(1, slots)
    negatives = exchange(
        jnp.broadcast_to(own_negs[None], (parts, neg_dev, columns))
    ).reshape(negs, columns)
    rows, queries, sent = call(
        query_kernel,
        [((edges, columns), BF), ((edges, columns), BF), ((slots, columns), BF)],
        (),
        head,
        rel,
        slot,
        entities,
        relations,
    )
    (found,) = call(lookup_kernel, [((slots, columns), BF)], (), asked, entities)
    got = exchange(found.reshape(parts, cap, columns)).reshape(slots, columns)
    sent, got = lax.optimization_barrier((sent, got))
    tail_queries = exchange(sent.reshape(parts, cap, columns)).reshape(slots, columns)

    if special:
        dom = lax.axis_index("dom")
        rep = lax.axis_index("rep")
        z, x, y, core = dom // 2, dom % 2, rep // 2, rep % 2
        picks = jnp.stack([2 * core, 2 * core + 1, 2 - 2 * core, 3 - 2 * core])
        by_y = [(2 * y + x) ^ k for k in range(4)]
        by_x = [(2 * x + y) ^ k for k in range(4)]
        blocks = jnp.stack((by_y + by_x) * 2)
        part_type = BF
    else:
        picks = jnp.arange(count, dtype=jnp.int32)
        blocks = jnp.tile(jnp.arange(4, dtype=jnp.int32), count)
        part_type = F32
    loss, weight, grad, prob, rel_grad = call(
        functools.partial(edge_kernel, factor),
        [
            ((1, edges), F32),
            ((1, slots), F32),
            ((edges, columns), BF),
            ((edges, negs), BF),
            ((count, columns, columns), part_type),
        ],
        (picks, blocks),
        queries,
        got,
        slot,
        negatives,
        rows,
        rel,
    )
    neg_part, high, low = call(
        functools.partial(back_kernel, factor),
        [((negs, columns), BF), ((edges, columns), BF), ((edges, columns), BF)],
        (),
        queries,
        prob,
        grad,
        rel,
        relations,
    )
    weight_high, weight_low = split(weight.reshape(parts, 1, cap))
    weights = jnp.pad(
        jnp.concatenate([weight_high, weight_low], axis=1), ((0, 0), (0, 14), (0, columns - cap))
    )
    back = exchange(
        jnp.concatenate([neg_part.reshape(parts, neg_dev, columns), weights], axis=1)
    )
    neg_sum = jnp.sum(back[:, :neg_dev].astype(F32), axis=0)
    tail_weight = (
        back[:, neg_dev, :cap].astype(F32) + back[:, neg_dev + 1, :cap].astype(F32)
    ).reshape(1, slots)

    def add(base, size, kind):
        return call(
            add_kernel,
            [((size, columns), kind)],
            (base.reshape(1),),
            asked,
            tail_weight,
            tail_queries,
            head,
            high,
            low,
            neg_own,
            neg_sum,
        )[0]

    if not special:
        relation_grad = lax.psum(rel_grad, ("dom", "rep"))
        whole = add(jnp.zeros((), jnp.int32), ent_dev, F32)
        return lax.psum(whole, "rep"), relation_grad, loss.reshape(edges)

    half = columns // 2
    other = flip(rel_grad[2:], "rep", 4, 1)
    mine = rel_grad[:2].astype(F32) + other.astype(F32)
    first_y = flip(mine[0, half:].astype(BF), "rep", 4, 2)
    first_x = flip(mine[1, half:].astype(BF), "dom", 8, 1)
    half_y = mine[0, :half] + first_y.astype(F32)
    half_x = mine[1, :half] + first_x.astype(F32)
    quarter = half // 2
    second_x = flip(half_y[quarter:].astype(BF), "dom", 8, 1)
    second_y = flip(half_x[quarter:].astype(BF), "rep", 4, 2)
    piece = jnp.stack(
        [half_y[:quarter] + second_x.astype(F32), half_x[:quarter] + second_y.astype(F32)]
    ).astype(BF)
    along_z = [[0, 2, 4, 6], [1, 3, 5, 7]]
    stripe = quarter // 4
    spread = piece.reshape(2, 4, stripe, columns).swapaxes(0, 1)
    gathered = lax.all_to_all(spread, "dom", 0, 0, tiled=True, axis_index_groups=along_z)
    summed = jnp.sum(gathered.astype(F32), axis=0).astype(BF)
    everywhere = lax.all_to_all(
        jnp.broadcast_to(summed[None], (4, 2, stripe, columns)),
        "dom",
        0,
        0,
        tiled=True,
        axis_index_groups=along_z,
    )
    pair = everywhere.swapaxes(0, 1).reshape(2, quarter, columns)
    other_x = flip(pair[0], "dom", 8, 1)
    other_y = flip(pair[1], "rep", 4, 2)
    by_y_half = jnp.stack([pair[0], other_x])
    by_x_half = jnp.stack([pair[1], other_y])
    far_y = flip(by_y_half, "rep", 4, 2)
    far_x = flip(by_x_half, "dom", 8, 1)
    own_ops = jnp.concatenate([by_y_half, far_y, by_x_half, far_x], axis=0)
    other_ops = flip(own_ops, "rep", 4, 1)
    (relation_grad,) = call(
        operator_kernel,
        [((count, columns, columns), F32)],
        (picks, blocks),
        own_ops,
        other_ops,
    )

    rows_half = ent_dev // 2
    away = add((1 - core) * rows_half, rows_half, BF)
    arrived = flip(away, "rep", 4, 1)
    kept = add(core * rows_half, rows_half, F32)
    both = (kept + arrived.astype(F32)).astype(BF)
    across = flip(both, "rep", 4, 2)
    done = both.astype(F32) + across.astype(F32)
    partner = flip(done, "rep", 4, 1)
    (entity_grad,) = call(
        join_kernel, [((ent_dev, columns), F32)], (core.reshape(1),), done, partner
    )
    return entity_grad, relation_grad, loss.reshape(edges)


def solution(mesh):
    special = dict(mesh.shape) == {"dom": 8, "rep": 4}
    return jax.shard_map(
        functools.partial(local, special),
        mesh=mesh,
        in_specs=(
            P("dom", None),
            P(),
            P(("dom", "rep")),
            P(("dom", "rep")),
            P(("dom", "rep"), None),
            P(("dom", "rep")),
            P("dom"),
        ),
        out_specs=(P("dom", None), P(), P(("dom", "rep"))),
        check_vma=False,
    )
```

```python
import functools
import math

import jax
import jax.numpy as jnp
from jax import lax
from jax.experimental import pallas as pl
from jax.experimental.pallas import tpu as pltpu
from jax.sharding import PartitionSpec as P

BF = jnp.bfloat16
F32 = jnp.float32
I32 = jnp.int32
VMEM = pl.BlockSpec(memory_space=pltpu.VMEM)
SMEM = pl.BlockSpec(memory_space=pltpu.SMEM)
FAR = pl.BlockSpec(memory_space=pl.ANY)


def call(body, outs, scalars, near, far=()):
    counts = len(scalars), len(near), len(far), len(outs)

    def kernel(*refs):
        refs = list(refs)
        groups = []
        for size in counts + (len(far),):
            groups.append(refs[:size])
            refs = refs[size:]
        scalar_refs, near_refs, far_refs, out_refs, held = groups
        copies = [
            pltpu.make_async_copy(source, target, refs[0].at[index])
            for index, (source, target) in enumerate(zip(far_refs, held))
        ]
        for copy in copies:
            copy.start()

        def take(index):
            copies[index].wait()
            return held[index]

        body(*scalar_refs, *near_refs, *([take] if far else []), *out_refs)

    scratch = [pltpu.VMEM(x.shape, x.dtype) for x in far]
    if far:
        scratch.append(pltpu.SemaphoreType.DMA((len(far),)))
    return pl.pallas_call(
        kernel,
        out_shape=[jax.ShapeDtypeStruct(s, d) for s, d in outs],
        in_specs=[SMEM] * len(scalars) + [VMEM] * len(near) + [FAR] * len(far),
        out_specs=[VMEM] * len(outs),
        scratch_shapes=scratch,
        compiler_params=pltpu.CompilerParams(vmem_limit_bytes=40 * 1024 * 1024),
    )(*scalars, *near, *far)


def iota(shape, axis):
    return lax.broadcasted_iota(I32, shape, axis)


def as_column(row):
    size = row.shape[1]
    step = min(128, size)
    eye = iota((step, step), 0) == iota((step, step), 1)
    pieces = [
        jnp.sum(jnp.where(eye, row[:, at : at + step], 0), axis=1, keepdims=True)
        for at in range(0, size, step)
    ]
    return jnp.concatenate(pieces, axis=0)


def as_row(column):
    size = column.shape[0]
    step = min(128, size)
    eye = iota((step, step), 0) == iota((step, step), 1)
    pieces = [
        jnp.sum(jnp.where(eye, column[at : at + step, :], 0.0), axis=0, keepdims=True)
        for at in range(0, size, step)
    ]
    return jnp.concatenate(pieces, axis=1)


def hot(mask):
    return mask.astype(F32).astype(BF)


def hot_rows(row, count):
    return hot(as_column(row) == iota((row.shape[1], count), 1))


def dot(a, b):
    return jnp.dot(a, b, preferred_element_type=F32)


def dot_t0(a, b):
    return lax.dot_general(a, b, (((0,), (0,)), ((), ())), preferred_element_type=F32)


def dot_t1(a, b):
    return lax.dot_general(a, b, (((1,), (1,)), ((), ())), preferred_element_type=F32)


def split(x):
    high = x.astype(BF)
    return high, (x - high.astype(F32)).astype(BF)


def slots_kernel(parts, cap, place_ref, take, slot_ref, neg_ref, request_ref):
    part = take(0)[...]
    edges = part.shape[1]
    slots = parts * cap
    named = (iota((parts, edges), 0) == part).astype(F32)
    before = hot(iota((edges, edges), 0) < iota((edges, edges), 1))
    earlier = dot(named.astype(BF), before)
    position = jnp.sum(earlier * named, axis=0, keepdims=True).astype(I32)
    slot = part * cap + position
    slot_ref[...] = slot
    placed = hot(iota((slots, edges), 0) == slot)
    which = iota((8, edges), 0)
    tail = take(1)[...]
    digits = jnp.where(which == 0, tail >> 7, jnp.where(which == 1, tail & 127, 0))
    found = dot_t1(digits.astype(F32).astype(BF), placed).astype(BF)
    neg = as_column(take(2)[...])
    negs = neg.shape[0]
    share = request_ref.shape[1]
    turned = iota((negs, negs), 0) == (iota((negs, negs), 1) ^ (place_ref[0] * share))
    ordered = jnp.sum(jnp.where(turned, neg, 0), axis=0, keepdims=True)
    neg_ref[...] = ordered
    entities = take(3)
    own = hot_rows(ordered, entities.shape[0])[:share]
    rows = dot(own, entities[...]).astype(BF)
    columns = rows.shape[1]
    for index in range(parts):
        request_ref[index, :, :columns] = rows
        ids = found[:, index * cap : (index + 1) * cap]
        if cap < 128:
            ids = jnp.concatenate([ids, jnp.zeros((share, 128 - cap), BF)], axis=1)
        request_ref[index, :, columns:] = ids


def query_kernel(slot_ref, take, rows_ref, query_ref):
    head, rel = take(0), take(1)
    entities = take(2)
    rows = dot(hot_rows(head[...], entities.shape[0]), entities[...]).astype(BF)
    rows_ref[...] = rows
    rel = as_column(rel[...])
    total = jnp.zeros(rows.shape, F32)
    operators = take(3)
    for relation in range(operators.shape[0]):
        picked = jnp.where(rel == relation, rows, jnp.zeros_like(rows))
        total = total + dot(picked, operators[relation])
    query_ref[...] = total.astype(BF)


def lookup_kernel(cap, request_ref, take, ids_ref, rows_ref, negs_ref):
    parts, share, width = request_ref.shape
    entities = take(0)
    columns = entities.shape[1]
    pieces = []
    for index in range(parts):
        digits = request_ref[index, :, columns : columns + cap].astype(F32)
        pieces.append(digits[0:1] * 128.0 + digits[1:2])
    ids = jnp.concatenate(pieces, axis=1).astype(I32)
    ids_ref[...] = ids
    rows_ref[...] = dot(hot_rows(ids, entities.shape[0]), entities[...]).astype(BF)
    negs_ref[...] = jnp.concatenate(
        [request_ref[index, :, :columns].astype(F32) for index in range(parts)], axis=0
    ).astype(BF)


def operator_terms(picks_ref, first, rows_ref, rel, grad, out_ref):
    width = out_ref.shape[1]
    for place in range(out_ref.shape[0]):
        at = pl.multiple_of(picks_ref[2 * (first + place) + 1] * width, width)
        picked = jnp.where(rel == picks_ref[2 * (first + place)], grad, jnp.zeros_like(grad))
        out_ref[place] = dot_t0(rows_ref[:, pl.ds(at, width)], picked).astype(out_ref.dtype)


def edge_kernel(
    factor,
    picks_ref,
    query_ref,
    got_ref,
    slot_ref,
    near_ref,
    core_ref,
    across_ref,
    both_ref,
    rows_ref,
    rel_ref,
    loss_ref,
    weight_ref,
    grad_ref,
    prob_ref,
    away_ref,
):
    queries = query_ref[...]
    negatives = jnp.concatenate(
        [near_ref[...], core_ref[...], across_ref[...], both_ref[...]], axis=0
    )
    slots = got_ref.shape[0]
    edges = queries.shape[0]
    scores = dot_t1(queries, negatives) * factor
    placed = as_column(slot_ref[...]) == iota((edges, slots), 1)
    tails = dot(hot(placed), got_ref[...])
    positive = jnp.sum(queries.astype(F32) * tails, axis=1, keepdims=True) * factor
    row_max = jnp.maximum(positive, jnp.max(scores, axis=1, keepdims=True))
    exp_pos = jnp.exp(positive - row_max)
    exp_neg = jnp.exp(scores - row_max)
    total = exp_pos + jnp.sum(exp_neg, axis=1, keepdims=True)
    loss_ref[...] = as_row(jnp.log(total) + row_max - positive)
    pull = exp_pos / total - 1.0
    prob = (exp_neg / total).astype(BF)
    prob_ref[...] = prob
    grad = (factor * (pull * tails + dot(prob, negatives))).astype(BF)
    grad_ref[...] = grad
    weight_ref[...] = factor * pull
    operator_terms(picks_ref, 0, rows_ref, as_column(rel_ref[...]), grad, away_ref)


def back_kernel(factor, cap, query_ref, prob_ref, weight_ref, slot_ref, back_ref):
    queries = query_ref[...]
    parts = back_ref.shape[0]
    share = prob_ref.shape[1] // parts // 4
    slots, edges = parts * cap, queries.shape[0]
    placed = hot(iota((slots, edges), 0) == slot_ref[...])
    weighted = (weight_ref[...] * queries.astype(F32)).astype(BF)
    tails = dot(placed, weighted).astype(BF)
    negs = factor * dot_t0(prob_ref[...], queries)
    for index in range(parts):
        back_ref[index, :cap] = tails[index * cap : (index + 1) * cap]
        pieces = [
            negs[(turn * parts + index) * share : (turn * parts + index + 1) * share]
            for turn in range(4)
        ]
        back_ref[index, cap:] = jnp.concatenate(pieces, axis=0).astype(BF)


def keep_kernel(picks_ref, rows_ref, rel_ref, grad_ref, op_ref, keep_ref, high_ref, low_ref):
    rel = as_column(rel_ref[...])
    grad = grad_ref[...]
    operator_terms(picks_ref, 4, rows_ref, rel, grad, keep_ref)
    total = jnp.zeros(grad.shape, F32)
    for relation in range(op_ref.shape[0]):
        picked = jnp.where(rel == relation, grad, jnp.zeros_like(grad))
        total = total + dot_t1(picked, op_ref[relation])
    high_ref[...], low_ref[...] = split(total)


def pair_kernel(keep_ref, got_ref, own_ref, *out_refs):
    own_ref[...] = keep_ref[0] + got_ref[0].astype(F32)
    for index, out_ref in enumerate(out_refs):
        out_ref[...] = (keep_ref[index + 1] + got_ref[index + 1].astype(F32)).astype(BF)


def quad_kernel(place_ref, own_ref, first_ref, second_ref, third_ref, *out_refs):
    size = out_refs[0].shape[0]
    for turn, out_ref in enumerate(out_refs):
        rows = pl.ds(pl.multiple_of((place_ref[1] ^ turn) * size, size), size)
        total = own_ref[rows, :] + first_ref[rows, :].astype(F32)
        total = total + (second_ref[rows, :].astype(F32) + third_ref[rows, :].astype(F32))
        out_ref[...] = total.astype(out_ref.dtype)


def sum_kernel(own_ref, first_ref, second_ref, third_ref, out_ref):
    total = own_ref[...] + first_ref[...].astype(F32)
    total = total + (second_ref[...].astype(F32) + third_ref[...].astype(F32))
    out_ref[...] = total.astype(BF)


def operator_kernel(picks_ref, place_ref, *refs):
    out_ref = refs[-1]
    size, width = refs[0].shape[0] // 4, refs[0].shape[0]
    for index, source in enumerate(refs[:-1]):
        pick = 2 * ((index + 4) % 8)
        for turn in range(4):
            at = picks_ref[pick + 1] * width + (place_ref[1] ^ turn) * size
            out_ref[picks_ref[pick], pl.ds(pl.multiple_of(at, size), size), :] = source[
                turn * size : (turn + 1) * size
            ].astype(F32)


def add_kernel(
    cap, base_ref, ids_ref, back_ref, head_ref, high_ref, low_ref, neg_ref, out_ref
):
    count = out_ref.shape[0]
    base = base_ref[0]
    parts = back_ref.shape[0]

    def pick(row):
        return hot((iota((count, row.shape[1]), 0) + base) == row)

    tails = jnp.concatenate([back_ref[index, :cap] for index in range(parts)], axis=0)
    total = dot(pick(ids_ref[...]), tails)
    heads = pick(head_ref[...])
    total = total + dot(heads, high_ref[...]) + dot(heads, low_ref[...])
    negs = back_ref[0, cap:].astype(F32)
    for index in range(1, parts):
        negs = negs + back_ref[index, cap:].astype(F32)
    own = pick(neg_ref[...])
    high, low = split(negs)
    out_ref[...] = (total + (dot(own, high) + dot(own, low))).astype(out_ref.dtype)


def join_kernel(place_ref, mine_ref, other_ref, out_ref):
    half = mine_ref.shape[0]
    core = place_ref[2]
    out_ref[pl.ds(pl.multiple_of(core * half, half), half), :] = mine_ref[...]
    out_ref[pl.ds(pl.multiple_of((1 - core) * half, half), half), :] = other_ref[...]


def flip(x, axis, size, bit):
    return lax.ppermute(x, axis, [(i, i ^ bit) for i in range(size)])


def exchange(x):
    return lax.all_to_all(x, "dom", split_axis=0, concat_axis=0, tiled=True)


def local(special, entities, relations, head_local, rel_ids, tail_part, tail_local, neg_local):
    columns = entities.shape[1]
    factor = 1.0 / math.sqrt(columns)
    ent_dev = entities.shape[0]
    edges = head_local.shape[0]
    parts = lax.axis_size("dom")
    reps = lax.axis_size("rep")
    cap = 2 * edges // parts
    slots = parts * cap
    neg_dev = neg_local.shape[0]
    negs = parts * neg_dev
    share = neg_dev // reps
    count = relations.shape[0]
    head = head_local.reshape(1, edges)
    rel = rel_ids.reshape(1, edges)
    dom = lax.axis_index("dom")
    rep = lax.axis_index("rep")
    z, x, y, core = dom // 2, dom % 2, rep // 2, rep % 2
    place = jnp.stack([rep, z, core])
    if special:
        quarters = [(2 * y + x) ^ k for k in range(4)]
        order = [(2 * (1 - core) + q // 2, q % 2) for q in quarters]
        order = order + [(2 * core + q // 2, q % 2) for q in quarters]
    else:
        order = [(k // 2, k % 2) for k in range(2 * count)]
    picks = jnp.stack([jnp.asarray(v, I32) for pair in order for v in pair])

    slot, neg_own, request = call(
        functools.partial(slots_kernel, parts, cap),
        [((1, edges), I32), ((1, neg_dev), I32), ((parts, share, columns + 128), BF)],
        (place,),
        (),
        (
            tail_part.reshape(1, edges),
            tail_local.reshape(1, edges),
            neg_local.reshape(1, neg_dev),
            entities,
        ),
    )
    requests = exchange(request)
    rows, queries = call(
        query_kernel,
        [((edges, columns), BF), ((edges, columns), BF)],
        (),
        (slot,),
        (head, rel, entities, relations),
    )
    requests, rows, queries = lax.optimization_barrier((requests, rows, queries))
    asked, found, neg_near = call(
        functools.partial(lookup_kernel, cap),
        [((1, slots), I32), ((slots, columns), BF), ((parts * share, columns), BF)],
        (),
        (requests,),
        (entities,),
    )
    got = exchange(found.reshape(parts, cap, columns)).reshape(slots, columns)
    neg_core, neg_across, neg_both = [flip(neg_near, "rep", reps, k) for k in (1, 2, 3)]

    terms = F32 if not special else BF
    loss, weight, grad, prob, away = call(
        functools.partial(edge_kernel, factor),
        [
            ((1, edges), F32),
            ((edges, 1), F32),
            ((edges, columns), BF),
            ((edges, negs), BF),
            ((4, columns // 2, columns), terms),
        ],
        (picks,),
        (queries, got, slot, neg_near, neg_core, neg_across, neg_both, rows, rel),
    )
    (back,) = call(
        functools.partial(back_kernel, factor, cap),
        [((parts, cap + neg_dev, columns), BF)],
        (),
        (queries, prob, weight, slot),
    )
    returned = exchange(back)
    keep, high, low = call(
        keep_kernel,
        [((4, columns // 2, columns), F32), ((edges, columns), BF), ((edges, columns), BF)],
        (picks,),
        (rows, rel, grad, relations),
    )

    def add(base, size, kind):
        return call(
            functools.partial(add_kernel, cap),
            [((size, columns), kind)],
            (base.reshape(1),),
            (asked, returned, head, high, low, neg_own),
        )[0]

    if not special:
        whole = jnp.concatenate([away, keep], axis=0).reshape(count, columns, columns)
        entity_grad = lax.psum(add(jnp.zeros((), I32), ent_dev, F32), "rep")
        return entity_grad, lax.psum(whole, ("dom", "rep")), loss.reshape(edges)

    half, quarter = columns // 2, columns // 8

    def quad(k):
        pairs = [
            (d * 4 + r, (d ^ (k & 1)) * 4 + (r ^ (k & 2))) for d in range(8) for r in range(4)
        ]
        return lambda v: lax.ppermute(v, ("dom", "rep"), pairs)

    other = flip(away, "rep", 4, 1)
    own, *sent = call(
        pair_kernel, [((half, columns), F32)] + [((half, columns), BF)] * 3, (), (keep, other)
    )
    met = [quad(k + 1)(v) for k, v in enumerate(sent)]
    own, *sent = call(
        quad_kernel,
        [((quarter, columns), F32)] + [((quarter, columns), BF)] * 3,
        (place,),
        (own, *met),
    )
    met = [flip(v, "dom", 8, 2 * (k + 1)) for k, v in enumerate(sent)]
    (own,) = call(sum_kernel, [((quarter, columns), BF)], (), (own, *met))
    stripes = [own] + [flip(own, "dom", 8, 2 * (k + 1)) for k in range(3)]
    own = jnp.concatenate(stripes, axis=0)
    mine = [own] + [quad(k)(own) for k in range(1, 4)]
    others = [flip(v, "rep", 4, 1) for v in mine]
    (relation_grad,) = call(
        operator_kernel, [((count, columns, columns), F32)], (picks, place), (*mine, *others)
    )

    rows_half = ent_dev // 2
    leaving = add((1 - core) * rows_half, rows_half, BF)
    arrived = flip(leaving, "rep", 4, 1)
    kept = add(core * rows_half, rows_half, F32)
    both = (kept + arrived.astype(F32)).astype(BF)
    across = flip(both, "rep", 4, 2)
    done = both.astype(F32) + across.astype(F32)
    partner = flip(done, "rep", 4, 1)
    (entity_grad,) = call(
        join_kernel, [((ent_dev, columns), F32)], (place,), (done, partner)
    )
    return entity_grad, relation_grad, loss.reshape(edges)


def solution(mesh):
    special = dict(mesh.shape) == {"dom": 8, "rep": 4}
    return jax.shard_map(
        functools.partial(local, special),
        mesh=mesh,
        in_specs=(
            P("dom", None),
            P(),
            P(("dom", "rep")),
            P(("dom", "rep")),
            P(("dom", "rep"), None),
            P(("dom", "rep")),
            P("dom"),
        ),
        out_specs=(P("dom", None), P(), P(("dom", "rep"))),
        check_vma=False,
    )
```

```python
import functools
import math

import jax
import jax.numpy as jnp
from jax import lax
from jax.experimental import pallas as pl
from jax.experimental.pallas import tpu as pltpu
from jax.sharding import PartitionSpec as P

BF = jnp.bfloat16
F32 = jnp.float32
I32 = jnp.int32
VMEM = pl.BlockSpec(memory_space=pltpu.VMEM)
SMEM = pl.BlockSpec(memory_space=pltpu.SMEM)
FAR = pl.BlockSpec(memory_space=pltpu.HBM)


def call(body, outs, scalars, near, far=(), after=()):
    counts = len(scalars), len(near), len(far), len(after), len(outs), len(far)
    away = [index for index, out in enumerate(outs) if len(out) == 3]

    def kernel(*refs):
        refs = list(refs)
        groups = []
        for size in counts:
            groups.append(refs[:size])
            refs = refs[size:]
        scalar_refs, near_refs, far_refs, _, out_refs, held = groups
        copies = [
            pltpu.make_async_copy(source, target, refs[len(away)].at[index])
            for index, (source, target) in enumerate(zip(far_refs, held))
        ]
        for copy in copies:
            copy.start()

        def take(index):
            copies[index].wait()
            return held[index]

        filled = list(out_refs)
        for place, index in enumerate(away):
            filled[index] = refs[place]
        body(*scalar_refs, *near_refs, *([take] if far else []), *filled)
        copies_out = [
            pltpu.make_async_copy(refs[place], out_refs[index], refs[-1].at[place])
            for place, index in enumerate(away)
        ]
        for copy in copies_out:
            copy.start()
        for copy in copies_out:
            copy.wait()

    scratch = [pltpu.VMEM(x.shape, x.dtype) for x in far]
    scratch += [pltpu.VMEM(outs[index][0], outs[index][1]) for index in away]
    if far:
        scratch.append(pltpu.SemaphoreType.DMA((len(far),)))
    if away:
        scratch.append(pltpu.SemaphoreType.DMA((len(away),)))
    return pl.pallas_call(
        kernel,
        out_shape=[jax.ShapeDtypeStruct(out[0], out[1]) for out in outs],
        in_specs=[SMEM] * len(scalars)
        + [VMEM] * len(near)
        + [FAR] * (len(far) + len(after)),
        out_specs=[FAR if len(out) == 3 else VMEM for out in outs],
        scratch_shapes=scratch,
        compiler_params=pltpu.CompilerParams(vmem_limit_bytes=60 * 1024 * 1024),
    )(*scalars, *near, *far, *after)


def iota(shape, axis):
    return lax.broadcasted_iota(I32, shape, axis)


def as_column(row):
    size = row.shape[1]
    step = min(128, size)
    eye = iota((step, step), 0) == iota((step, step), 1)
    pieces = [
        jnp.sum(jnp.where(eye, row[:, at : at + step], 0), axis=1, keepdims=True)
        for at in range(0, size, step)
    ]
    return jnp.concatenate(pieces, axis=0)


def as_row(column):
    size = column.shape[0]
    step = min(128, size)
    eye = iota((step, step), 0) == iota((step, step), 1)
    pieces = [
        jnp.sum(jnp.where(eye, column[at : at + step, :], 0.0), axis=0, keepdims=True)
        for at in range(0, size, step)
    ]
    return jnp.concatenate(pieces, axis=1)


def hot(mask):
    return mask.astype(F32).astype(BF)


def hot_rows(row, count):
    return hot(as_column(row) == iota((row.shape[1], count), 1))


def dot(a, b):
    return jnp.dot(a, b, preferred_element_type=F32)


def dot_t0(a, b):
    return lax.dot_general(a, b, (((0,), (0,)), ((), ())), preferred_element_type=F32)


def dot_t1(a, b):
    return lax.dot_general(a, b, (((1,), (1,)), ((), ())), preferred_element_type=F32)


def split(x):
    high = x.astype(BF)
    return high, (x - high.astype(F32)).astype(BF)


def slots_kernel(parts, cap, place_ref, take, slot_ref, neg_ref, request_ref):
    part = take(0)[...]
    edges = part.shape[1]
    slots = parts * cap
    named = (iota((parts, edges), 0) == part).astype(F32)
    before = hot(iota((edges, edges), 0) < iota((edges, edges), 1))
    earlier = dot(named.astype(BF), before)
    position = jnp.sum(earlier * named, axis=0, keepdims=True).astype(I32)
    slot = part * cap + position
    slot_ref[...] = slot
    placed = hot(iota((slots, edges), 0) == slot)
    which = iota((8, edges), 0)
    tail = take(1)[...]
    digits = jnp.where(which == 0, tail >> 7, jnp.where(which == 1, tail & 127, 0))
    found = dot_t1(digits.astype(F32).astype(BF), placed).astype(BF)
    neg = as_column(take(2)[...])
    negs = neg.shape[0]
    share = request_ref.shape[1]
    turned = iota((negs, negs), 0) == (iota((negs, negs), 1) ^ (place_ref[0] * share))
    ordered = jnp.sum(jnp.where(turned, neg, 0), axis=0, keepdims=True)
    neg_ref[...] = ordered
    entities = take(3)
    own = hot_rows(ordered, entities.shape[0])[:share]
    rows = dot(own, entities[...]).astype(BF)
    columns = rows.shape[1]
    for index in range(parts):
        request_ref[index, :, :columns] = rows
        ids = found[:, index * cap : (index + 1) * cap]
        if cap < 128:
            ids = jnp.concatenate([ids, jnp.zeros((share, 128 - cap), BF)], axis=1)
        request_ref[index, :, columns:] = ids


def query_kernel(take, rows_ref, query_ref):
    head, rel = take(0), take(1)
    entities = take(2)
    rows = dot(hot_rows(head[...], entities.shape[0]), entities[...]).astype(BF)
    rows_ref[...] = rows
    rel = as_column(rel[...])
    total = jnp.zeros(rows.shape, F32)
    operators = take(3)
    for relation in range(operators.shape[0]):
        picked = jnp.where(rel == relation, rows, jnp.zeros_like(rows))
        total = total + dot(picked, operators[relation])
    query_ref[...] = total.astype(BF)


def lookup_kernel(cap, request_ref, take, ids_ref, rows_ref, negs_ref):
    parts, share, width = request_ref.shape
    entities = take(0)
    columns = entities.shape[1]
    pieces = []
    for index in range(parts):
        digits = request_ref[index, :, columns : columns + cap].astype(F32)
        pieces.append(digits[0:1] * 128.0 + digits[1:2])
    ids = jnp.concatenate(pieces, axis=1).astype(I32)
    ids_ref[...] = ids
    rows_ref[...] = dot(hot_rows(ids, entities.shape[0]), entities[...]).astype(BF)
    negs_ref[...] = jnp.concatenate(
        [request_ref[index, :, :columns].astype(F32) for index in range(parts)], axis=0
    ).astype(BF)


def operator_terms(picks_ref, first, rows_ref, rel, grad, out_ref):
    width = out_ref.shape[1]
    for place in range(out_ref.shape[0]):
        at = pl.multiple_of(picks_ref[2 * (first + place) + 1] * width, width)
        picked = jnp.where(rel == picks_ref[2 * (first + place)], grad, jnp.zeros_like(grad))
        out_ref[place] = dot_t0(rows_ref[:, pl.ds(at, width)], picked).astype(out_ref.dtype)


def edge_kernel(
    factor,
    picks_ref,
    slot_ref,
    near_ref,
    core_ref,
    across_ref,
    both_ref,
    take,
    loss_ref,
    weight_ref,
    grad_ref,
    prob_ref,
    away_ref,
):
    queries = take(0)[...]
    negatives = jnp.concatenate(
        [near_ref[...], core_ref[...], across_ref[...], both_ref[...]], axis=0
    )
    scores = dot_t1(queries, negatives) * factor
    got = take(1)
    placed = as_column(slot_ref[...]) == iota((queries.shape[0], got.shape[0]), 1)
    tails = dot(hot(placed), got[...])
    positive = jnp.sum(queries.astype(F32) * tails, axis=1, keepdims=True) * factor
    row_max = jnp.maximum(positive, jnp.max(scores, axis=1, keepdims=True))
    exp_pos = jnp.exp(positive - row_max)
    exp_neg = jnp.exp(scores - row_max)
    total = exp_pos + jnp.sum(exp_neg, axis=1, keepdims=True)
    loss_ref[...] = as_row(jnp.log(total) + row_max - positive)
    pull = exp_pos / total - 1.0
    prob = (exp_neg / total).astype(BF)
    prob_ref[...] = prob
    grad = (factor * (pull * tails + dot(prob, negatives))).astype(BF)
    grad_ref[...] = grad
    weight_ref[...] = factor * pull
    rows = take(2)
    operator_terms(picks_ref, 0, rows, as_column(take(3)[...]), grad, away_ref)


def back_kernel(factor, cap, weight_ref, slot_ref, take, back_ref):
    parts = back_ref.shape[0]
    queries = take(0)[...]
    slots, edges = parts * cap, queries.shape[0]
    placed = hot(iota((slots, edges), 0) == slot_ref[...])
    weighted = (weight_ref[...] * queries.astype(F32)).astype(BF)
    tails = dot(placed, weighted).astype(BF)
    prob = take(1)
    share = prob.shape[1] // parts // 4
    negs = factor * dot_t0(prob[...], queries)
    for index in range(parts):
        back_ref[index, :cap] = tails[index * cap : (index + 1) * cap]
        pieces = [
            negs[(turn * parts + index) * share : (turn * parts + index + 1) * share]
            for turn in range(4)
        ]
        back_ref[index, cap:] = jnp.concatenate(pieces, axis=0).astype(BF)


def keep_kernel(picks_ref, take, keep_ref):
    rel = as_column(take(2)[...])
    rows = take(0)
    operator_terms(picks_ref, 4, rows, rel, take(1)[...], keep_ref)


def pair_kernel(picks_ref, take, own_ref, *out_refs):
    rel = as_column(take(2)[...])
    rows, grad = take(0), take(1)[...]
    width = own_ref.shape[0]
    got = take(3)
    for place in (1, 2, 3, 0):
        relation = picks_ref[2 * (4 + place)]
        at = pl.multiple_of(picks_ref[2 * (4 + place) + 1] * width, width)
        picked = jnp.where(rel == relation, grad, jnp.zeros_like(grad))
        term = dot_t0(rows[:, pl.ds(at, width)], picked) + got[place].astype(F32)
        if place:
            out_refs[place - 1][...] = term.astype(BF)
        else:
            own_ref[...] = term


def head_kernel(take, high_ref, low_ref):
    rel = as_column(take(1)[...])
    grad = take(0)[...]
    operators = take(2)
    total = jnp.zeros(grad.shape, F32)
    for relation in range(operators.shape[0]):
        picked = jnp.where(rel == relation, grad, jnp.zeros_like(grad))
        total = total + dot_t1(picked, operators[relation])
    high_ref[...], low_ref[...] = split(total)


def quad_kernel(place_ref, own_ref, first_ref, second_ref, third_ref, *out_refs):
    size = out_refs[0].shape[0]
    for turn, out_ref in enumerate(out_refs):
        rows = pl.ds(pl.multiple_of((place_ref[1] ^ turn) * size, size), size)
        total = own_ref[rows, :] + first_ref[rows, :].astype(F32)
        total = total + (second_ref[rows, :].astype(F32) + third_ref[rows, :].astype(F32))
        out_ref[...] = total.astype(out_ref.dtype)


def sum_kernel(own_ref, first_ref, second_ref, third_ref, out_ref):
    total = own_ref[...] + first_ref[...].astype(F32)
    total = total + (second_ref[...].astype(F32) + third_ref[...].astype(F32))
    out_ref[...] = total.astype(BF)


def operator_kernel(picks_ref, place_ref, *refs):
    sources, (out_ref, wide, sems) = refs[:-3], refs[-3:]
    width = sources[0].shape[0]
    size = width // 4
    copies = []
    for index, source in enumerate(sources):
        wide[index] = source[...].astype(F32)
        pick = 2 * ((index + 4) % 8)
        for turn in range(4):
            at = picks_ref[pick + 1] * width + (place_ref[1] ^ turn) * size
            copy = pltpu.make_async_copy(
                wide.at[index, pl.ds(turn * size, size)],
                out_ref.at[picks_ref[pick], pl.ds(pl.multiple_of(at, size), size)],
                sems.at[index, turn],
            )
            copy.start()
            copies.append(copy)
    for copy in copies:
        copy.wait()


def add_kernel(cap, base_ref, ids_ref, neg_ref, take, out_ref):
    count = out_ref.shape[0]
    base = base_ref[0]

    def pick(row):
        return hot((iota((count, row.shape[1]), 0) + base) == row)

    heads = pick(take(0)[...])
    total = dot(heads, take(1)[...]) + dot(heads, take(2)[...])
    back_ref = take(3)
    parts = back_ref.shape[0]
    tails = jnp.concatenate([back_ref[index, :cap] for index in range(parts)], axis=0)
    total = total + dot(pick(ids_ref[...]), tails)
    negs = back_ref[0, cap:].astype(F32)
    for index in range(1, parts):
        negs = negs + back_ref[index, cap:].astype(F32)
    own = pick(neg_ref[...])
    high, low = split(negs)
    out_ref[...] = (total + (dot(own, high) + dot(own, low))).astype(out_ref.dtype)


def both_kernel(kept_ref, arrived_ref, out_ref):
    out_ref[...] = (kept_ref[...] + arrived_ref[...].astype(F32)).astype(BF)


def join_kernel(place_ref, mine_ref, over_ref, other_ref, far_ref, out_ref, wide, sems):
    half = mine_ref.shape[0]
    core = place_ref[2]
    copies = []
    for index, (first, second, at) in enumerate(
        ((mine_ref, over_ref, core), (other_ref, far_ref, 1 - core))
    ):
        wide[index] = first[...].astype(F32) + second[...].astype(F32)
        copy = pltpu.make_async_copy(
            wide.at[index],
            out_ref.at[pl.ds(pl.multiple_of(at * half, half), half)],
            sems.at[index],
        )
        copy.start()
        copies.append(copy)
    for copy in copies:
        copy.wait()


def write(body, out, scalars, near, scratch):
    return pl.pallas_call(
        body,
        out_shape=jax.ShapeDtypeStruct(*out),
        in_specs=[SMEM] * len(scalars) + [VMEM] * len(near),
        out_specs=FAR,
        scratch_shapes=scratch,
        compiler_params=pltpu.CompilerParams(vmem_limit_bytes=60 * 1024 * 1024),
    )(*scalars, *near)


def flip(x, axis, size, bit):
    return lax.ppermute(x, axis, [(i, i ^ bit) for i in range(size)])


def exchange(x):
    return lax.all_to_all(x, "dom", split_axis=0, concat_axis=0, tiled=True)


def local(special, entities, relations, head_local, rel_ids, tail_part, tail_local, neg_local):
    columns = entities.shape[1]
    factor = 1.0 / math.sqrt(columns)
    ent_dev = entities.shape[0]
    edges = head_local.shape[0]
    parts = lax.axis_size("dom")
    reps = lax.axis_size("rep")
    cap = 2 * edges // parts
    slots = parts * cap
    neg_dev = neg_local.shape[0]
    negs = parts * neg_dev
    share = neg_dev // reps
    count = relations.shape[0]
    head = head_local.reshape(1, edges)
    rel = rel_ids.reshape(1, edges)
    dom = lax.axis_index("dom")
    rep = lax.axis_index("rep")
    z, x, y, core = dom // 2, dom % 2, rep // 2, rep % 2
    place = jnp.stack([rep, z, core])
    if special:
        quarters = [(2 * y + x) ^ k for k in range(4)]
        order = [(2 * (1 - core) + q // 2, q % 2) for q in quarters]
        order = order + [(2 * core + q // 2, q % 2) for q in quarters]
    else:
        order = [(k // 2, k % 2) for k in range(2 * count)]
    picks = jnp.stack([jnp.asarray(v, I32) for pair in order for v in pair])

    slot, neg_own, request = call(
        functools.partial(slots_kernel, parts, cap),
        [((1, edges), I32), ((1, neg_dev), I32), ((parts, share, columns + 128), BF)],
        (place,),
        (),
        (
            tail_part.reshape(1, edges),
            tail_local.reshape(1, edges),
            neg_local.reshape(1, neg_dev),
            entities,
        ),
    )
    requests = exchange(request)
    rows, queries = call(
        query_kernel,
        [((edges, columns), BF, True), ((edges, columns), BF, True)],
        (),
        (),
        (head, rel, entities, relations),
        (slot,),
    )
    asked, found, neg_near = call(
        functools.partial(lookup_kernel, cap),
        [((1, slots), I32), ((slots, columns), BF, True), ((parts * share, columns), BF)],
        (),
        (requests,),
        (entities,),
        (rows,),
    )
    got = exchange(found.reshape(parts, cap, columns)).reshape(slots, columns)
    neg_core, neg_across, neg_both = [flip(neg_near, "rep", reps, k) for k in (1, 2, 3)]

    loss, weight, grad, prob, away = call(
        functools.partial(edge_kernel, factor),
        [
            ((1, edges), F32),
            ((edges, 1), F32),
            ((edges, columns), BF, True),
            ((edges, negs), BF, True),
            ((4, columns // 2, columns), BF if special else F32, True),
        ],
        (picks,),
        (slot, neg_near, neg_core, neg_across, neg_both),
        (queries, got, rows, rel),
    )
    (back,) = call(
        functools.partial(back_kernel, factor, cap),
        [((parts, cap + neg_dev, columns), BF, True)],
        (),
        (weight, slot),
        (queries, prob),
    )
    returned = exchange(back)

    def add(base, size, kind, after):
        return call(
            functools.partial(add_kernel, cap),
            [((size, columns), kind)],
            (base.reshape(1),),
            (asked, neg_own),
            (head, high, low, returned),
            after,
        )[0]

    def head_grads(after):
        return call(
            head_kernel,
            [((edges, columns), BF, True), ((edges, columns), BF, True)],
            (),
            (),
            (grad, rel, relations),
            after,
        )

    if not special:
        (keep,) = call(
            keep_kernel,
            [((4, columns // 2, columns), F32, True)],
            (picks,),
            (),
            (rows, grad, rel),
        )
        whole = jnp.concatenate([away, keep], axis=0).reshape(count, columns, columns)
        high, low = head_grads(())
        entity_grad = lax.psum(add(jnp.zeros((), I32), ent_dev, F32, ()), "rep")
        return entity_grad, lax.psum(whole, ("dom", "rep")), loss.reshape(edges)

    half, quarter = columns // 2, columns // 8

    def quad(k):
        pairs = [
            (d * 4 + r, (d ^ (k & 1)) * 4 + (r ^ (k & 2))) for d in range(8) for r in range(4)
        ]
        return lambda v: lax.ppermute(v, ("dom", "rep"), pairs)

    other = flip(away, "rep", 4, 1)
    own, *sent = call(
        pair_kernel,
        [((half, columns), F32)] + [((half, columns), BF)] * 3,
        (picks,),
        (),
        (rows, grad, rel, other),
        (back,),
    )
    met = [quad(k + 1)(v) for k, v in enumerate(sent)]
    high, low = head_grads((sent[0],))
    own, *sent = call(
        quad_kernel,
        [((quarter, columns), F32)] + [((quarter, columns), BF)] * 3,
        (place,),
        (own, *met),
        (),
        (high,),
    )
    met = [flip(v, "dom", 8, 2 * (k + 1)) for k, v in enumerate(sent)]
    (own,) = call(sum_kernel, [((quarter, columns), BF)], (), (own, *met))
    stripes = [own] + [flip(own, "dom", 8, 2 * (k + 1)) for k in range(3)]
    own = jnp.concatenate(stripes, axis=0)
    over_y = quad(2)(own)
    mine = [own, quad(1)(own), over_y, quad(1)(over_y)]
    others = [flip(v, "rep", 4, 1) for v in mine]
    relation_grad = write(
        operator_kernel,
        ((count, columns, columns), F32),
        (picks, place),
        (*mine, *others),
        [pltpu.VMEM((8, half, columns), F32), pltpu.SemaphoreType.DMA((8, 4))],
    )

    rows_half = ent_dev // 2
    leaving = add((1 - core) * rows_half, rows_half, BF, (own,))
    arrived = flip(leaving, "rep", 4, 1)
    kept = add(core * rows_half, rows_half, F32, (leaving, over_y))
    (both,) = call(both_kernel, [((rows_half, columns), BF)], (), (kept, arrived))
    across = flip(both, "rep", 4, 2)
    pieces = (both, across, flip(both, "rep", 4, 1), flip(across, "rep", 4, 1))
    entity_grad = write(
        join_kernel,
        ((ent_dev, columns), F32),
        (place,),
        pieces,
        [pltpu.VMEM((2, rows_half, columns), F32), pltpu.SemaphoreType.DMA((2,))],
    )
    return entity_grad, relation_grad, loss.reshape(edges)


def solution(mesh):
    special = dict(mesh.shape) == {"dom": 8, "rep": 4}
    return jax.shard_map(
        functools.partial(local, special),
        mesh=mesh,
        in_specs=(
            P("dom", None),
            P(),
            P(("dom", "rep")),
            P(("dom", "rep")),
            P(("dom", "rep"), None),
            P(("dom", "rep")),
            P("dom"),
        ),
        out_specs=(P("dom", None), P(), P(("dom", "rep"))),
        check_vma=False,
    )
```

```python
import functools
import math

import jax
import jax.numpy as jnp
from jax import lax
from jax.experimental import pallas as pl
from jax.experimental.pallas import tpu as pltpu
from jax.sharding import PartitionSpec as P

BF = jnp.bfloat16
F32 = jnp.float32
I32 = jnp.int32
VMEM = pl.BlockSpec(memory_space=pltpu.VMEM)
SMEM = pl.BlockSpec(memory_space=pltpu.SMEM)
FAR = pl.BlockSpec(memory_space=pltpu.HBM)


def call(body, outs, scalars, near, far=(), after=(), room=40):
    counts = len(scalars), len(near), len(far), len(after), len(outs), len(far)
    away = [index for index, out in enumerate(outs) if len(out) == 3]

    def kernel(*refs):
        refs = list(refs)
        groups = []
        for size in counts:
            groups.append(refs[:size])
            refs = refs[size:]
        scalar_refs, near_refs, far_refs, _, out_refs, held = groups
        copies = [
            pltpu.make_async_copy(source, target, refs[len(away)].at[index])
            for index, (source, target) in enumerate(zip(far_refs, held))
        ]
        for copy in copies:
            copy.start()

        def take(index):
            copies[index].wait()
            return held[index]

        filled = list(out_refs)
        for place, index in enumerate(away):
            filled[index] = refs[place]
        body(*scalar_refs, *near_refs, *([take] if far else []), *filled)
        copies_out = [
            pltpu.make_async_copy(refs[place], out_refs[index], refs[-1].at[place])
            for place, index in enumerate(away)
        ]
        for copy in copies_out:
            copy.start()
        for copy in copies_out:
            copy.wait()

    scratch = [pltpu.VMEM(x.shape, x.dtype) for x in far]
    scratch += [pltpu.VMEM(outs[index][0], outs[index][1]) for index in away]
    if far:
        scratch.append(pltpu.SemaphoreType.DMA((len(far),)))
    if away:
        scratch.append(pltpu.SemaphoreType.DMA((len(away),)))
    return pl.pallas_call(
        kernel,
        out_shape=[jax.ShapeDtypeStruct(out[0], out[1]) for out in outs],
        in_specs=[SMEM] * len(scalars)
        + [VMEM] * len(near)
        + [FAR] * (len(far) + len(after)),
        out_specs=[FAR if len(out) == 3 else VMEM for out in outs],
        scratch_shapes=scratch,
        compiler_params=pltpu.CompilerParams(vmem_limit_bytes=room * 1024 * 1024),
    )(*scalars, *near, *far, *after)


def iota(shape, axis):
    return lax.broadcasted_iota(I32, shape, axis)


def as_column(row):
    size = row.shape[1]
    step = min(128, size)
    eye = iota((step, step), 0) == iota((step, step), 1)
    pieces = [
        jnp.sum(jnp.where(eye, row[:, at : at + step], 0), axis=1, keepdims=True)
        for at in range(0, size, step)
    ]
    return jnp.concatenate(pieces, axis=0)


def as_row(column):
    size = column.shape[0]
    step = min(128, size)
    eye = iota((step, step), 0) == iota((step, step), 1)
    pieces = [
        jnp.sum(jnp.where(eye, column[at : at + step, :], 0.0), axis=0, keepdims=True)
        for at in range(0, size, step)
    ]
    return jnp.concatenate(pieces, axis=1)


def hot(mask):
    return mask.astype(F32).astype(BF)


def hot_rows(row, count):
    return hot(as_column(row) == iota((row.shape[1], count), 1))


def dot(a, b):
    return jnp.dot(a, b, preferred_element_type=F32)


def dot_t0(a, b):
    return lax.dot_general(a, b, (((0,), (0,)), ((), ())), preferred_element_type=F32)


def dot_t1(a, b):
    return lax.dot_general(a, b, (((1,), (1,)), ((), ())), preferred_element_type=F32)


def split(x):
    high = x.astype(BF)
    return high, (x - high.astype(F32)).astype(BF)


def slots_kernel(parts, cap, place_ref, take, slot_ref, neg_ref, request_ref):
    part = take(0)[...]
    edges = part.shape[1]
    slots = parts * cap
    named = (iota((parts, edges), 0) == part).astype(F32)
    before = hot(iota((edges, edges), 0) < iota((edges, edges), 1))
    earlier = dot(named.astype(BF), before)
    position = jnp.sum(earlier * named, axis=0, keepdims=True).astype(I32)
    slot = part * cap + position
    slot_ref[...] = slot
    placed = hot(iota((slots, edges), 0) == slot)
    which = iota((8, edges), 0)
    tail = take(1)[...]
    digits = jnp.where(which == 0, tail >> 7, jnp.where(which == 1, tail & 127, 0))
    found = dot_t1(digits.astype(F32).astype(BF), placed).astype(BF)
    neg = as_column(take(2)[...])
    negs = neg.shape[0]
    share = request_ref.shape[1]
    turned = iota((negs, negs), 0) == (iota((negs, negs), 1) ^ (place_ref[0] * share))
    ordered = jnp.sum(jnp.where(turned, neg, 0), axis=0, keepdims=True)
    neg_ref[...] = ordered
    entities = take(3)
    own = hot_rows(ordered, entities.shape[0])[:share]
    rows = dot(own, entities[...]).astype(BF)
    columns = rows.shape[1]
    for index in range(parts):
        request_ref[index, :, :columns] = rows
        ids = found[:, index * cap : (index + 1) * cap]
        if cap < 128:
            ids = jnp.concatenate([ids, jnp.zeros((share, 128 - cap), BF)], axis=1)
        request_ref[index, :, columns:] = ids


def query_kernel(take, rows_ref, query_ref):
    head, rel = take(0), take(1)
    entities = take(2)
    rows = dot(hot_rows(head[...], entities.shape[0]), entities[...]).astype(BF)
    rows_ref[...] = rows
    rel = as_column(rel[...])
    total = jnp.zeros(rows.shape, F32)
    operators = take(3)
    for relation in range(operators.shape[0]):
        picked = jnp.where(rel == relation, rows, jnp.zeros_like(rows))
        total = total + dot(picked, operators[relation])
    query_ref[...] = total.astype(BF)


def lookup_kernel(cap, request_ref, entities, ids_ref, rows_ref, negs_ref):
    parts, share, width = request_ref.shape
    columns = entities.shape[1]
    pieces = []
    for index in range(parts):
        digits = request_ref[index, :, columns : columns + cap].astype(F32)
        pieces.append(digits[0:1] * 128.0 + digits[1:2])
    ids = jnp.concatenate(pieces, axis=1).astype(I32)
    ids_ref[...] = ids
    rows_ref[...] = dot(hot_rows(ids, entities.shape[0]), entities[...]).astype(BF)
    negs_ref[...] = jnp.concatenate(
        [request_ref[index, :, :columns].astype(F32) for index in range(parts)], axis=0
    ).astype(BF)


def operator_terms(picks_ref, first, rows_ref, rel, grad, out_ref):
    width = out_ref.shape[1]
    for place in range(out_ref.shape[0]):
        at = pl.multiple_of(picks_ref[2 * (first + place) + 1] * width, width)
        picked = jnp.where(rel == picks_ref[2 * (first + place)], grad, jnp.zeros_like(grad))
        out_ref[place] = dot_t0(rows_ref[:, pl.ds(at, width)], picked).astype(out_ref.dtype)


def edge_kernel(
    factor,
    picks_ref,
    slot_ref,
    near_ref,
    core_ref,
    across_ref,
    both_ref,
    query_ref,
    got_ref,
    rows_ref,
    rel_ref,
    loss_ref,
    grad_ref,
    away_ref,
    back_ref,
    keep_ref,
):
    queries = query_ref[...]
    negatives = jnp.concatenate(
        [near_ref[...], core_ref[...], across_ref[...], both_ref[...]], axis=0
    )
    edges, slots = queries.shape[0], got_ref.shape[0]
    slot = slot_ref[...]
    scores = dot_t1(queries, negatives) * factor
    tails = dot(hot(as_column(slot) == iota((edges, slots), 1)), got_ref[...])
    positive = jnp.sum(queries.astype(F32) * tails, axis=1, keepdims=True) * factor
    row_max = jnp.maximum(positive, jnp.max(scores, axis=1, keepdims=True))
    exp_pos = jnp.exp(positive - row_max)
    exp_neg = jnp.exp(scores - row_max)
    total = exp_pos + jnp.sum(exp_neg, axis=1, keepdims=True)
    loss_ref[...] = as_row(jnp.log(total) + row_max - positive)
    pull = exp_pos / total - 1.0
    prob = (exp_neg / total).astype(BF)
    grad = (factor * (pull * tails + dot(prob, negatives))).astype(BF)
    grad_ref[...] = grad
    rel = as_column(rel_ref[...])
    operator_terms(picks_ref, 0, rows_ref, rel, grad, away_ref)
    operator_terms(picks_ref, 4, rows_ref, rel, grad, keep_ref)
    parts = back_ref.shape[0]
    cap = slots // parts
    weighted = (factor * pull * queries.astype(F32)).astype(BF)
    rows = dot(hot(iota((slots, edges), 0) == slot), weighted).astype(BF)
    negs = factor * dot_t0(prob, queries)
    share = negs.shape[0] // parts // 4
    for index in range(parts):
        back_ref[index, :cap] = rows[index * cap : (index + 1) * cap]
        pieces = [
            negs[(turn * parts + index) * share : (turn * parts + index + 1) * share]
            for turn in range(4)
        ]
        back_ref[index, cap:] = jnp.concatenate(pieces, axis=0).astype(BF)


def pair_kernel(keep_ref, got_ref, own_ref, *out_refs):
    for index, out_ref in enumerate(out_refs):
        term = keep_ref[index + 1].astype(F32) + got_ref[index + 1].astype(F32)
        out_ref[...] = term.astype(BF)
    own_ref[...] = keep_ref[0].astype(F32) + got_ref[0].astype(F32)


def head_kernel(grad_ref, rel_ref, operators, out_ref):
    rel = as_column(rel_ref[...])
    grad = grad_ref[...]
    edges = grad.shape[0]
    total = jnp.zeros(grad.shape, F32)
    for relation in range(operators.shape[0]):
        picked = jnp.where(rel == relation, grad, jnp.zeros_like(grad))
        total = total + dot_t1(picked, operators[relation])
    out_ref[:edges], out_ref[edges:] = split(total)


def quad_kernel(place_ref, own_ref, first_ref, second_ref, third_ref, *out_refs):
    size = out_refs[0].shape[0]
    for turn, out_ref in enumerate(out_refs):
        rows = pl.ds(pl.multiple_of((place_ref[1] ^ turn) * size, size), size)
        total = own_ref[rows, :] + first_ref[rows, :].astype(F32)
        total = total + (second_ref[rows, :].astype(F32) + third_ref[rows, :].astype(F32))
        out_ref[...] = total.astype(out_ref.dtype)


def sum_kernel(own_ref, first_ref, second_ref, third_ref, out_ref):
    total = own_ref[...] + first_ref[...].astype(F32)
    total = total + (second_ref[...].astype(F32) + third_ref[...].astype(F32))
    out_ref[...] = total.astype(BF)


def operator_kernel(picks_ref, place_ref, *refs):
    sources, (out_ref, wide, sems) = refs[:-3], refs[-3:]
    width = sources[0].shape[0]
    size = width // 4
    copies = []
    for index, source in enumerate(sources):
        wide[index] = source[...].astype(F32)
        pick = 2 * ((index + 4) % 8)
        for turn in range(4):
            at = picks_ref[pick + 1] * width + (place_ref[1] ^ turn) * size
            copy = pltpu.make_async_copy(
                wide.at[index, pl.ds(turn * size, size)],
                out_ref.at[picks_ref[pick], pl.ds(pl.multiple_of(at, size), size)],
                sems.at[index, turn],
            )
            copy.start()
            copies.append(copy)
    for copy in copies:
        copy.wait()


def add_kernel(base_ref, ids_ref, neg_ref, head_ref, grads_ref, back_ref, out_ref):
    count = out_ref.shape[0]
    base = base_ref[0]

    def pick(row):
        return hot((iota((count, row.shape[1]), 0) + base) == row)

    heads = pick(head_ref[...])
    total = dot(jnp.concatenate([heads, heads], axis=1), grads_ref[...])
    parts = back_ref.shape[0]
    cap = ids_ref.shape[1] // parts
    tails = jnp.concatenate([back_ref[index, :cap] for index in range(parts)], axis=0)
    total = total + dot(pick(ids_ref[...]), tails)
    negs = back_ref[0, cap:].astype(F32)
    for index in range(1, parts):
        negs = negs + back_ref[index, cap:].astype(F32)
    own = pick(neg_ref[...])
    high, low = split(negs)
    out_ref[...] = (total + (dot(own, high) + dot(own, low))).astype(out_ref.dtype)


def both_kernel(kept_ref, arrived_ref, out_ref):
    out_ref[...] = (kept_ref[...] + arrived_ref[...].astype(F32)).astype(BF)


def join_kernel(place_ref, mine_ref, over_ref, other_ref, far_ref, out_ref, wide, sems):
    half = mine_ref.shape[0]
    core = place_ref[2]
    copies = []
    for index, (first, second, at) in enumerate(
        ((mine_ref, over_ref, core), (other_ref, far_ref, 1 - core))
    ):
        wide[index] = first[...].astype(F32) + second[...].astype(F32)
        copy = pltpu.make_async_copy(
            wide.at[index],
            out_ref.at[pl.ds(pl.multiple_of(at * half, half), half)],
            sems.at[index],
        )
        copy.start()
        copies.append(copy)
    for copy in copies:
        copy.wait()


def write(body, out, scalars, near, scratch):
    return pl.pallas_call(
        body,
        out_shape=jax.ShapeDtypeStruct(*out),
        in_specs=[SMEM] * len(scalars) + [VMEM] * len(near),
        out_specs=FAR,
        scratch_shapes=scratch,
        compiler_params=pltpu.CompilerParams(vmem_limit_bytes=40 * 1024 * 1024),
    )(*scalars, *near)


def flip(x, axis, size, bit):
    return lax.ppermute(x, axis, [(i, i ^ bit) for i in range(size)])


def exchange(x):
    return lax.all_to_all(x, "dom", split_axis=0, concat_axis=0, tiled=True)


def local(special, entities, relations, head_local, rel_ids, tail_part, tail_local, neg_local):
    columns = entities.shape[1]
    factor = 1.0 / math.sqrt(columns)
    ent_dev = entities.shape[0]
    edges = head_local.shape[0]
    parts = lax.axis_size("dom")
    reps = lax.axis_size("rep")
    cap = 2 * edges // parts
    slots = parts * cap
    neg_dev = neg_local.shape[0]
    negs = parts * neg_dev
    share = neg_dev // reps
    count = relations.shape[0]
    head = head_local.reshape(1, edges)
    rel = rel_ids.reshape(1, edges)
    dom = lax.axis_index("dom")
    rep = lax.axis_index("rep")
    z, x, y, core = dom // 2, dom % 2, rep // 2, rep % 2
    place = jnp.stack([rep, z, core])
    if special:
        quarters = [(2 * y + x) ^ k for k in range(4)]
        order = [(2 * (1 - core) + q // 2, q % 2) for q in quarters]
        order = order + [(2 * core + q // 2, q % 2) for q in quarters]
    else:
        order = [(k // 2, k % 2) for k in range(2 * count)]
    picks = jnp.stack([jnp.asarray(v, I32) for pair in order for v in pair])

    slot, neg_own, request = call(
        functools.partial(slots_kernel, parts, cap),
        [((1, edges), I32), ((1, neg_dev), I32), ((parts, share, columns + 128), BF)],
        (place,),
        (),
        (
            tail_part.reshape(1, edges),
            tail_local.reshape(1, edges),
            neg_local.reshape(1, neg_dev),
            entities,
        ),
        room=60,
    )
    requests = exchange(request)
    rows, queries = call(
        query_kernel,
        [((edges, columns), BF, True), ((edges, columns), BF, True)],
        (),
        (),
        (head, rel, entities, relations),
        (slot,),
        room=60,
    )
    asked, found, neg_near = call(
        functools.partial(lookup_kernel, cap),
        [((1, slots), I32), ((slots, columns), BF), ((parts * share, columns), BF)],
        (),
        (requests, entities),
        (),
        (rows,),
    )
    got = exchange(found.reshape(parts, cap, columns)).reshape(slots, columns)
    neg_core, neg_across, neg_both = [flip(neg_near, "rep", reps, k) for k in (1, 2, 3)]

    loss, grad, away, back, keep = call(
        functools.partial(edge_kernel, factor),
        [
            ((1, edges), F32),
            ((edges, columns), BF),
            ((4, columns // 2, columns), BF if special else F32),
            ((parts, cap + neg_dev, columns), BF),
            ((4, columns // 2, columns), F32),
        ],
        (picks,),
        (slot, neg_near, neg_core, neg_across, neg_both, queries, got, rows, rel),
    )
    returned = exchange(back)

    def add(base, size, kind, after):
        return call(
            add_kernel,
            [((size, columns), kind)],
            (base.reshape(1),),
            (asked, neg_own, head, head_grads, returned),
            (),
            after,
        )[0]

    if not special:
        whole = jnp.concatenate([away, keep], axis=0).reshape(count, columns, columns)
        (head_grads,) = call(
            head_kernel, [((2 * edges, columns), BF)], (), (grad, rel, relations)
        )
        entity_grad = lax.psum(add(jnp.zeros((), I32), ent_dev, F32, ()), "rep")
        return entity_grad, lax.psum(whole, ("dom", "rep")), loss.reshape(edges)

    half, quarter = columns // 2, columns // 8

    def quad(k):
        pairs = [
            (d * 4 + r, (d ^ (k & 1)) * 4 + (r ^ (k & 2))) for d in range(8) for r in range(4)
        ]
        return lambda v: lax.ppermute(v, ("dom", "rep"), pairs)

    other = flip(away, "rep", 4, 1)
    own, *sent = call(
        pair_kernel,
        [((half, columns), F32)] + [((half, columns), BF)] * 3,
        (),
        (keep, other),
    )
    met = [quad(k + 1)(v) for k, v in enumerate(sent)]
    (head_grads,) = call(
        head_kernel,
        [((2 * edges, columns), BF)],
        (),
        (grad, rel, relations),
        (),
        (sent[0],),
    )
    own, *sent = call(
        quad_kernel,
        [((quarter, columns), F32)] + [((quarter, columns), BF)] * 3,
        (place,),
        (own, *met),
        (),
        (head_grads,),
    )
    met = [flip(v, "dom", 8, 2 * (k + 1)) for k, v in enumerate(sent)]
    (own,) = call(sum_kernel, [((quarter, columns), BF)], (), (own, *met))
    stripes = [own] + [flip(own, "dom", 8, 2 * (k + 1)) for k in range(3)]
    own = jnp.concatenate(stripes, axis=0)
    over_y = quad(2)(own)
    mine = [own, quad(1)(own), over_y, quad(1)(over_y)]
    others = [flip(v, "rep", 4, 1) for v in mine]
    relation_grad = write(
        operator_kernel,
        ((count, columns, columns), F32),
        (picks, place),
        (*mine, *others),
        [pltpu.VMEM((8, half, columns), F32), pltpu.SemaphoreType.DMA((8, 4))],
    )

    rows_half = ent_dev // 2
    leaving = add((1 - core) * rows_half, rows_half, BF, (own,))
    arrived = flip(leaving, "rep", 4, 1)
    kept = add(core * rows_half, rows_half, F32, (leaving, over_y))
    (both,) = call(both_kernel, [((rows_half, columns), BF)], (), (kept, arrived))
    across = flip(both, "rep", 4, 2)
    pieces = (both, across, flip(both, "rep", 4, 1), flip(across, "rep", 4, 1))
    entity_grad = write(
        join_kernel,
        ((ent_dev, columns), F32),
        (place,),
        pieces,
        [pltpu.VMEM((2, rows_half, columns), F32), pltpu.SemaphoreType.DMA((2,))],
    )
    return entity_grad, relation_grad, loss.reshape(edges)


def solution(mesh):
    special = dict(mesh.shape) == {"dom": 8, "rep": 4}
    return jax.shard_map(
        functools.partial(local, special),
        mesh=mesh,
        in_specs=(
            P("dom", None),
            P(),
            P(("dom", "rep")),
            P(("dom", "rep")),
            P(("dom", "rep"), None),
            P(("dom", "rep")),
            P("dom"),
        ),
        out_specs=(P("dom", None), P(), P(("dom", "rep"))),
        check_vma=False,
    )
```

```python
import functools
import math

import jax
import jax.numpy as jnp
from jax import lax
from jax.experimental import pallas as pl
from jax.experimental.pallas import tpu as pltpu
from jax.sharding import PartitionSpec as P

BF = jnp.bfloat16
F32 = jnp.float32
I32 = jnp.int32
VMEM = pl.BlockSpec(memory_space=pltpu.VMEM)
SMEM = pl.BlockSpec(memory_space=pltpu.SMEM)
FAR = pl.BlockSpec(memory_space=pltpu.HBM)


def call(body, outs, scalars, near, far=(), after=(), room=40):
    counts = len(scalars), len(near), len(far), len(after), len(outs), len(far)
    away = [index for index, out in enumerate(outs) if len(out) == 3]

    def kernel(*refs):
        refs = list(refs)
        groups = []
        for size in counts:
            groups.append(refs[:size])
            refs = refs[size:]
        scalar_refs, near_refs, far_refs, _, out_refs, held = groups
        copies = [
            pltpu.make_async_copy(source, target, refs[len(away)].at[index])
            for index, (source, target) in enumerate(zip(far_refs, held))
        ]
        for copy in copies:
            copy.start()

        def take(index):
            copies[index].wait()
            return held[index]

        filled = list(out_refs)
        for place, index in enumerate(away):
            filled[index] = refs[place]
        body(*scalar_refs, *near_refs, *([take] if far else []), *filled)
        copies_out = [
            pltpu.make_async_copy(refs[place], out_refs[index], refs[-1].at[place])
            for place, index in enumerate(away)
        ]
        for copy in copies_out:
            copy.start()
        for copy in copies_out:
            copy.wait()

    scratch = [pltpu.VMEM(x.shape, x.dtype) for x in far]
    scratch += [pltpu.VMEM(outs[index][0], outs[index][1]) for index in away]
    if far:
        scratch.append(pltpu.SemaphoreType.DMA((len(far),)))
    if away:
        scratch.append(pltpu.SemaphoreType.DMA((len(away),)))
    return pl.pallas_call(
        kernel,
        out_shape=[jax.ShapeDtypeStruct(out[0], out[1]) for out in outs],
        in_specs=[SMEM] * len(scalars)
        + [VMEM] * len(near)
        + [FAR] * (len(far) + len(after)),
        out_specs=[FAR if len(out) == 3 else VMEM for out in outs],
        scratch_shapes=scratch,
        compiler_params=pltpu.CompilerParams(vmem_limit_bytes=room * 1024 * 1024),
    )(*scalars, *near, *far, *after)


def iota(shape, axis):
    return lax.broadcasted_iota(I32, shape, axis)


def as_column(row):
    size = row.shape[1]
    step = min(128, size)
    eye = iota((step, step), 0) == iota((step, step), 1)
    pieces = [
        jnp.sum(jnp.where(eye, row[:, at : at + step], 0), axis=1, keepdims=True)
        for at in range(0, size, step)
    ]
    return jnp.concatenate(pieces, axis=0)


def as_row(column):
    size = column.shape[0]
    step = min(128, size)
    eye = iota((step, step), 0) == iota((step, step), 1)
    pieces = [
        jnp.sum(jnp.where(eye, column[at : at + step, :], 0.0), axis=0, keepdims=True)
        for at in range(0, size, step)
    ]
    return jnp.concatenate(pieces, axis=1)


def hot(mask):
    return mask.astype(F32).astype(BF)


def hot_rows(row, count):
    return hot(as_column(row) == iota((row.shape[1], count), 1))


def dot(a, b):
    return jnp.dot(a, b, preferred_element_type=F32)


def dot_t0(a, b):
    return lax.dot_general(a, b, (((0,), (0,)), ((), ())), preferred_element_type=F32)


def dot_t1(a, b):
    return lax.dot_general(a, b, (((1,), (1,)), ((), ())), preferred_element_type=F32)


def split(x):
    high = x.astype(BF)
    return high, (x - high.astype(F32)).astype(BF)


def slots_kernel(parts, cap, place_ref, take, slot_ref, neg_ref, request_ref):
    part = take(0)[...]
    edges = part.shape[1]
    slots = parts * cap
    named = (iota((parts, edges), 0) == part).astype(F32)
    before = hot(iota((edges, edges), 0) < iota((edges, edges), 1))
    earlier = dot(named.astype(BF), before)
    position = jnp.sum(earlier * named, axis=0, keepdims=True).astype(I32)
    slot = part * cap + position
    slot_ref[...] = slot
    placed = hot(iota((slots, edges), 0) == slot)
    which = iota((8, edges), 0)
    tail = take(1)[...]
    digits = jnp.where(which == 0, tail >> 7, jnp.where(which == 1, tail & 127, 0))
    found = dot_t1(digits.astype(F32).astype(BF), placed).astype(BF)
    neg = as_column(take(2)[...])
    negs = neg.shape[0]
    share = request_ref.shape[1]
    turned = iota((negs, negs), 0) == (iota((negs, negs), 1) ^ (place_ref[0] * share))
    ordered = jnp.sum(jnp.where(turned, neg, 0), axis=0, keepdims=True)
    neg_ref[...] = ordered
    entities = take(3)
    own = hot_rows(ordered, entities.shape[0])[:share]
    rows = dot(own, entities[...]).astype(BF)
    columns = rows.shape[1]
    for index in range(parts):
        request_ref[index, :, :columns] = rows
        ids = found[:, index * cap : (index + 1) * cap]
        if cap < 128:
            ids = jnp.concatenate([ids, jnp.zeros((share, 128 - cap), BF)], axis=1)
        request_ref[index, :, columns:] = ids


def query_kernel(take, rows_ref, query_ref):
    head, rel = take(0), take(1)
    entities = take(2)
    rows = dot(hot_rows(head[...], entities.shape[0]), entities[...]).astype(BF)
    rows_ref[...] = rows
    rel = as_column(rel[...])
    total = jnp.zeros(rows.shape, F32)
    operators = take(3)
    for relation in range(operators.shape[0]):
        picked = jnp.where(rel == relation, rows, jnp.zeros_like(rows))
        total = total + dot(picked, operators[relation])
    query_ref[...] = total.astype(BF)


def lookup_kernel(cap, request_ref, take, ids_ref, rows_ref, negs_ref):
    parts, share, width = request_ref.shape
    columns = rows_ref.shape[1]
    pieces = []
    for index in range(parts):
        digits = request_ref[index, :, columns : columns + cap].astype(F32)
        pieces.append(digits[0:1] * 128.0 + digits[1:2])
    ids = jnp.concatenate(pieces, axis=1).astype(I32)
    ids_ref[...] = ids
    entities = take(0)
    rows_ref[...] = dot(hot_rows(ids, entities.shape[0]), entities[...]).astype(BF)
    negs_ref[...] = jnp.concatenate(
        [request_ref[index, :, :columns].astype(F32) for index in range(parts)], axis=0
    ).astype(BF)


def operator_terms(picks_ref, first, rows_ref, rel, grad, out_ref):
    width = out_ref.shape[1]
    for place in range(out_ref.shape[0]):
        at = pl.multiple_of(picks_ref[2 * (first + place) + 1] * width, width)
        picked = jnp.where(rel == picks_ref[2 * (first + place)], grad, jnp.zeros_like(grad))
        out_ref[place] = dot_t0(rows_ref[:, pl.ds(at, width)], picked).astype(out_ref.dtype)


def edge_kernel(
    factor,
    picks_ref,
    slot_ref,
    near_ref,
    core_ref,
    across_ref,
    both_ref,
    query_ref,
    got_ref,
    rows_ref,
    rel_ref,
    loss_ref,
    weight_ref,
    prob_ref,
    grad_ref,
    away_ref,
    keep_ref,
):
    queries = query_ref[...]
    negatives = jnp.concatenate(
        [near_ref[...], core_ref[...], across_ref[...], both_ref[...]], axis=0
    )
    edges, slots = queries.shape[0], got_ref.shape[0]
    scores = dot_t1(queries, negatives) * factor
    tails = dot(hot(as_column(slot_ref[...]) == iota((edges, slots), 1)), got_ref[...])
    positive = jnp.sum(queries.astype(F32) * tails, axis=1, keepdims=True) * factor
    row_max = jnp.maximum(positive, jnp.max(scores, axis=1, keepdims=True))
    exp_pos = jnp.exp(positive - row_max)
    exp_neg = jnp.exp(scores - row_max)
    total = exp_pos + jnp.sum(exp_neg, axis=1, keepdims=True)
    loss_ref[...] = as_row(jnp.log(total) + row_max - positive)
    pull = exp_pos / total - 1.0
    weight_ref[...] = factor * pull
    prob = (exp_neg / total).astype(BF)
    prob_ref[...] = prob
    grad = (factor * (pull * tails + dot(prob, negatives))).astype(BF)
    grad_ref[...] = grad
    rel = as_column(rel_ref[...])
    operator_terms(picks_ref, 0, rows_ref, rel, grad, away_ref)
    operator_terms(picks_ref, 4, rows_ref, rel, grad, keep_ref)


def back_kernel(factor, weight_ref, prob_ref, query_ref, slot_ref, back_ref):
    queries = query_ref[...]
    edges = queries.shape[0]
    parts = back_ref.shape[0]
    slots = 2 * edges
    cap = slots // parts
    weighted = (weight_ref[...] * queries.astype(F32)).astype(BF)
    rows = dot(hot(iota((slots, edges), 0) == slot_ref[...]), weighted).astype(BF)
    negs = factor * dot_t0(prob_ref[...], queries)
    share = negs.shape[0] // parts // 4
    for index in range(parts):
        back_ref[index, :cap] = rows[index * cap : (index + 1) * cap]
        pieces = [
            negs[(turn * parts + index) * share : (turn * parts + index + 1) * share]
            for turn in range(4)
        ]
        back_ref[index, cap:] = jnp.concatenate(pieces, axis=0).astype(BF)


def pair_kernel(keep_ref, got_ref, own_ref, *out_refs):
    for index, out_ref in enumerate(out_refs):
        term = keep_ref[index + 1].astype(F32) + got_ref[index + 1].astype(F32)
        out_ref[...] = term.astype(BF)
    own_ref[...] = keep_ref[0].astype(F32) + got_ref[0].astype(F32)


def head_kernel(grad_ref, rel_ref, operators, out_ref):
    rel = as_column(rel_ref[...])
    grad = grad_ref[...]
    edges = grad.shape[0]
    total = jnp.zeros(grad.shape, F32)
    for relation in range(operators.shape[0]):
        picked = jnp.where(rel == relation, grad, jnp.zeros_like(grad))
        total = total + dot_t1(picked, operators[relation])
    out_ref[:edges], out_ref[edges:] = split(total)


def quad_kernel(place_ref, own_ref, first_ref, second_ref, third_ref, *out_refs):
    size = out_refs[0].shape[0]
    for turn, out_ref in enumerate(out_refs):
        rows = pl.ds(pl.multiple_of((place_ref[1] ^ turn) * size, size), size)
        total = own_ref[rows, :] + first_ref[rows, :].astype(F32)
        total = total + (second_ref[rows, :].astype(F32) + third_ref[rows, :].astype(F32))
        out_ref[...] = total.astype(out_ref.dtype)


def sum_kernel(own_ref, first_ref, second_ref, third_ref, out_ref):
    total = own_ref[...] + first_ref[...].astype(F32)
    total = total + (second_ref[...].astype(F32) + third_ref[...].astype(F32))
    out_ref[...] = total.astype(BF)


def operator_kernel(picks_ref, place_ref, *refs):
    sources, (out_ref, wide, sems) = refs[:-3], refs[-3:]
    width = sources[0].shape[0]
    size = width // 4
    copies = []
    for index, source in enumerate(sources):
        wide[index] = source[...].astype(F32)
        pick = 2 * ((index + 4) % 8)
        for turn in range(4):
            at = picks_ref[pick + 1] * width + (place_ref[1] ^ turn) * size
            copy = pltpu.make_async_copy(
                wide.at[index, pl.ds(turn * size, size)],
                out_ref.at[picks_ref[pick], pl.ds(pl.multiple_of(at, size), size)],
                sems.at[index, turn],
            )
            copy.start()
            copies.append(copy)
    for copy in copies:
        copy.wait()


def add_kernel(base_ref, ids_ref, neg_ref, head_ref, grads_ref, back_ref, out_ref):
    count = out_ref.shape[0]
    base = base_ref[0]

    def pick(row):
        return hot((iota((count, row.shape[1]), 0) + base) == row)

    heads = pick(head_ref[...])
    total = dot(jnp.concatenate([heads, heads], axis=1), grads_ref[...])
    parts = back_ref.shape[0]
    cap = ids_ref.shape[1] // parts
    tails = jnp.concatenate([back_ref[index, :cap] for index in range(parts)], axis=0)
    total = total + dot(pick(ids_ref[...]), tails)
    negs = back_ref[0, cap:].astype(F32)
    for index in range(1, parts):
        negs = negs + back_ref[index, cap:].astype(F32)
    own = pick(neg_ref[...])
    high, low = split(negs)
    out_ref[...] = (total + (dot(own, high) + dot(own, low))).astype(out_ref.dtype)


def both_kernel(kept_ref, arrived_ref, out_ref):
    out_ref[...] = (kept_ref[...] + arrived_ref[...].astype(F32)).astype(BF)


def join_kernel(place_ref, mine_ref, over_ref, other_ref, far_ref, out_ref, wide, sems):
    half = mine_ref.shape[0]
    core = place_ref[2]
    copies = []
    for index, (first, second, at) in enumerate(
        ((mine_ref, over_ref, core), (other_ref, far_ref, 1 - core))
    ):
        wide[index] = first[...].astype(F32) + second[...].astype(F32)
        copy = pltpu.make_async_copy(
            wide.at[index],
            out_ref.at[pl.ds(pl.multiple_of(at * half, half), half)],
            sems.at[index],
        )
        copy.start()
        copies.append(copy)
    for copy in copies:
        copy.wait()


def write(body, out, scalars, near, scratch):
    return pl.pallas_call(
        body,
        out_shape=jax.ShapeDtypeStruct(*out),
        in_specs=[SMEM] * len(scalars) + [VMEM] * len(near),
        out_specs=FAR,
        scratch_shapes=scratch,
        compiler_params=pltpu.CompilerParams(vmem_limit_bytes=40 * 1024 * 1024),
    )(*scalars, *near)


def flip(x, axis, size, bit):
    return lax.ppermute(x, axis, [(i, i ^ bit) for i in range(size)])


def exchange(x):
    return lax.all_to_all(x, "dom", split_axis=0, concat_axis=0, tiled=True)


def local(special, entities, relations, head_local, rel_ids, tail_part, tail_local, neg_local):
    columns = entities.shape[1]
    factor = 1.0 / math.sqrt(columns)
    ent_dev = entities.shape[0]
    edges = head_local.shape[0]
    parts = lax.axis_size("dom")
    reps = lax.axis_size("rep")
    cap = 2 * edges // parts
    slots = parts * cap
    neg_dev = neg_local.shape[0]
    negs = parts * neg_dev
    share = neg_dev // reps
    count = relations.shape[0]
    head = head_local.reshape(1, edges)
    rel = rel_ids.reshape(1, edges)
    dom = lax.axis_index("dom")
    rep = lax.axis_index("rep")
    z, x, y, core = dom // 2, dom % 2, rep // 2, rep % 2
    place = jnp.stack([rep, z, core])
    if special:
        quarters = [(2 * y + x) ^ k for k in range(4)]
        order = [(2 * (1 - core) + q // 2, q % 2) for q in quarters]
        order = order + [(2 * core + q // 2, q % 2) for q in quarters]
    else:
        order = [(k // 2, k % 2) for k in range(2 * count)]
    picks = jnp.stack([jnp.asarray(v, I32) for pair in order for v in pair])

    slot, neg_own, request = call(
        functools.partial(slots_kernel, parts, cap),
        [((1, edges), I32), ((1, neg_dev), I32), ((parts, share, columns + 128), BF)],
        (place,),
        (),
        (
            tail_part.reshape(1, edges),
            tail_local.reshape(1, edges),
            neg_local.reshape(1, neg_dev),
            entities,
        ),
        room=60,
    )
    requests = exchange(request)
    rows, queries = call(
        query_kernel,
        [((edges, columns), BF, True), ((edges, columns), BF, True)],
        (),
        (),
        (head, rel, entities, relations),
        (slot,),
        room=60,
    )
    asked, found, neg_near = call(
        functools.partial(lookup_kernel, cap),
        [((1, slots), I32), ((slots, columns), BF), ((parts * share, columns), BF)],
        (),
        (requests,),
        (entities,),
        (rows,),
        room=60,
    )
    got = exchange(found.reshape(parts, cap, columns)).reshape(slots, columns)
    neg_core, neg_across, neg_both = [flip(neg_near, "rep", reps, k) for k in (1, 2, 3)]

    terms = ((4, columns // 2, columns), BF if special else F32)
    loss, weight, prob, grad, away, keep = call(
        functools.partial(edge_kernel, factor),
        [
            ((1, edges), F32),
            ((edges, 1), F32),
            ((edges, negs), BF),
            ((edges, columns), BF),
            terms,
            terms,
        ],
        (picks,),
        (slot, neg_near, neg_core, neg_across, neg_both, queries, got, rows, rel),
    )
    (head_grads,) = call(
        head_kernel, [((2 * edges, columns), BF)], (), (grad, rel, relations)
    )

    def give_back(after):
        (back,) = call(
            functools.partial(back_kernel, factor),
            [((parts, cap + neg_dev, columns), BF)],
            (),
            (weight, prob, queries, slot),
            (),
            after,
        )
        return back, exchange(back)

    def add(base, size, kind, returned, after):
        return call(
            add_kernel,
            [((size, columns), kind)],
            (base.reshape(1),),
            (asked, neg_own, head, head_grads, returned),
            (),
            after,
        )[0]

    if not special:
        whole = jnp.concatenate([away, keep], axis=0).reshape(count, columns, columns)
        back, returned = give_back(())
        entity_grad = lax.psum(add(jnp.zeros((), I32), ent_dev, F32, returned, ()), "rep")
        return entity_grad, lax.psum(whole, ("dom", "rep")), loss.reshape(edges)

    half, quarter = columns // 2, columns // 8

    def quad(k):
        pairs = [
            (d * 4 + r, (d ^ (k & 1)) * 4 + (r ^ (k & 2))) for d in range(8) for r in range(4)
        ]
        return lambda v: lax.ppermute(v, ("dom", "rep"), pairs)

    other = flip(away, "rep", 4, 1)
    own, *sent = call(
        pair_kernel,
        [((half, columns), F32)] + [((half, columns), BF)] * 3,
        (),
        (keep, other),
        (),
        (head_grads,),
    )
    met = [quad(k + 1)(v) for k, v in enumerate(sent)]
    back, returned = give_back((sent[0],))
    own, *sent = call(
        quad_kernel,
        [((quarter, columns), F32)] + [((quarter, columns), BF)] * 3,
        (place,),
        (own, *met),
        (),
        (back,),
    )
    met = [flip(v, "dom", 8, 2 * (k + 1)) for k, v in enumerate(sent)]
    (own,) = call(sum_kernel, [((quarter, columns), BF)], (), (own, *met))
    stripes = [own] + [flip(own, "dom", 8, 2 * (k + 1)) for k in range(3)]
    own = jnp.concatenate(stripes, axis=0)
    over_y = quad(2)(own)
    over_x = quad(1)(own)
    mine = [own, over_x, over_y, quad(1)(over_y)]
    others = [flip(v, "rep", 4, 1) for v in mine]
    relation_grad = write(
        operator_kernel,
        ((count, columns, columns), F32),
        (picks, place),
        (*mine, *others),
        [pltpu.VMEM((8, half, columns), F32), pltpu.SemaphoreType.DMA((8, 4))],
    )

    rows_half = ent_dev // 2
    leaving = add((1 - core) * rows_half, rows_half, BF, returned, (own,))
    arrived = flip(leaving, "rep", 4, 1)
    kept = add(core * rows_half, rows_half, F32, returned, (leaving, over_x))
    (both,) = call(both_kernel, [((rows_half, columns), BF)], (), (kept, arrived))
    across = flip(both, "rep", 4, 2)
    pieces = (both, across, flip(both, "rep", 4, 1), flip(across, "rep", 4, 1))
    entity_grad = write(
        join_kernel,
        ((ent_dev, columns), F32),
        (place,),
        pieces,
        [pltpu.VMEM((2, rows_half, columns), F32), pltpu.SemaphoreType.DMA((2,))],
    )
    return entity_grad, relation_grad, loss.reshape(edges)


def solution(mesh):
    special = dict(mesh.shape) == {"dom": 8, "rep": 4}
    return jax.shard_map(
        functools.partial(local, special),
        mesh=mesh,
        in_specs=(
            P("dom", None),
            P(),
            P(("dom", "rep")),
            P(("dom", "rep")),
            P(("dom", "rep"), None),
            P(("dom", "rep")),
            P("dom"),
        ),
        out_specs=(P("dom", None), P(), P(("dom", "rep"))),
        check_vma=False,
    )
```

```python
import functools
import math

import jax
import jax.numpy as jnp
from jax import lax
from jax.experimental import pallas as pl
from jax.experimental.pallas import tpu as pltpu
from jax.sharding import PartitionSpec as P

BF = jnp.bfloat16
F32 = jnp.float32
I32 = jnp.int32
VMEM = pl.BlockSpec(memory_space=pltpu.VMEM)
SMEM = pl.BlockSpec(memory_space=pltpu.SMEM)
FAR = pl.BlockSpec(memory_space=pltpu.HBM)


def call(body, outs, scalars, near, far=(), after=(), room=40, cost=0):
    counts = len(scalars), len(near), len(far), len(after), len(outs), len(far)
    away = [index for index, out in enumerate(outs) if len(out) == 3]

    def kernel(*refs):
        refs = list(refs)
        groups = []
        for size in counts:
            groups.append(refs[:size])
            refs = refs[size:]
        scalar_refs, near_refs, far_refs, _, out_refs, held = groups
        copies = [
            pltpu.make_async_copy(source, target, refs[len(away)].at[index])
            for index, (source, target) in enumerate(zip(far_refs, held))
        ]
        for copy in copies:
            copy.start()

        def take(index):
            copies[index].wait()
            return held[index]

        filled = list(out_refs)
        for place, index in enumerate(away):
            filled[index] = refs[place]
        body(*scalar_refs, *near_refs, *([take] if far else []), *filled)
        copies_out = [
            pltpu.make_async_copy(refs[place], out_refs[index], refs[-1].at[place])
            for place, index in enumerate(away)
        ]
        for copy in copies_out:
            copy.start()
        for copy in copies_out:
            copy.wait()

    scratch = [pltpu.VMEM(x.shape, x.dtype) for x in far]
    scratch += [pltpu.VMEM(outs[index][0], outs[index][1]) for index in away]
    if far:
        scratch.append(pltpu.SemaphoreType.DMA((len(far),)))
    if away:
        scratch.append(pltpu.SemaphoreType.DMA((len(away),)))
    return pl.pallas_call(
        kernel,
        out_shape=[jax.ShapeDtypeStruct(out[0], out[1]) for out in outs],
        in_specs=[SMEM] * len(scalars)
        + [VMEM] * len(near)
        + [FAR] * (len(far) + len(after)),
        out_specs=[FAR if len(out) == 3 else VMEM for out in outs],
        scratch_shapes=scratch,
        compiler_params=pltpu.CompilerParams(vmem_limit_bytes=room * 1024 * 1024),
        cost_estimate=estimate(cost),
    )(*scalars, *near, *far, *after)


def estimate(cost):
    if not cost:
        return None
    return pl.CostEstimate(flops=0, bytes_accessed=int(cost * 3.6e6), transcendentals=0)


def iota(shape, axis):
    return lax.broadcasted_iota(I32, shape, axis)


def as_column(row):
    size = row.shape[1]
    step = min(128, size)
    eye = iota((step, step), 0) == iota((step, step), 1)
    pieces = [
        jnp.sum(jnp.where(eye, row[:, at : at + step], 0), axis=1, keepdims=True)
        for at in range(0, size, step)
    ]
    return jnp.concatenate(pieces, axis=0)


def as_row(column):
    size = column.shape[0]
    step = min(128, size)
    eye = iota((step, step), 0) == iota((step, step), 1)
    pieces = [
        jnp.sum(jnp.where(eye, column[at : at + step, :], 0.0), axis=0, keepdims=True)
        for at in range(0, size, step)
    ]
    return jnp.concatenate(pieces, axis=1)


def hot(mask):
    return mask.astype(F32).astype(BF)


def hot_rows(row, count):
    return hot(as_column(row) == iota((row.shape[1], count), 1))


def dot(a, b):
    return jnp.dot(a, b, preferred_element_type=F32)


def dot_t0(a, b):
    return lax.dot_general(a, b, (((0,), (0,)), ((), ())), preferred_element_type=F32)


def dot_t1(a, b):
    return lax.dot_general(a, b, (((1,), (1,)), ((), ())), preferred_element_type=F32)


def split(x):
    high = x.astype(BF)
    return high, (x - high.astype(F32)).astype(BF)


def slots_kernel(parts, cap, take, slot_ref, neg_ref, request_ref):
    part = take(0)[...]
    edges = part.shape[1]
    slots = parts * cap
    named = (iota((parts, edges), 0) == part).astype(F32)
    before = hot(iota((edges, edges), 0) < iota((edges, edges), 1))
    earlier = dot(named.astype(BF), before)
    position = jnp.sum(earlier * named, axis=0, keepdims=True).astype(I32)
    slot = part * cap + position
    slot_ref[...] = slot
    placed = hot(iota((slots, edges), 0) == slot)
    which = iota((8, edges), 0)
    tail = take(1)[...]
    digits = jnp.where(which == 0, tail >> 7, jnp.where(which == 1, tail & 127, 0))
    found = dot_t1(digits.astype(F32).astype(BF), placed).astype(BF)
    neg = as_column(take(2)[...])
    negs = neg.shape[0]
    share = request_ref.shape[1]
    turned = iota((negs, negs), 0) == (iota((negs, negs), 1) ^ (lax.axis_index("rep") * share))
    ordered = jnp.sum(jnp.where(turned, neg, 0), axis=0, keepdims=True)
    neg_ref[...] = ordered
    entities = take(3)
    own = hot_rows(ordered, entities.shape[0])[:share]
    rows = dot(own, entities[...]).astype(BF)
    columns = rows.shape[1]
    for index in range(parts):
        request_ref[index, :, :columns] = rows
        ids = found[:, index * cap : (index + 1) * cap]
        if cap < 128:
            ids = jnp.concatenate([ids, jnp.zeros((share, 128 - cap), BF)], axis=1)
        request_ref[index, :, columns:] = ids


def query_kernel(take, rows_ref, query_ref):
    head, rel = take(0), take(1)
    entities = take(2)
    rows = dot(hot_rows(head[...], entities.shape[0]), entities[...]).astype(BF)
    rows_ref[...] = rows
    rel = as_column(rel[...])
    total = jnp.zeros(rows.shape, F32)
    operators = take(3)
    for relation in range(operators.shape[0]):
        picked = jnp.where(rel == relation, rows, jnp.zeros_like(rows))
        total = total + dot(picked, operators[relation])
    query_ref[...] = total.astype(BF)


def lookup_kernel(cap, request_ref, entities, ids_ref, rows_ref, negs_ref):
    parts, share, width = request_ref.shape
    columns = rows_ref.shape[1]
    pieces = []
    for index in range(parts):
        digits = request_ref[index, :, columns : columns + cap].astype(F32)
        pieces.append(digits[0:1] * 128.0 + digits[1:2])
    ids = jnp.concatenate(pieces, axis=1).astype(I32)
    ids_ref[...] = ids
    rows_ref[...] = dot(hot_rows(ids, entities.shape[0]), entities[...]).astype(BF)
    negs_ref[...] = jnp.concatenate(
        [request_ref[index, :, :columns].astype(F32) for index in range(parts)], axis=0
    ).astype(BF)


def operator_terms(picks_ref, first, rows_ref, rel, grad, out_ref):
    width = out_ref.shape[1]
    for place in range(out_ref.shape[0]):
        at = pl.multiple_of(picks_ref[2 * (first + place) + 1] * width, width)
        picked = jnp.where(rel == picks_ref[2 * (first + place)], grad, jnp.zeros_like(grad))
        out_ref[place] = dot_t0(rows_ref[:, pl.ds(at, width)], picked).astype(out_ref.dtype)


def edge_kernel(
    factor,
    picks_ref,
    slot_ref,
    near_ref,
    core_ref,
    across_ref,
    both_ref,
    query_ref,
    got_ref,
    rows_ref,
    rel_ref,
    loss_ref,
    weight_ref,
    prob_ref,
    grad_ref,
    away_ref,
    keep_ref,
):
    queries = query_ref[...]
    negatives = jnp.concatenate(
        [near_ref[...], core_ref[...], across_ref[...], both_ref[...]], axis=0
    )
    edges, slots = queries.shape[0], got_ref.shape[0]
    scores = dot_t1(queries, negatives) * factor
    tails = dot(hot(as_column(slot_ref[...]) == iota((edges, slots), 1)), got_ref[...])
    positive = jnp.sum(queries.astype(F32) * tails, axis=1, keepdims=True) * factor
    row_max = jnp.maximum(positive, jnp.max(scores, axis=1, keepdims=True))
    exp_pos = jnp.exp(positive - row_max)
    exp_neg = jnp.exp(scores - row_max)
    total = exp_pos + jnp.sum(exp_neg, axis=1, keepdims=True)
    loss_ref[...] = as_row(jnp.log(total) + row_max - positive)
    pull = exp_pos / total - 1.0
    weight_ref[...] = factor * pull
    prob = (exp_neg / total).astype(BF)
    prob_ref[...] = prob
    grad = (factor * (pull * tails + dot(prob, negatives))).astype(BF)
    grad_ref[...] = grad
    rel = as_column(rel_ref[...])
    operator_terms(picks_ref, 0, rows_ref, rel, grad, away_ref)
    operator_terms(picks_ref, 4, rows_ref, rel, grad, keep_ref)


def back_kernel(factor, weight_ref, prob_ref, query_ref, slot_ref, back_ref):
    queries = query_ref[...]
    edges = queries.shape[0]
    parts = back_ref.shape[0]
    slots = 2 * edges
    cap = slots // parts
    weighted = (weight_ref[...] * queries.astype(F32)).astype(BF)
    rows = dot(hot(iota((slots, edges), 0) == slot_ref[...]), weighted).astype(BF)
    negs = factor * dot_t0(prob_ref[...], queries)
    share = negs.shape[0] // parts // 4
    for index in range(parts):
        back_ref[index, :cap] = rows[index * cap : (index + 1) * cap]
        pieces = [
            negs[(turn * parts + index) * share : (turn * parts + index + 1) * share]
            for turn in range(4)
        ]
        back_ref[index, cap:] = jnp.concatenate(pieces, axis=0).astype(BF)


def pair_kernel(keep_ref, got_ref, own_ref, sent_ref):
    half = own_ref.shape[0] // 2
    for place in range(4):
        term = keep_ref[place].astype(F32) + got_ref[place].astype(F32)
        if place < 2:
            own_ref[place * half : (place + 1) * half] = term
        else:
            sent_ref[(place - 2) * half : (place - 1) * half] = term.astype(BF)


def middle_kernel(own_ref, got_ref, keep_ref, sent_ref):
    half = keep_ref.shape[0]
    keep_ref[...] = own_ref[:half] + got_ref[:half].astype(F32)
    sent_ref[...] = (own_ref[half:] + got_ref[half:].astype(F32)).astype(BF)


def head_kernel(grad_ref, rel_ref, operators, out_ref):
    rel = as_column(rel_ref[...])
    grad = grad_ref[...]
    edges = grad.shape[0]
    total = jnp.zeros(grad.shape, F32)
    for relation in range(operators.shape[0]):
        picked = jnp.where(rel == relation, grad, jnp.zeros_like(grad))
        total = total + dot_t1(picked, operators[relation])
    out_ref[:edges], out_ref[edges:] = split(total)


def spread_kernel(place_ref, own_ref, got_ref, *out_refs):
    size = out_refs[0].shape[0]
    for turn, out_ref in enumerate(out_refs):
        rows = pl.ds(pl.multiple_of((place_ref[1] ^ turn) * size, size), size)
        total = own_ref[rows, :] + got_ref[rows, :].astype(F32)
        out_ref[...] = total.astype(out_ref.dtype)


def sum_kernel(own_ref, first_ref, second_ref, third_ref, out_ref):
    total = own_ref[...] + first_ref[...].astype(F32)
    total = total + (second_ref[...].astype(F32) + third_ref[...].astype(F32))
    out_ref[...] = total.astype(BF)


def place_operators(picks_ref, place_ref, indices, sources, out_ref, wide, sems):
    width = sources[0].shape[0]
    size = width // 4
    copies = []
    for slot, (index, source) in enumerate(zip(indices, sources)):
        wide[slot] = source[...].astype(F32)
        pick = 2 * ((index + 4) % 8)
        for turn in range(4):
            at = picks_ref[pick + 1] * width + (place_ref[1] ^ turn) * size
            copy = pltpu.make_async_copy(
                wide.at[slot, pl.ds(turn * size, size)],
                out_ref.at[picks_ref[pick], pl.ds(pl.multiple_of(at, size), size)],
                sems.at[slot, turn],
            )
            copy.start()
            copies.append(copy)
    return copies


def operator_kernel(indices, picks_ref, place_ref, *refs):
    sources, (out_ref, wide, sems) = refs[:-3], refs[-3:]
    for copy in place_operators(picks_ref, place_ref, indices, sources, out_ref, wide, sems):
        copy.wait()


def add_kernel(base_ref, ids_ref, neg_ref, head_ref, grads_ref, back_ref, out_ref):
    count = out_ref.shape[0]
    base = base_ref[0]

    def pick(row):
        return hot((iota((count, row.shape[1]), 0) + base) == row)

    heads = pick(head_ref[...])
    total = dot(jnp.concatenate([heads, heads], axis=1), grads_ref[...])
    parts = back_ref.shape[0]
    cap = ids_ref.shape[1] // parts
    tails = jnp.concatenate([back_ref[index, :cap] for index in range(parts)], axis=0)
    total = total + dot(pick(ids_ref[...]), tails)
    negs = back_ref[0, cap:].astype(F32)
    for index in range(1, parts):
        negs = negs + back_ref[index, cap:].astype(F32)
    own = pick(neg_ref[...])
    high, low = split(negs)
    out_ref[...] = (total + (dot(own, high) + dot(own, low))).astype(out_ref.dtype)


def both_kernel(kept_ref, arrived_ref, out_ref):
    out_ref[...] = (kept_ref[...] + arrived_ref[...].astype(F32)).astype(BF)


def join_kernel(
    indices, picks_ref, place_ref, mine_ref, other_ref, over_ref, far_ref, *refs
):
    sources, rest = refs[: len(indices)], refs[len(indices) :]
    _, out_ref, operators_ref, wide, sems, operators_wide, operators_sems = rest
    half = mine_ref.shape[0]
    core = place_ref[2]
    copies = []
    for index, (first, second, at) in enumerate(
        ((mine_ref, over_ref, core), (other_ref, far_ref, 1 - core))
    ):
        wide[index] = first[...].astype(F32) + second[...].astype(F32)
        copy = pltpu.make_async_copy(
            wide.at[index],
            out_ref.at[pl.ds(pl.multiple_of(at * half, half), half)],
            sems.at[index],
        )
        copy.start()
        copies.append(copy)
    copies += place_operators(
        picks_ref, place_ref, indices, sources, operators_ref, operators_wide, operators_sems
    )
    for copy in copies:
        copy.wait()


def flip(x, axis, size, bit):
    return lax.ppermute(x, axis, [(i, i ^ bit) for i in range(size)])


def exchange(x):
    return lax.all_to_all(x, "dom", split_axis=0, concat_axis=0, tiled=True)


def local(special, entities, relations, head_local, rel_ids, tail_part, tail_local, neg_local):
    columns = entities.shape[1]
    factor = 1.0 / math.sqrt(columns)
    ent_dev = entities.shape[0]
    edges = head_local.shape[0]
    parts = lax.axis_size("dom")
    reps = lax.axis_size("rep")
    cap = 2 * edges // parts
    slots = parts * cap
    neg_dev = neg_local.shape[0]
    negs = parts * neg_dev
    share = neg_dev // reps
    count = relations.shape[0]
    head = head_local.reshape(1, edges)
    rel = rel_ids.reshape(1, edges)
    dom = lax.axis_index("dom")
    rep = lax.axis_index("rep")
    z, x, y, core = dom // 2, dom % 2, rep // 2, rep % 2
    place = jnp.stack([rep, z, core])
    if special:
        quarters = [(2 * y + x) ^ k for k in range(4)]
        order = [(2 * (1 - core) + q // 2, q % 2) for q in quarters]
        order = order + [(2 * core + q // 2, q % 2) for q in quarters]
    else:
        order = [(k // 2, k % 2) for k in range(2 * count)]
    picks = jnp.stack([jnp.asarray(v, I32) for pair in order for v in pair])

    slot, neg_own, request = call(
        functools.partial(slots_kernel, parts, cap),
        [((1, edges), I32), ((1, neg_dev), I32), ((parts, share, columns + 128), BF)],
        (),
        (),
        (
            tail_part.reshape(1, edges),
            tail_local.reshape(1, edges),
            neg_local.reshape(1, neg_dev),
            entities,
        ),
        room=60,
    )
    requests = exchange(request)
    rows, queries = call(
        query_kernel,
        [((edges, columns), BF, True), ((edges, columns), BF, True)],
        (),
        (),
        (head, rel, entities, relations),
        (slot,),
        room=60,
    )
    asked, found, neg_near = call(
        functools.partial(lookup_kernel, cap),
        [((1, slots), I32), ((slots, columns), BF), ((parts * share, columns), BF)],
        (),
        (requests, entities),
        (),
        (rows,),
    )
    got = exchange(found.reshape(parts, cap, columns)).reshape(slots, columns)
    neg_core, neg_across, neg_both = [flip(neg_near, "rep", reps, k) for k in (1, 2, 3)]

    terms = ((4, columns // 2, columns), BF if special else F32)
    loss, weight, prob, grad, away, keep = call(
        functools.partial(edge_kernel, factor),
        [
            ((1, edges), F32),
            ((edges, 1), F32),
            ((edges, negs), BF),
            ((edges, columns), BF),
            terms,
            terms,
        ],
        (picks,),
        (slot, neg_near, neg_core, neg_across, neg_both, queries, got, rows, rel),
    )
    (head_grads,) = call(
        head_kernel, [((2 * edges, columns), BF)], (), (grad, rel, relations), cost=4
    )

    def give_back(after):
        (back,) = call(
            functools.partial(back_kernel, factor),
            [((parts, cap + neg_dev, columns), BF)],
            (),
            (weight, prob, queries, slot),
            (),
            after,
        )
        return back, exchange(back)

    def add(base, size, kind, returned, after):
        return call(
            add_kernel,
            [((size, columns), kind)],
            (base.reshape(1),),
            (asked, neg_own, head, head_grads, returned),
            (),
            after,
            cost=5,
        )[0]

    if not special:
        whole = jnp.concatenate([away, keep], axis=0).reshape(count, columns, columns)
        back, returned = give_back(())
        entity_grad = lax.psum(add(jnp.zeros((), I32), ent_dev, F32, returned, ()), "rep")
        return entity_grad, lax.psum(whole, ("dom", "rep")), loss.reshape(edges)

    half, quarter = columns // 2, columns // 8

    def over_y(v):
        return flip(v, "rep", 4, 2)

    def over_x(v):
        return flip(v, "dom", 8, 1)

    def over_core(v):
        return flip(v, "rep", 4, 1)

    own, sent = call(
        pair_kernel,
        [((columns, columns), F32), ((columns, columns), BF)],
        (),
        (keep, over_core(away)),
        (),
        (head_grads,),
    )
    met = over_y(sent)
    back, returned = give_back((sent,))
    own, sent = call(
        middle_kernel,
        [((half, columns), F32), ((half, columns), BF)],
        (),
        (own, met),
        (),
        (back,),
        cost=15,
    )
    own, *sent = call(
        spread_kernel,
        [((quarter, columns), F32)] + [((quarter, columns), BF)] * 3,
        (place,),
        (own, over_x(sent)),
        cost=15,
    )
    met = [flip(v, "dom", 8, 2 * (k + 1)) for k, v in enumerate(sent)]
    (own,) = call(sum_kernel, [((quarter, columns), BF)], (), (own, *met), cost=15)
    stripes = [own] + [flip(own, "dom", 8, 2 * (k + 1)) for k in range(3)]
    whole = jnp.concatenate(stripes, axis=0)

    rows_half = ent_dev // 2
    leaving = add((1 - core) * rows_half, rows_half, BF, returned, (own,))
    arrived = over_core(leaving)
    kept = add(core * rows_half, rows_half, F32, returned, (leaving,))
    (both,) = call(both_kernel, [((rows_half, columns), BF)], (), (kept, arrived))
    across = over_y(both)

    y_whole = over_y(whole)
    mine = [whole, over_x(whole), y_whole, over_x(y_whole)]
    others = [over_core(v) for v in mine]
    early, late = (0, 1, 2, 4, 5, 6), (3, 7)
    quarters = mine + others
    limit = pltpu.CompilerParams(vmem_limit_bytes=40 * 1024 * 1024)
    shape = jax.ShapeDtypeStruct((count, columns, columns), F32)
    relation_grad = pl.pallas_call(
        functools.partial(operator_kernel, early),
        out_shape=shape,
        in_specs=[SMEM] * 2 + [VMEM] * len(early),
        out_specs=FAR,
        scratch_shapes=[
            pltpu.VMEM((len(early), half, columns), F32),
            pltpu.SemaphoreType.DMA((len(early), 4)),
        ],
        compiler_params=limit,
    )(picks, place, *[quarters[k] for k in early])
    entity_grad, relation_grad = pl.pallas_call(
        functools.partial(join_kernel, late),
        out_shape=[jax.ShapeDtypeStruct((ent_dev, columns), F32), shape],
        in_specs=[SMEM] * 2 + [VMEM] * (4 + len(late)) + [FAR],
        out_specs=[FAR, FAR],
        scratch_shapes=[
            pltpu.VMEM((2, rows_half, columns), F32),
            pltpu.SemaphoreType.DMA((2,)),
            pltpu.VMEM((len(late), half, columns), F32),
            pltpu.SemaphoreType.DMA((len(late), 4)),
        ],
        input_output_aliases={6 + len(late): 1},
        compiler_params=limit,
    )(
        picks,
        place,
        both,
        over_core(both),
        across,
        over_core(across),
        *[quarters[k] for k in late],
        relation_grad,
    )
    return entity_grad, relation_grad, loss.reshape(edges)


def solution(mesh):
    special = dict(mesh.shape) == {"dom": 8, "rep": 4}
    return jax.shard_map(
        functools.partial(local, special),
        mesh=mesh,
        in_specs=(
            P("dom", None),
            P(),
            P(("dom", "rep")),
            P(("dom", "rep")),
            P(("dom", "rep"), None),
            P(("dom", "rep")),
            P("dom"),
        ),
        out_specs=(P("dom", None), P(), P(("dom", "rep"))),
        check_vma=False,
    )
```

```python
import functools
import math

import jax
import jax.numpy as jnp
from jax import lax
from jax.experimental import pallas as pl
from jax.experimental.pallas import tpu as pltpu
from jax.sharding import PartitionSpec as P

BF = jnp.bfloat16
F32 = jnp.float32
I32 = jnp.int32
VMEM = pl.BlockSpec(memory_space=pltpu.VMEM)
SMEM = pl.BlockSpec(memory_space=pltpu.SMEM)
FAR = pl.BlockSpec(memory_space=pltpu.HBM)


def call(body, outs, scalars, near, far=(), after=(), room=40, cost=0):
    counts = len(scalars), len(near), len(far), len(after), len(outs), len(far)
    away = [index for index, out in enumerate(outs) if len(out) == 3]

    def kernel(*refs):
        refs = list(refs)
        groups = []
        for size in counts:
            groups.append(refs[:size])
            refs = refs[size:]
        scalar_refs, near_refs, far_refs, _, out_refs, held = groups
        copies = [
            pltpu.make_async_copy(source, target, refs[len(away)].at[index])
            for index, (source, target) in enumerate(zip(far_refs, held))
        ]
        for copy in copies:
            copy.start()

        def take(index):
            copies[index].wait()
            return held[index]

        filled = list(out_refs)
        for place, index in enumerate(away):
            filled[index] = refs[place]
        body(*scalar_refs, *near_refs, *([take] if far else []), *filled)
        copies_out = [
            pltpu.make_async_copy(refs[place], out_refs[index], refs[-1].at[place])
            for place, index in enumerate(away)
        ]
        for copy in copies_out:
            copy.start()
        for copy in copies_out:
            copy.wait()

    scratch = [pltpu.VMEM(x.shape, x.dtype) for x in far]
    scratch += [pltpu.VMEM(outs[index][0], outs[index][1]) for index in away]
    if far:
        scratch.append(pltpu.SemaphoreType.DMA((len(far),)))
    if away:
        scratch.append(pltpu.SemaphoreType.DMA((len(away),)))
    return pl.pallas_call(
        kernel,
        out_shape=[jax.ShapeDtypeStruct(out[0], out[1]) for out in outs],
        in_specs=[SMEM] * len(scalars)
        + [VMEM] * len(near)
        + [FAR] * (len(far) + len(after)),
        out_specs=[FAR if len(out) == 3 else VMEM for out in outs],
        scratch_shapes=scratch,
        compiler_params=pltpu.CompilerParams(vmem_limit_bytes=room * 1024 * 1024),
        cost_estimate=estimate(cost),
    )(*scalars, *near, *far, *after)


def estimate(cost):
    return pl.CostEstimate(flops=1 + int(cost * 1e9), bytes_accessed=1, transcendentals=0)


def iota(shape, axis):
    return lax.broadcasted_iota(I32, shape, axis)


def as_column(row):
    size = row.shape[1]
    step = min(128, size)
    eye = iota((step, step), 0) == iota((step, step), 1)
    pieces = [
        jnp.sum(jnp.where(eye, row[:, at : at + step], 0), axis=1, keepdims=True)
        for at in range(0, size, step)
    ]
    return jnp.concatenate(pieces, axis=0)


def as_row(column):
    size = column.shape[0]
    step = min(128, size)
    eye = iota((step, step), 0) == iota((step, step), 1)
    pieces = [
        jnp.sum(jnp.where(eye, column[at : at + step, :], 0.0), axis=0, keepdims=True)
        for at in range(0, size, step)
    ]
    return jnp.concatenate(pieces, axis=1)


def hot(mask):
    return mask.astype(F32).astype(BF)


def hot_rows(row, count):
    return hot(as_column(row) == iota((row.shape[1], count), 1))


def dot(a, b):
    return jnp.dot(a, b, preferred_element_type=F32)


def dot_t0(a, b):
    return lax.dot_general(a, b, (((0,), (0,)), ((), ())), preferred_element_type=F32)


def dot_t1(a, b):
    return lax.dot_general(a, b, (((1,), (1,)), ((), ())), preferred_element_type=F32)


def split(x):
    high = x.astype(BF)
    return high, (x - high.astype(F32)).astype(BF)


def slots_kernel(parts, cap, take, slot_ref, neg_ref, request_ref):
    part = take(0)[...]
    edges = part.shape[1]
    slots = parts * cap
    named = (iota((parts, edges), 0) == part).astype(F32)
    before = hot(iota((edges, edges), 0) < iota((edges, edges), 1))
    earlier = dot(named.astype(BF), before)
    position = jnp.sum(earlier * named, axis=0, keepdims=True).astype(I32)
    slot = part * cap + position
    slot_ref[...] = slot
    placed = hot(iota((slots, edges), 0) == slot)
    which = iota((8, edges), 0)
    tail = take(1)[...]
    digits = jnp.where(which == 0, tail >> 7, jnp.where(which == 1, tail & 127, 0))
    found = dot_t1(digits.astype(F32).astype(BF), placed).astype(BF)
    neg = as_column(take(2)[...])
    negs = neg.shape[0]
    share = request_ref.shape[1]
    turned = iota((negs, negs), 0) == (iota((negs, negs), 1) ^ (lax.axis_index("rep") * share))
    ordered = jnp.sum(jnp.where(turned, neg, 0), axis=0, keepdims=True)
    neg_ref[...] = ordered
    entities = take(3)
    own = hot_rows(ordered, entities.shape[0])[:share]
    rows = dot(own, entities[...]).astype(BF)
    columns = rows.shape[1]
    for index in range(parts):
        request_ref[index, :, :columns] = rows
        ids = found[:, index * cap : (index + 1) * cap]
        if cap < 128:
            ids = jnp.concatenate([ids, jnp.zeros((share, 128 - cap), BF)], axis=1)
        request_ref[index, :, columns:] = ids


def query_kernel(take, rows_ref, query_ref):
    head, rel = take(0), take(1)
    entities = take(2)
    rows = dot(hot_rows(head[...], entities.shape[0]), entities[...]).astype(BF)
    rows_ref[...] = rows
    rel = as_column(rel[...])
    total = jnp.zeros(rows.shape, F32)
    operators = take(3)
    for relation in range(operators.shape[0]):
        picked = jnp.where(rel == relation, rows, jnp.zeros_like(rows))
        total = total + dot(picked, operators[relation])
    query_ref[...] = total.astype(BF)


def lookup_kernel(cap, request_ref, entities, ids_ref, rows_ref, negs_ref):
    parts, share, width = request_ref.shape
    columns = rows_ref.shape[1]
    pieces = []
    for index in range(parts):
        digits = request_ref[index, :, columns : columns + cap].astype(F32)
        pieces.append(digits[0:1] * 128.0 + digits[1:2])
    ids = jnp.concatenate(pieces, axis=1).astype(I32)
    ids_ref[...] = ids
    rows_ref[...] = dot(hot_rows(ids, entities.shape[0]), entities[...]).astype(BF)
    negs_ref[...] = jnp.concatenate(
        [request_ref[index, :, :columns].astype(F32) for index in range(parts)], axis=0
    ).astype(BF)


def quarter_of(special, index):
    if not special:
        return index // 2, index % 2
    rep, x = lax.axis_index("rep"), lax.axis_index("dom") & 1
    quarter = ((rep & 2) + x) ^ (index % 4)
    core = (rep & 1) ^ (1 if index < 4 else 0)
    return 2 * core + (quarter >> 1), quarter & 1


def operator_terms(special, first, rows_ref, rel, grad, out_ref):
    width = grad.shape[1] // 2
    for place in range(4):
        relation, part = quarter_of(special, first + place)
        at = part * width if isinstance(part, int) else pl.multiple_of(part * width, width)
        picked = jnp.where(rel == relation, grad, jnp.zeros_like(grad))
        term = dot_t0(rows_ref[:, pl.ds(at, width)], picked)
        out_ref[place * width : (place + 1) * width] = term.astype(out_ref.dtype)


def edge_kernel(
    factor,
    slot_ref,
    near_ref,
    core_ref,
    across_ref,
    both_ref,
    got_ref,
    take,
    loss_ref,
    grad_ref,
    back_ref,
):
    edges = slot_ref.shape[1]
    negatives = jnp.concatenate(
        [near_ref[...], core_ref[...], across_ref[...], both_ref[...]], axis=0
    )
    slots = got_ref.shape[0]
    tails = dot(hot(as_column(slot_ref[...]) == iota((edges, slots), 1)), got_ref[...])
    queries = take(0)[...]
    scores = dot_t1(queries, negatives) * factor
    positive = jnp.sum(queries.astype(F32) * tails, axis=1, keepdims=True) * factor
    row_max = jnp.maximum(positive, jnp.max(scores, axis=1, keepdims=True))
    exp_pos = jnp.exp(positive - row_max)
    exp_neg = jnp.exp(scores - row_max)
    total = exp_pos + jnp.sum(exp_neg, axis=1, keepdims=True)
    loss_ref[...] = as_row(jnp.log(total) + row_max - positive)
    pull = exp_pos / total - 1.0
    prob = (exp_neg / total).astype(BF)
    grad = (factor * (pull * tails + dot(prob, negatives))).astype(BF)
    grad_ref[...] = grad
    parts = back_ref.shape[0]
    cap = slots // parts
    weighted = (factor * pull * queries.astype(F32)).astype(BF)
    rows = dot(hot(iota((slots, edges), 0) == slot_ref[...]), weighted).astype(BF)
    negs = factor * dot_t0(prob, queries)
    share = negs.shape[0] // parts // 4
    for index in range(parts):
        back_ref[index, :cap] = rows[index * cap : (index + 1) * cap]
        pieces = [
            negs[(turn * parts + index) * share : (turn * parts + index + 1) * share]
            for turn in range(4)
        ]
        back_ref[index, cap:] = jnp.concatenate(pieces, axis=0).astype(BF)


def terms_kernel(special, grad_ref, take, away_ref, keep_ref):
    grad = grad_ref[...]
    rel = as_column(take(1)[...])
    rows_ref = take(0)
    operator_terms(special, 0, rows_ref, rel, grad, away_ref)
    operator_terms(special, 4, rows_ref, rel, grad, keep_ref)


def pair_kernel(keep_ref, got_ref, own_ref, sent_ref):
    half = own_ref.shape[0] // 2
    for place in range(4):
        at = slice(place * half, (place + 1) * half)
        term = keep_ref[at].astype(F32) + got_ref[at].astype(F32)
        if place < 2:
            own_ref[place * half : (place + 1) * half] = term
        else:
            sent_ref[(place - 2) * half : (place - 1) * half] = term.astype(BF)


def middle_kernel(own_ref, got_ref, keep_ref, sent_ref):
    half = keep_ref.shape[0]
    keep_ref[...] = own_ref[:half] + got_ref[:half].astype(F32)
    sent_ref[...] = (own_ref[half:] + got_ref[half:].astype(F32)).astype(BF)


def head_kernel(grad_ref, rel_ref, operators, out_ref):
    rel = as_column(rel_ref[...])
    grad = grad_ref[...]
    edges = grad.shape[0]
    total = jnp.zeros(grad.shape, F32)
    for relation in range(operators.shape[0]):
        picked = jnp.where(rel == relation, grad, jnp.zeros_like(grad))
        total = total + dot_t1(picked, operators[relation])
    out_ref[:edges], out_ref[edges:] = split(total)


def spread_kernel(own_ref, got_ref, *out_refs):
    size = out_refs[0].shape[0]
    for turn, out_ref in enumerate(out_refs):
        rows = pl.ds(pl.multiple_of(((lax.axis_index("dom") >> 1) ^ turn) * size, size), size)
        total = own_ref[rows, :] + got_ref[rows, :].astype(F32)
        out_ref[...] = total.astype(out_ref.dtype)


def sum_kernel(own_ref, first_ref, second_ref, third_ref, out_ref):
    total = own_ref[...] + first_ref[...].astype(F32)
    total = total + (second_ref[...].astype(F32) + third_ref[...].astype(F32))
    out_ref[...] = total.astype(BF)


def stack_kernel(*refs):
    size = refs[0].shape[0]
    for index, ref in enumerate(refs[:-1]):
        refs[-1][index * size : (index + 1) * size] = ref[...]


def place_operators(indices, sources, out_ref, wide, sems):
    width = sources[0].shape[0]
    size = width // 4
    copies = []
    for slot, (index, source) in enumerate(zip(indices, sources)):
        wide[slot] = source[...].astype(F32)
        relation, part = quarter_of(True, (index + 4) % 8)
        for turn in range(4):
            at = part * width + ((lax.axis_index("dom") >> 1) ^ turn) * size
            copy = pltpu.make_async_copy(
                wide.at[slot, pl.ds(turn * size, size)],
                out_ref.at[relation, pl.ds(pl.multiple_of(at, size), size)],
                sems.at[slot, turn],
            )
            copy.start()
            copies.append(copy)
    return copies


def operator_kernel(indices, *refs):
    sources, (out_ref, wide, sems) = refs[:-3], refs[-3:]
    for copy in place_operators(indices, sources, out_ref, wide, sems):
        copy.wait()


def add_kernel(halves, ids_ref, neg_ref, back_ref, take, *out_refs):
    parts = back_ref.shape[0]
    cap = ids_ref.shape[1] // parts
    tails = jnp.concatenate([back_ref[index, :cap] for index in range(parts)], axis=0)
    negs = back_ref[0, cap:].astype(F32)
    for index in range(1, parts):
        negs = negs + back_ref[index, cap:].astype(F32)
    high, low = split(negs)
    negs = jnp.concatenate([high, low], axis=0)
    head = take(0)[...]
    grads = take(1)
    for turn, out_ref in enumerate(out_refs):
        count = out_ref.shape[0]
        base = (lax.axis_index("rep") % 2 ^ (1 - turn)) * count if halves else 0

        def pick(row):
            return hot((iota((count, row.shape[1]), 0) + base) == row)

        total = dot(pick(ids_ref[...]), tails)
        heads = pick(head)
        total = total + dot(jnp.concatenate([heads, heads], axis=1), grads[...])
        own = pick(neg_ref[...])
        total = total + dot(jnp.concatenate([own, own], axis=1), negs)
        out_ref[...] = total.astype(out_ref.dtype)


def both_kernel(kept_ref, arrived_ref, out_ref):
    out_ref[...] = (kept_ref[...] + arrived_ref[...].astype(F32)).astype(BF)


def join_kernel(
    indices, mine_ref, other_ref, over_ref, far_ref, *refs
):
    sources, rest = refs[: len(indices)], refs[len(indices) :]
    _, out_ref, operators_ref, wide, sems, operators_wide, operators_sems = rest
    half = mine_ref.shape[0]
    core = lax.axis_index("rep") & 1
    copies = []
    for index, (first, second, at) in enumerate(
        ((mine_ref, over_ref, core), (other_ref, far_ref, 1 - core))
    ):
        wide[index] = first[...].astype(F32) + second[...].astype(F32)
        copy = pltpu.make_async_copy(
            wide.at[index],
            out_ref.at[pl.ds(pl.multiple_of(at * half, half), half)],
            sems.at[index],
        )
        copy.start()
        copies.append(copy)
    copies += place_operators(
        indices, sources, operators_ref, operators_wide, operators_sems
    )
    for copy in copies:
        copy.wait()


def flip(x, axis, size, bit):
    return lax.ppermute(x, axis, [(i, i ^ bit) for i in range(size)])


def exchange(x):
    return lax.all_to_all(x, "dom", split_axis=0, concat_axis=0, tiled=True)


def local(special, entities, relations, head_local, rel_ids, tail_part, tail_local, neg_local):
    columns = entities.shape[1]
    factor = 1.0 / math.sqrt(columns)
    ent_dev = entities.shape[0]
    edges = head_local.shape[0]
    parts = lax.axis_size("dom")
    reps = lax.axis_size("rep")
    cap = 2 * edges // parts
    slots = parts * cap
    neg_dev = neg_local.shape[0]
    negs = parts * neg_dev
    share = neg_dev // reps
    count = relations.shape[0]
    head = head_local.reshape(1, edges)
    rel = rel_ids.reshape(1, edges)
    slot, neg_own, request = call(
        functools.partial(slots_kernel, parts, cap),
        [((1, edges), I32), ((1, neg_dev), I32), ((parts, share, columns + 128), BF)],
        (),
        (),
        (
            tail_part.reshape(1, edges),
            tail_local.reshape(1, edges),
            neg_local.reshape(1, neg_dev),
            entities,
        ),
        room=60,
    )
    requests = exchange(request)
    rows, queries = call(
        query_kernel,
        [((edges, columns), BF, True), ((edges, columns), BF, True)],
        (),
        (),
        (head, rel, entities, relations),
        (slot,),
        room=60,
    )
    asked, found, neg_near = call(
        functools.partial(lookup_kernel, cap),
        [((1, slots), I32), ((slots, columns), BF), ((parts * share, columns), BF)],
        (),
        (requests, entities),
        (),
        (rows,),
    )
    got = exchange(found.reshape(parts, cap, columns)).reshape(slots, columns)
    neg_core, neg_across, neg_both = [flip(neg_near, "rep", reps, k) for k in (1, 2, 3)]

    loss, grad, back = call(
        functools.partial(edge_kernel, factor),
        [
            ((1, edges), F32),
            ((edges, columns), BF),
            ((parts, cap + neg_dev, columns), BF),
        ],
        (),
        (slot, neg_near, neg_core, neg_across, neg_both, got),
        (queries,),
    )
    returned = exchange(back)
    kind = BF if special else F32
    away, keep = call(
        functools.partial(terms_kernel, special),
        [((2 * columns, columns), kind), ((2 * columns, columns), kind)],
        (),
        (grad,),
        (rows, rel),
        (back,),
    )

    def head_terms(after):
        return call(
            head_kernel,
            [((2 * edges, columns), BF)],
            (),
            (grad, rel, relations),
            (),
            after,
            cost=0,
        )[0]

    def add(outs, after):
        return call(
            functools.partial(add_kernel, special),
            outs,
            (),
            (asked, neg_own, returned),
            (head, head_grads),
            after,
        )

    if not special:
        whole = jnp.concatenate([away, keep], axis=0)
        whole = whole.reshape(count, columns, columns)
        head_grads = head_terms(())
        (added,) = add([((ent_dev, columns), F32)], ())
        entity_grad = lax.psum(added, "rep")
        return entity_grad, lax.psum(whole, ("dom", "rep")), loss.reshape(edges)

    half, quarter = columns // 2, columns // 8

    def over_y(v):
        return flip(v, "rep", 4, 2)

    def over_x(v):
        return flip(v, "dom", 8, 1)

    def over_core(v):
        return flip(v, "rep", 4, 1)

    own, sent = call(
        pair_kernel,
        [((columns, columns), F32), ((columns, columns), BF)],
        (),
        (keep, over_core(away)),
    )
    own, sent = call(
        middle_kernel,
        [((half, columns), F32), ((half, columns), BF)],
        (),
        (own, over_y(sent)),
        cost=0,
    )
    head_grads = head_terms((sent,))
    own, *sent = call(
        spread_kernel,
        [((quarter, columns), F32)] + [((quarter, columns), BF)] * 3,
        (),
        (own, over_x(sent)),
        (),
        (head_grads,),
        cost=0,
    )
    met = [flip(v, "dom", 8, 2 * (k + 1)) for k, v in enumerate(sent)]
    rows_half = ent_dev // 2
    leaving, kept = add(
        [((rows_half, columns), BF), ((rows_half, columns), F32)], tuple(met)
    )
    arrived = over_core(leaving)
    (own,) = call(
        sum_kernel, [((quarter, columns), BF)], (), (own, *met), cost=0
    )
    stripes = [own] + [flip(own, "dom", 8, 2 * (k + 1)) for k in range(3)]
    (whole,) = call(
        stack_kernel, [((half, columns), BF)], (), stripes, cost=0
    )
    (both,) = call(both_kernel, [((rows_half, columns), BF)], (), (kept, arrived))
    across = over_y(both)

    y_whole = over_y(whole)
    mine = [whole, over_x(whole), y_whole, over_x(y_whole)]
    others = [over_core(v) for v in mine]
    early, late = (0, 1, 2, 4, 5, 6), (3, 7)
    quarters = mine + others
    limit = pltpu.CompilerParams(vmem_limit_bytes=40 * 1024 * 1024)
    shape = jax.ShapeDtypeStruct((count, columns, columns), F32)
    relation_grad = pl.pallas_call(
        functools.partial(operator_kernel, early),
        out_shape=shape,
        in_specs=[VMEM] * len(early),
        out_specs=FAR,
        scratch_shapes=[
            pltpu.VMEM((len(early), half, columns), F32),
            pltpu.SemaphoreType.DMA((len(early), 4)),
        ],
        compiler_params=limit,
    )(*[quarters[k] for k in early])
    entity_grad, relation_grad = pl.pallas_call(
        functools.partial(join_kernel, late),
        out_shape=[jax.ShapeDtypeStruct((ent_dev, columns), F32), shape],
        in_specs=[VMEM] * (4 + len(late)) + [FAR],
        out_specs=[FAR, FAR],
        scratch_shapes=[
            pltpu.VMEM((2, rows_half, columns), F32),
            pltpu.SemaphoreType.DMA((2,)),
            pltpu.VMEM((len(late), half, columns), F32),
            pltpu.SemaphoreType.DMA((len(late), 4)),
        ],
        input_output_aliases={4 + len(late): 1},
        compiler_params=limit,
    )(
        both,
        over_core(both),
        across,
        over_core(across),
        *[quarters[k] for k in late],
        relation_grad,
    )
    return entity_grad, relation_grad, loss.reshape(edges)


def solution(mesh):
    special = dict(mesh.shape) == {"dom": 8, "rep": 4}
    return jax.shard_map(
        functools.partial(local, special),
        mesh=mesh,
        in_specs=(
            P("dom", None),
            P(),
            P(("dom", "rep")),
            P(("dom", "rep")),
            P(("dom", "rep"), None),
            P(("dom", "rep")),
            P("dom"),
        ),
        out_specs=(P("dom", None), P(), P(("dom", "rep"))),
        check_vma=False,
    )
```

```python
import functools
import math

import jax
import jax.numpy as jnp
from jax import lax
from jax.experimental import pallas as pl
from jax.experimental.pallas import tpu as pltpu
from jax.sharding import PartitionSpec as P

BF = jnp.bfloat16
F32 = jnp.float32
I32 = jnp.int32
VMEM = pl.BlockSpec(memory_space=pltpu.VMEM)
SMEM = pl.BlockSpec(memory_space=pltpu.SMEM)
FAR = pl.BlockSpec(memory_space=pltpu.HBM)


def call(body, outs, scalars, near, far=(), after=(), room=40, cost=0):
    counts = len(scalars), len(near), len(far), len(after), len(outs), len(far)
    away = [index for index, out in enumerate(outs) if len(out) == 3]

    def kernel(*refs):
        refs = list(refs)
        groups = []
        for size in counts:
            groups.append(refs[:size])
            refs = refs[size:]
        scalar_refs, near_refs, far_refs, _, out_refs, held = groups
        copies = [
            pltpu.make_async_copy(source, target, refs[len(away)].at[index])
            for index, (source, target) in enumerate(zip(far_refs, held))
        ]
        for copy in copies:
            copy.start()

        def take(index):
            copies[index].wait()
            return held[index]

        filled = list(out_refs)
        for place, index in enumerate(away):
            filled[index] = refs[place]
        body(*scalar_refs, *near_refs, *([take] if far else []), *filled)
        copies_out = [
            pltpu.make_async_copy(refs[place], out_refs[index], refs[-1].at[place])
            for place, index in enumerate(away)
        ]
        for copy in copies_out:
            copy.start()
        for copy in copies_out:
            copy.wait()

    scratch = [pltpu.VMEM(x.shape, x.dtype) for x in far]
    scratch += [pltpu.VMEM(outs[index][0], outs[index][1]) for index in away]
    if far:
        scratch.append(pltpu.SemaphoreType.DMA((len(far),)))
    if away:
        scratch.append(pltpu.SemaphoreType.DMA((len(away),)))
    return pl.pallas_call(
        kernel,
        out_shape=[jax.ShapeDtypeStruct(out[0], out[1]) for out in outs],
        in_specs=[SMEM] * len(scalars)
        + [VMEM] * len(near)
        + [FAR] * (len(far) + len(after)),
        out_specs=[FAR if len(out) == 3 else VMEM for out in outs],
        scratch_shapes=scratch,
        compiler_params=pltpu.CompilerParams(vmem_limit_bytes=room * 1024 * 1024),
        cost_estimate=estimate(cost),
    )(*scalars, *near, *far, *after)


def estimate(cost):
    return pl.CostEstimate(flops=1 + int(cost * 1e9), bytes_accessed=1, transcendentals=0)


def iota(shape, axis):
    return lax.broadcasted_iota(I32, shape, axis)


def as_column(row):
    size = row.shape[1]
    step = min(128, size)
    eye = iota((step, step), 0) == iota((step, step), 1)
    pieces = [
        jnp.sum(jnp.where(eye, row[:, at : at + step], 0), axis=1, keepdims=True)
        for at in range(0, size, step)
    ]
    return jnp.concatenate(pieces, axis=0)


def as_row(column):
    size = column.shape[0]
    step = min(128, size)
    eye = iota((step, step), 0) == iota((step, step), 1)
    pieces = [
        jnp.sum(jnp.where(eye, column[at : at + step, :], 0.0), axis=0, keepdims=True)
        for at in range(0, size, step)
    ]
    return jnp.concatenate(pieces, axis=1)


def hot(mask):
    return mask.astype(F32).astype(BF)


def hot_rows(row, count):
    return hot(as_column(row) == iota((row.shape[1], count), 1))


def dot(a, b):
    return jnp.dot(a, b, preferred_element_type=F32)


def dot_t0(a, b):
    return lax.dot_general(a, b, (((0,), (0,)), ((), ())), preferred_element_type=F32)


def dot_t1(a, b):
    return lax.dot_general(a, b, (((1,), (1,)), ((), ())), preferred_element_type=F32)


def split(x):
    high = x.astype(BF)
    return high, (x - high.astype(F32)).astype(BF)


def slots_kernel(parts, cap, take, slot_ref, neg_ref, request_ref):
    part = take(0)[...]
    edges = part.shape[1]
    slots = parts * cap
    named = (iota((parts, edges), 0) == part).astype(F32)
    before = hot(iota((edges, edges), 0) < iota((edges, edges), 1))
    earlier = dot(named.astype(BF), before)
    position = jnp.sum(earlier * named, axis=0, keepdims=True).astype(I32)
    slot = part * cap + position
    slot_ref[...] = slot
    placed = hot(iota((slots, edges), 0) == slot)
    which = iota((8, edges), 0)
    tail = take(1)[...]
    digits = jnp.where(which == 0, tail >> 7, jnp.where(which == 1, tail & 127, 0))
    found = dot_t1(digits.astype(F32).astype(BF), placed).astype(BF)
    neg = as_column(take(2)[...])
    negs = neg.shape[0]
    share = request_ref.shape[1]
    turned = iota((negs, negs), 0) == (iota((negs, negs), 1) ^ (lax.axis_index("rep") * share))
    ordered = jnp.sum(jnp.where(turned, neg, 0), axis=0, keepdims=True)
    neg_ref[...] = ordered
    entities = take(3)
    own = hot_rows(ordered, entities.shape[0])[:share]
    rows = dot(own, entities[...]).astype(BF)
    columns = rows.shape[1]
    for index in range(parts):
        request_ref[index, :, :columns] = rows
        ids = found[:, index * cap : (index + 1) * cap]
        if cap < 128:
            ids = jnp.concatenate([ids, jnp.zeros((share, 128 - cap), BF)], axis=1)
        request_ref[index, :, columns:] = ids


def query_kernel(take, rows_ref, query_ref):
    head, rel = take(0), take(1)
    entities = take(2)
    rows = dot(hot_rows(head[...], entities.shape[0]), entities[...]).astype(BF)
    rows_ref[...] = rows
    rel = as_column(rel[...])
    total = jnp.zeros(rows.shape, F32)
    operators = take(3)
    for relation in range(operators.shape[0]):
        picked = jnp.where(rel == relation, rows, jnp.zeros_like(rows))
        total = total + dot(picked, operators[relation])
    query_ref[...] = total.astype(BF)


def lookup_kernel(cap, request_ref, entities, ids_ref, rows_ref, negs_ref):
    parts, share, width = request_ref.shape
    columns = rows_ref.shape[1]
    pieces = []
    for index in range(parts):
        digits = request_ref[index, :, columns : columns + cap].astype(F32)
        pieces.append(digits[0:1] * 128.0 + digits[1:2])
    ids = jnp.concatenate(pieces, axis=1).astype(I32)
    ids_ref[...] = ids
    rows_ref[...] = dot(hot_rows(ids, entities.shape[0]), entities[...]).astype(BF)
    negs_ref[...] = jnp.concatenate(
        [request_ref[index, :, :columns].astype(F32) for index in range(parts)], axis=0
    ).astype(BF)


def quarter_of(special, index):
    if not special:
        return index // 2, index % 2
    rep, x = lax.axis_index("rep"), lax.axis_index("dom") & 1
    quarter = ((rep & 2) + x) ^ (index % 4)
    core = (rep & 1) ^ (1 if index < 4 else 0)
    return 2 * core + (quarter >> 1), quarter & 1


def operator_terms(special, first, rows_ref, rel, grad, out_ref):
    width = grad.shape[1] // 2
    for place in range(4):
        relation, part = quarter_of(special, first + place)
        at = part * width if isinstance(part, int) else pl.multiple_of(part * width, width)
        picked = jnp.where(rel == relation, grad, jnp.zeros_like(grad))
        term = dot_t0(rows_ref[:, pl.ds(at, width)], picked)
        out_ref[place * width : (place + 1) * width] = term.astype(out_ref.dtype)


def edge_kernel(
    factor,
    slot_ref,
    near_ref,
    core_ref,
    across_ref,
    both_ref,
    got_ref,
    take,
    loss_ref,
    grad_ref,
    back_ref,
):
    edges = slot_ref.shape[1]
    negatives = jnp.concatenate(
        [near_ref[...], core_ref[...], across_ref[...], both_ref[...]], axis=0
    )
    slots = got_ref.shape[0]
    tails = dot(hot(as_column(slot_ref[...]) == iota((edges, slots), 1)), got_ref[...])
    queries = take(0)[...]
    scores = dot_t1(queries, negatives) * factor
    positive = jnp.sum(queries.astype(F32) * tails, axis=1, keepdims=True) * factor
    row_max = jnp.maximum(positive, jnp.max(scores, axis=1, keepdims=True))
    exp_pos = jnp.exp(positive - row_max)
    exp_neg = jnp.exp(scores - row_max)
    total = exp_pos + jnp.sum(exp_neg, axis=1, keepdims=True)
    loss_ref[...] = as_row(jnp.log(total) + row_max - positive)
    pull = exp_pos / total - 1.0
    prob = (exp_neg / total).astype(BF)
    grad = (factor * (pull * tails + dot(prob, negatives))).astype(BF)
    grad_ref[...] = grad
    parts = back_ref.shape[0]
    cap = slots // parts
    weighted = (factor * pull * queries.astype(F32)).astype(BF)
    rows = dot(hot(iota((slots, edges), 0) == slot_ref[...]), weighted).astype(BF)
    negs = factor * dot_t0(prob, queries)
    share = negs.shape[0] // parts // 4
    for index in range(parts):
        back_ref[index, :cap] = rows[index * cap : (index + 1) * cap]
        pieces = [
            negs[(turn * parts + index) * share : (turn * parts + index + 1) * share]
            for turn in range(4)
        ]
        back_ref[index, cap:] = jnp.concatenate(pieces, axis=0).astype(BF)


def terms_kernel(special, first, grad_ref, rows_ref, rel_ref, out_ref):
    operator_terms(special, first, rows_ref, as_column(rel_ref[...]), grad_ref[...], out_ref)


def pair_kernel(keep_ref, got_ref, own_ref, sent_ref):
    half = own_ref.shape[0] // 2
    for place in range(4):
        at = slice(place * half, (place + 1) * half)
        term = keep_ref[at].astype(F32) + got_ref[at].astype(F32)
        if place < 2:
            own_ref[place * half : (place + 1) * half] = term
        else:
            sent_ref[(place - 2) * half : (place - 1) * half] = term.astype(BF)


def middle_kernel(own_ref, got_ref, keep_ref, sent_ref):
    half = keep_ref.shape[0]
    keep_ref[...] = own_ref[:half] + got_ref[:half].astype(F32)
    sent_ref[...] = (own_ref[half:] + got_ref[half:].astype(F32)).astype(BF)


def head_kernel(grad_ref, rel_ref, operators, out_ref):
    rel = as_column(rel_ref[...])
    grad = grad_ref[...]
    edges = grad.shape[0]
    total = jnp.zeros(grad.shape, F32)
    for relation in range(operators.shape[0]):
        picked = jnp.where(rel == relation, grad, jnp.zeros_like(grad))
        total = total + dot_t1(picked, operators[relation])
    out_ref[:edges], out_ref[edges:] = split(total)


def spread_kernel(own_ref, got_ref, *out_refs):
    size = out_refs[0].shape[0]
    for turn, out_ref in enumerate(out_refs):
        rows = pl.ds(pl.multiple_of(((lax.axis_index("dom") >> 1) ^ turn) * size, size), size)
        total = own_ref[rows, :] + got_ref[rows, :].astype(F32)
        out_ref[...] = total.astype(out_ref.dtype)


def sum_kernel(own_ref, first_ref, second_ref, third_ref, out_ref):
    total = own_ref[...] + first_ref[...].astype(F32)
    total = total + (second_ref[...].astype(F32) + third_ref[...].astype(F32))
    out_ref[...] = total.astype(BF)


def stack_kernel(*refs):
    size = refs[0].shape[0]
    for index, ref in enumerate(refs[:-1]):
        refs[-1][index * size : (index + 1) * size] = ref[...]


def half_kernel(which, in_ref, out_ref):
    size = out_ref.shape[0]
    out_ref[...] = in_ref[which * size : (which + 1) * size]


def place_operators(places, sources, out_ref, wide, sems):
    width = out_ref.shape[1] // 2
    size = width // 4
    copies = []
    for slot, ((index, first), source) in enumerate(zip(places, sources)):
        wide[slot, : source.shape[0]] = source[...].astype(F32)
        relation, part = quarter_of(True, (index + 4) % 8)
        for turn in range(source.shape[0] // size):
            at = part * width + ((lax.axis_index("dom") >> 1) ^ (first + turn)) * size
            copy = pltpu.make_async_copy(
                wide.at[slot, pl.ds(turn * size, size)],
                out_ref.at[relation, pl.ds(pl.multiple_of(at, size), size)],
                sems.at[slot, turn],
            )
            copy.start()
            copies.append(copy)
    return copies


def operator_kernel(indices, *refs):
    sources, (out_ref, wide, sems) = refs[:-3], refs[-3:]
    for copy in place_operators(indices, sources, out_ref, wide, sems):
        copy.wait()


def add_kernel(halves, away, ids_ref, neg_ref, back_ref, take, *out_refs):
    parts = back_ref.shape[0]
    cap = ids_ref.shape[1] // parts
    tails = jnp.concatenate([back_ref[index, :cap] for index in range(parts)], axis=0)
    negs = back_ref[0, cap:].astype(F32)
    for index in range(1, parts):
        negs = negs + back_ref[index, cap:].astype(F32)
    high, low = split(negs)
    negs = jnp.concatenate([high, low], axis=0)
    head = take(0)[...]
    grads = take(1)
    for out_ref in out_refs:
        count = out_ref.shape[0]
        base = ((lax.axis_index("rep") & 1) ^ away) * count if halves else 0

        def pick(row):
            return hot((iota((count, row.shape[1]), 0) + base) == row)

        total = dot(pick(ids_ref[...]), tails)
        heads = pick(head)
        total = total + dot(jnp.concatenate([heads, heads], axis=1), grads[...])
        own = pick(neg_ref[...])
        total = total + dot(jnp.concatenate([own, own], axis=1), negs)
        out_ref[...] = total.astype(out_ref.dtype)


def both_kernel(kept_ref, arrived_ref, out_ref):
    out_ref[...] = (kept_ref[...] + arrived_ref[...].astype(F32)).astype(BF)


def join_kernel(
    indices, mine_ref, other_ref, over_ref, far_ref, *refs
):
    sources, rest = refs[: len(indices)], refs[len(indices) :]
    _, out_ref, operators_ref, wide, sems, operators_wide, operators_sems = rest
    half = mine_ref.shape[0]
    core = lax.axis_index("rep") & 1
    copies = []
    for index, (first, second, at) in enumerate(
        ((mine_ref, over_ref, core), (other_ref, far_ref, 1 - core))
    ):
        wide[index] = first[...].astype(F32) + second[...].astype(F32)
        copy = pltpu.make_async_copy(
            wide.at[index],
            out_ref.at[pl.ds(pl.multiple_of(at * half, half), half)],
            sems.at[index],
        )
        copy.start()
        copies.append(copy)
    copies += place_operators(
        indices, sources, operators_ref, operators_wide, operators_sems
    )
    for copy in copies:
        copy.wait()


def flip(x, axis, size, bit):
    return lax.ppermute(x, axis, [(i, i ^ bit) for i in range(size)])


def exchange(x):
    return lax.all_to_all(x, "dom", split_axis=0, concat_axis=0, tiled=True)


def local(special, entities, relations, head_local, rel_ids, tail_part, tail_local, neg_local):
    columns = entities.shape[1]
    factor = 1.0 / math.sqrt(columns)
    ent_dev = entities.shape[0]
    edges = head_local.shape[0]
    parts = lax.axis_size("dom")
    reps = lax.axis_size("rep")
    cap = 2 * edges // parts
    slots = parts * cap
    neg_dev = neg_local.shape[0]
    negs = parts * neg_dev
    share = neg_dev // reps
    count = relations.shape[0]
    head = head_local.reshape(1, edges)
    rel = rel_ids.reshape(1, edges)
    slot, neg_own, request = call(
        functools.partial(slots_kernel, parts, cap),
        [((1, edges), I32), ((1, neg_dev), I32), ((parts, share, columns + 128), BF)],
        (),
        (),
        (
            tail_part.reshape(1, edges),
            tail_local.reshape(1, edges),
            neg_local.reshape(1, neg_dev),
            entities,
        ),
        room=60,
    )
    requests = exchange(request)
    rows, queries = call(
        query_kernel,
        [((edges, columns), BF, True), ((edges, columns), BF, True)],
        (),
        (),
        (head, rel, entities, relations),
        (slot,),
        room=60,
    )
    asked, found, neg_near = call(
        functools.partial(lookup_kernel, cap),
        [((1, slots), I32), ((slots, columns), BF), ((parts * share, columns), BF)],
        (),
        (requests, entities),
        (),
        (rows,),
    )
    got = exchange(found.reshape(parts, cap, columns)).reshape(slots, columns)
    neg_core, neg_across, neg_both = [flip(neg_near, "rep", reps, k) for k in (1, 2, 3)]

    loss, grad, back = call(
        functools.partial(edge_kernel, factor),
        [
            ((1, edges), F32),
            ((edges, columns), BF),
            ((parts, cap + neg_dev, columns), BF),
        ],
        (),
        (slot, neg_near, neg_core, neg_across, neg_both, got),
        (queries,),
    )
    returned = exchange(back)
    kind = BF if special else F32

    def terms(first, after):
        return call(
            functools.partial(terms_kernel, special, first),
            [((2 * columns, columns), kind)],
            (),
            (grad, rows, rel),
            (),
            after,
        )[0]

    away = terms(0, (back,))
    keep = terms(4, (away,))

    def head_terms(after):
        return call(
            head_kernel,
            [((2 * edges, columns), BF)],
            (),
            (grad, rel, relations),
            (),
            after,
            cost=0,
        )[0]

    def add(away, outs, after, cost=0):
        return call(
            functools.partial(add_kernel, special, away),
            outs,
            (),
            (asked, neg_own, returned),
            (head, head_grads),
            after,
            cost=cost,
        )

    if not special:
        whole = jnp.concatenate([away, keep], axis=0)
        whole = whole.reshape(count, columns, columns)
        head_grads = head_terms(())
        (added,) = add(0, [((ent_dev, columns), F32)], ())
        entity_grad = lax.psum(added, "rep")
        return entity_grad, lax.psum(whole, ("dom", "rep")), loss.reshape(edges)

    half, quarter = columns // 2, columns // 8

    def over_y(v):
        return flip(v, "rep", 4, 2)

    def over_x(v):
        return flip(v, "dom", 8, 1)

    def over_core(v):
        return flip(v, "rep", 4, 1)

    own, sent = call(
        pair_kernel,
        [((columns, columns), F32), ((columns, columns), BF)],
        (),
        (keep, over_core(away)),
    )
    own, sent = call(
        middle_kernel,
        [((half, columns), F32), ((half, columns), BF)],
        (),
        (own, over_y(sent)),
        cost=0,
    )
    head_grads = head_terms((sent,))
    own, *sent = call(
        spread_kernel,
        [((quarter, columns), F32)] + [((quarter, columns), BF)] * 3,
        (),
        (own, over_x(sent)),
        (),
        (head_grads,),
        cost=0,
    )
    met = [flip(v, "dom", 8, 2 * (k + 1)) for k, v in enumerate(sent)]
    rows_half = ent_dev // 2
    (leaving,) = add(1, [((rows_half, columns), BF)], (sent[0],))
    (kept,) = add(0, [((rows_half, columns), F32)], (leaving,), 20)
    arrived = over_core(leaving)
    (own,) = call(
        sum_kernel, [((quarter, columns), BF)], (), (own, *met), (), (kept,), cost=100
    )
    stripes = [own] + [flip(own, "dom", 8, 2 * (k + 1)) for k in range(3)]
    (whole,) = call(
        stack_kernel, [((half, columns), BF)], (), stripes, cost=0
    )
    (both,) = call(both_kernel, [((rows_half, columns), BF)], (), (kept, arrived))
    across = over_y(both)

    y_whole = over_y(whole)
    x_whole = over_x(whole)

    def half_of(which, v):
        return call(
            functools.partial(half_kernel, which), [((half // 2, columns), BF)], (), (v,)
        )[0]

    mine = [whole, x_whole, y_whole]
    mine += [over_y(half_of(0, x_whole)), over_x(half_of(1, y_whole))]
    places = [(0, 0), (1, 0), (2, 0), (3, 0), (3, 2)]
    places += [(4 + index, first) for index, first in places]
    quarters = mine + [over_core(v) for v in mine]
    early, late = (0, 1, 2, 5, 6, 7), (3, 4, 8, 9)
    limit = pltpu.CompilerParams(vmem_limit_bytes=40 * 1024 * 1024)
    shape = jax.ShapeDtypeStruct((count, columns, columns), F32)
    relation_grad = pl.pallas_call(
        functools.partial(operator_kernel, [places[k] for k in early]),
        out_shape=shape,
        in_specs=[VMEM] * len(early),
        out_specs=FAR,
        scratch_shapes=[
            pltpu.VMEM((len(early), half, columns), F32),
            pltpu.SemaphoreType.DMA((len(early), 4)),
        ],
        compiler_params=limit,
    )(*[quarters[k] for k in early])
    entity_grad, relation_grad = pl.pallas_call(
        functools.partial(join_kernel, [places[k] for k in late]),
        out_shape=[jax.ShapeDtypeStruct((ent_dev, columns), F32), shape],
        in_specs=[VMEM] * (4 + len(late)) + [FAR],
        out_specs=[FAR, FAR],
        scratch_shapes=[
            pltpu.VMEM((2, rows_half, columns), F32),
            pltpu.SemaphoreType.DMA((2,)),
            pltpu.VMEM((len(late), half, columns), F32),
            pltpu.SemaphoreType.DMA((len(late), 4)),
        ],
        input_output_aliases={4 + len(late): 1},
        compiler_params=limit,
    )(
        both,
        over_core(both),
        across,
        over_core(across),
        *[quarters[k] for k in late],
        relation_grad,
    )
    return entity_grad, relation_grad, loss.reshape(edges)


def solution(mesh):
    special = dict(mesh.shape) == {"dom": 8, "rep": 4}
    return jax.shard_map(
        functools.partial(local, special),
        mesh=mesh,
        in_specs=(
            P("dom", None),
            P(),
            P(("dom", "rep")),
            P(("dom", "rep")),
            P(("dom", "rep"), None),
            P(("dom", "rep")),
            P("dom"),
        ),
        out_specs=(P("dom", None), P(), P(("dom", "rep"))),
        check_vma=False,
    )
```

```python
import functools
import math

import jax
import jax.numpy as jnp
from jax import lax
from jax.experimental import pallas as pl
from jax.experimental.pallas import tpu as pltpu
from jax.sharding import PartitionSpec as P

BF = jnp.bfloat16
F32 = jnp.float32
I32 = jnp.int32
VMEM = pl.BlockSpec(memory_space=pltpu.VMEM)
SMEM = pl.BlockSpec(memory_space=pltpu.SMEM)
FAR = pl.BlockSpec(memory_space=pltpu.HBM)


def call(body, outs, scalars, near, far=(), after=(), room=40, cost=0):
    counts = len(scalars), len(near), len(far), len(after), len(outs), len(far)
    away = [index for index, out in enumerate(outs) if len(out) == 3]

    def kernel(*refs):
        refs = list(refs)
        groups = []
        for size in counts:
            groups.append(refs[:size])
            refs = refs[size:]
        scalar_refs, near_refs, far_refs, _, out_refs, held = groups
        copies = [
            pltpu.make_async_copy(source, target, refs[len(away)].at[index])
            for index, (source, target) in enumerate(zip(far_refs, held))
        ]
        for copy in copies:
            copy.start()

        def take(index):
            copies[index].wait()
            return held[index]

        filled = list(out_refs)
        for place, index in enumerate(away):
            filled[index] = refs[place]
        body(*scalar_refs, *near_refs, *([take] if far else []), *filled)
        copies_out = [
            pltpu.make_async_copy(refs[place], out_refs[index], refs[-1].at[place])
            for place, index in enumerate(away)
        ]
        for copy in copies_out:
            copy.start()
        for copy in copies_out:
            copy.wait()

    scratch = [pltpu.VMEM(x.shape, x.dtype) for x in far]
    scratch += [pltpu.VMEM(outs[index][0], outs[index][1]) for index in away]
    if far:
        scratch.append(pltpu.SemaphoreType.DMA((len(far),)))
    if away:
        scratch.append(pltpu.SemaphoreType.DMA((len(away),)))
    return pl.pallas_call(
        kernel,
        out_shape=[jax.ShapeDtypeStruct(out[0], out[1]) for out in outs],
        in_specs=[SMEM] * len(scalars)
        + [VMEM] * len(near)
        + [FAR] * (len(far) + len(after)),
        out_specs=[FAR if len(out) == 3 else VMEM for out in outs],
        scratch_shapes=scratch,
        compiler_params=pltpu.CompilerParams(vmem_limit_bytes=room * 1024 * 1024),
        cost_estimate=estimate(cost),
    )(*scalars, *near, *far, *after)


def estimate(cost):
    return pl.CostEstimate(flops=1 + int(cost * 1e9), bytes_accessed=1, transcendentals=0)


def iota(shape, axis):
    return lax.broadcasted_iota(I32, shape, axis)


def as_column(row):
    size = row.shape[1]
    step = min(128, size)
    eye = iota((step, step), 0) == iota((step, step), 1)
    pieces = [
        jnp.sum(jnp.where(eye, row[:, at : at + step], 0), axis=1, keepdims=True)
        for at in range(0, size, step)
    ]
    return jnp.concatenate(pieces, axis=0)


def as_row(column):
    size = column.shape[0]
    step = min(128, size)
    eye = iota((step, step), 0) == iota((step, step), 1)
    pieces = [
        jnp.sum(jnp.where(eye, column[at : at + step, :], 0.0), axis=0, keepdims=True)
        for at in range(0, size, step)
    ]
    return jnp.concatenate(pieces, axis=1)


def hot(mask):
    return mask.astype(F32).astype(BF)


def hot_rows(row, count):
    return hot(as_column(row) == iota((row.shape[1], count), 1))


def dot(a, b):
    return jnp.dot(a, b, preferred_element_type=F32)


def dot_t0(a, b):
    return lax.dot_general(a, b, (((0,), (0,)), ((), ())), preferred_element_type=F32)


def dot_t1(a, b):
    return lax.dot_general(a, b, (((1,), (1,)), ((), ())), preferred_element_type=F32)


def split(x):
    high = x.astype(BF)
    return high, (x - high.astype(F32)).astype(BF)


def slots_kernel(parts, cap, take, slot_ref, neg_ref, request_ref):
    part = take(0)[...]
    edges = part.shape[1]
    slots = parts * cap
    named = (iota((parts, edges), 0) == part).astype(F32)
    before = hot(iota((edges, edges), 0) < iota((edges, edges), 1))
    earlier = dot(named.astype(BF), before)
    position = jnp.sum(earlier * named, axis=0, keepdims=True).astype(I32)
    slot = part * cap + position
    slot_ref[...] = slot
    placed = hot(iota((slots, edges), 0) == slot)
    which = iota((8, edges), 0)
    tail = take(1)[...]
    digits = jnp.where(which == 0, tail >> 7, jnp.where(which == 1, tail & 127, 0))
    found = dot_t1(digits.astype(F32).astype(BF), placed).astype(BF)
    neg = as_column(take(2)[...])
    negs = neg.shape[0]
    share = request_ref.shape[1]
    turned = iota((negs, negs), 0) == (iota((negs, negs), 1) ^ (lax.axis_index("rep") * share))
    ordered = jnp.sum(jnp.where(turned, neg, 0), axis=0, keepdims=True)
    neg_ref[...] = ordered
    entities = take(3)
    own = hot_rows(ordered, entities.shape[0])[:share]
    rows = dot(own, entities[...]).astype(BF)
    columns = rows.shape[1]
    for index in range(parts):
        request_ref[index, :, :columns] = rows
        ids = found[:, index * cap : (index + 1) * cap]
        if cap < 128:
            ids = jnp.concatenate([ids, jnp.zeros((share, 128 - cap), BF)], axis=1)
        request_ref[index, :, columns:] = ids


def query_kernel(take, rows_ref, query_ref):
    head, rel = take(0), take(1)
    entities = take(2)
    rows = dot(hot_rows(head[...], entities.shape[0]), entities[...]).astype(BF)
    rows_ref[...] = rows
    rel = as_column(rel[...])
    total = jnp.zeros(rows.shape, F32)
    operators = take(3)
    for relation in range(operators.shape[0]):
        picked = jnp.where(rel == relation, rows, jnp.zeros_like(rows))
        total = total + dot(picked, operators[relation])
    query_ref[...] = total.astype(BF)


def lookup_kernel(cap, request_ref, entities, ids_ref, rows_ref, negs_ref):
    parts, share, width = request_ref.shape
    columns = rows_ref.shape[1]
    pieces = []
    for index in range(parts):
        digits = request_ref[index, :, columns : columns + cap].astype(F32)
        pieces.append(digits[0:1] * 128.0 + digits[1:2])
    ids = jnp.concatenate(pieces, axis=1).astype(I32)
    ids_ref[...] = ids
    rows_ref[...] = dot(hot_rows(ids, entities.shape[0]), entities[...]).astype(BF)
    negs_ref[...] = jnp.concatenate(
        [request_ref[index, :, :columns].astype(F32) for index in range(parts)], axis=0
    ).astype(BF)


def quarter_of(special, index):
    if not special:
        return index // 2, index % 2
    rep, x = lax.axis_index("rep"), lax.axis_index("dom") & 1
    quarter = ((rep & 2) + x) ^ (index % 4)
    core = (rep & 1) ^ (1 if index < 4 else 0)
    return 2 * core + (quarter >> 1), quarter & 1


def operator_terms(special, first, rows_ref, rel, grad, out_ref):
    width = grad.shape[1] // 2
    for place in range(4):
        relation, part = quarter_of(special, first + place)
        at = part * width if isinstance(part, int) else pl.multiple_of(part * width, width)
        picked = jnp.where(rel == relation, grad, jnp.zeros_like(grad))
        term = dot_t0(rows_ref[:, pl.ds(at, width)], picked)
        out_ref[place * width : (place + 1) * width] = term.astype(out_ref.dtype)


def edge_kernel(
    factor,
    slot_ref,
    near_ref,
    core_ref,
    across_ref,
    both_ref,
    got_ref,
    take,
    loss_ref,
    grad_ref,
    back_ref,
):
    edges = slot_ref.shape[1]
    negatives = jnp.concatenate(
        [near_ref[...], core_ref[...], across_ref[...], both_ref[...]], axis=0
    )
    slots = got_ref.shape[0]
    tails = dot(hot(as_column(slot_ref[...]) == iota((edges, slots), 1)), got_ref[...])
    queries = take(0)[...]
    scores = dot_t1(queries, negatives) * factor
    positive = jnp.sum(queries.astype(F32) * tails, axis=1, keepdims=True) * factor
    row_max = jnp.maximum(positive, jnp.max(scores, axis=1, keepdims=True))
    exp_pos = jnp.exp(positive - row_max)
    exp_neg = jnp.exp(scores - row_max)
    total = exp_pos + jnp.sum(exp_neg, axis=1, keepdims=True)
    loss_ref[...] = as_row(jnp.log(total) + row_max - positive)
    pull = exp_pos / total - 1.0
    prob = (exp_neg / total).astype(BF)
    grad = (factor * (pull * tails + dot(prob, negatives))).astype(BF)
    grad_ref[...] = grad
    parts = back_ref.shape[0]
    cap = slots // parts
    weighted = (factor * pull * queries.astype(F32)).astype(BF)
    rows = dot(hot(iota((slots, edges), 0) == slot_ref[...]), weighted).astype(BF)
    negs = factor * dot_t0(prob, queries)
    share = negs.shape[0] // parts // 4
    for index in range(parts):
        back_ref[index, :cap] = rows[index * cap : (index + 1) * cap]
        pieces = [
            negs[(turn * parts + index) * share : (turn * parts + index + 1) * share]
            for turn in range(4)
        ]
        back_ref[index, cap:] = jnp.concatenate(pieces, axis=0).astype(BF)


def terms_kernel(special, first, grad_ref, rows_ref, rel_ref, out_ref):
    operator_terms(special, first, rows_ref, as_column(rel_ref[...]), grad_ref[...], out_ref)


def pair_kernel(keep_ref, got_ref, own_ref, sent_ref):
    half = own_ref.shape[0] // 2
    for place in range(4):
        at = slice(place * half, (place + 1) * half)
        term = keep_ref[at].astype(F32) + got_ref[at].astype(F32)
        if place < 2:
            own_ref[place * half : (place + 1) * half] = term
        else:
            sent_ref[(place - 2) * half : (place - 1) * half] = term.astype(BF)


def middle_kernel(own_ref, got_ref, keep_ref, sent_ref):
    half = keep_ref.shape[0]
    keep_ref[...] = own_ref[:half] + got_ref[:half].astype(F32)
    sent_ref[...] = (own_ref[half:] + got_ref[half:].astype(F32)).astype(BF)


def head_kernel(grad_ref, rel_ref, operators, out_ref):
    rel = as_column(rel_ref[...])
    grad = grad_ref[...]
    edges = grad.shape[0]
    total = jnp.zeros(grad.shape, F32)
    for relation in range(operators.shape[0]):
        picked = jnp.where(rel == relation, grad, jnp.zeros_like(grad))
        total = total + dot_t1(picked, operators[relation])
    out_ref[:edges], out_ref[edges:] = split(total)


def spread_kernel(own_ref, got_ref, *out_refs):
    size = out_refs[0].shape[0]
    for turn, out_ref in enumerate(out_refs):
        rows = pl.ds(pl.multiple_of(((lax.axis_index("dom") >> 1) ^ turn) * size, size), size)
        total = own_ref[rows, :] + got_ref[rows, :].astype(F32)
        out_ref[...] = total.astype(out_ref.dtype)


def sum_kernel(own_ref, first_ref, second_ref, third_ref, out_ref):
    total = own_ref[...] + first_ref[...].astype(F32)
    total = total + (second_ref[...].astype(F32) + third_ref[...].astype(F32))
    out_ref[...] = total.astype(BF)


def stack_kernel(*refs):
    size = refs[0].shape[0]
    for index, ref in enumerate(refs[:-1]):
        refs[-1][index * size : (index + 1) * size] = ref[...]


def half_kernel(which, in_ref, out_ref):
    size = out_ref.shape[0]
    out_ref[...] = in_ref[which * size : (which + 1) * size]


def place_operators(places, sources, out_ref, wide, sems):
    width = out_ref.shape[1] // 2
    size = width // 4
    copies = []
    for slot, ((index, first), source) in enumerate(zip(places, sources)):
        wide[slot, : source.shape[0]] = source[...].astype(F32)
        relation, part = quarter_of(True, (index + 4) % 8)
        for turn in range(source.shape[0] // size):
            at = part * width + ((lax.axis_index("dom") >> 1) ^ (first + turn)) * size
            copy = pltpu.make_async_copy(
                wide.at[slot, pl.ds(turn * size, size)],
                out_ref.at[relation, pl.ds(pl.multiple_of(at, size), size)],
                sems.at[slot, turn],
            )
            copy.start()
            copies.append(copy)
    return copies


def same_kernel(in_ref, out_ref):
    out_ref[...] = in_ref[...]


def operator_kernel(places, *refs):
    sources, (_, out_ref, wide, sems) = refs[:-4], refs[-4:]
    for copy in place_operators(places, sources, out_ref, wide, sems):
        copy.wait()


def add_kernel(halves, away, ids_ref, neg_ref, back_ref, take, *out_refs):
    parts = back_ref.shape[0]
    cap = ids_ref.shape[1] // parts
    tails = jnp.concatenate([back_ref[index, :cap] for index in range(parts)], axis=0)
    negs = back_ref[0, cap:].astype(F32)
    for index in range(1, parts):
        negs = negs + back_ref[index, cap:].astype(F32)
    high, low = split(negs)
    negs = jnp.concatenate([high, low], axis=0)
    head = take(0)[...]
    grads = take(1)
    for out_ref in out_refs:
        count = out_ref.shape[0]
        base = ((lax.axis_index("rep") & 1) ^ away) * count if halves else 0

        def pick(row):
            return hot((iota((count, row.shape[1]), 0) + base) == row)

        total = dot(pick(ids_ref[...]), tails)
        heads = pick(head)
        total = total + dot(jnp.concatenate([heads, heads], axis=1), grads[...])
        own = pick(neg_ref[...])
        total = total + dot(jnp.concatenate([own, own], axis=1), negs)
        out_ref[...] = total.astype(out_ref.dtype)


def both_kernel(kept_ref, arrived_ref, out_ref):
    out_ref[...] = (kept_ref[...] + arrived_ref[...].astype(F32)).astype(BF)


def join_kernel(
    indices, mine_ref, other_ref, over_ref, far_ref, *refs
):
    sources, rest = refs[: len(indices)], refs[len(indices) :]
    out_ref, operators_ref, token_ref, wide, sems, operators_wide, operators_sems = rest
    token_ref[...] = jnp.zeros_like(token_ref)
    half = mine_ref.shape[0]
    core = lax.axis_index("rep") & 1
    copies = []
    for index, (first, second, at) in enumerate(
        ((mine_ref, over_ref, core), (other_ref, far_ref, 1 - core))
    ):
        wide[index] = first[...].astype(F32) + second[...].astype(F32)
        copy = pltpu.make_async_copy(
            wide.at[index],
            out_ref.at[pl.ds(pl.multiple_of(at * half, half), half)],
            sems.at[index],
        )
        copy.start()
        copies.append(copy)
    copies += place_operators(
        indices, sources, operators_ref, operators_wide, operators_sems
    )
    for copy in copies:
        copy.wait()


def flip(x, axis, size, bit):
    return lax.ppermute(x, axis, [(i, i ^ bit) for i in range(size)])


def exchange(x):
    return lax.all_to_all(x, "dom", split_axis=0, concat_axis=0, tiled=True)


def local(special, entities, relations, head_local, rel_ids, tail_part, tail_local, neg_local):
    columns = entities.shape[1]
    factor = 1.0 / math.sqrt(columns)
    ent_dev = entities.shape[0]
    edges = head_local.shape[0]
    parts = lax.axis_size("dom")
    reps = lax.axis_size("rep")
    cap = 2 * edges // parts
    slots = parts * cap
    neg_dev = neg_local.shape[0]
    negs = parts * neg_dev
    share = neg_dev // reps
    count = relations.shape[0]
    head = head_local.reshape(1, edges)
    rel = rel_ids.reshape(1, edges)
    slot, neg_own, request = call(
        functools.partial(slots_kernel, parts, cap),
        [((1, edges), I32), ((1, neg_dev), I32), ((parts, share, columns + 128), BF)],
        (),
        (),
        (
            tail_part.reshape(1, edges),
            tail_local.reshape(1, edges),
            neg_local.reshape(1, neg_dev),
            entities,
        ),
        room=60,
    )
    requests = exchange(request)
    rows, queries = call(
        query_kernel,
        [((edges, columns), BF, True), ((edges, columns), BF, True)],
        (),
        (),
        (head, rel, entities, relations),
        (slot,),
        room=60,
    )
    asked, found, neg_near = call(
        functools.partial(lookup_kernel, cap),
        [((1, slots), I32), ((slots, columns), BF), ((parts * share, columns), BF)],
        (),
        (requests, entities),
        (),
        (rows,),
    )
    got = exchange(found.reshape(parts, cap, columns)).reshape(slots, columns)
    neg_core, neg_across, neg_both = [flip(neg_near, "rep", reps, k) for k in (1, 2, 3)]

    loss, grad, back = call(
        functools.partial(edge_kernel, factor),
        [
            ((1, edges), F32),
            ((edges, columns), BF),
            ((parts, cap + neg_dev, columns), BF),
        ],
        (),
        (slot, neg_near, neg_core, neg_across, neg_both, got),
        (queries,),
    )
    returned = exchange(back)
    kind = BF if special else F32

    def terms(first, after):
        return call(
            functools.partial(terms_kernel, special, first),
            [((2 * columns, columns), kind)],
            (),
            (grad, rows, rel),
            (),
            after,
        )[0]

    away = terms(0, (back,))
    keep = terms(4, (away,))

    def head_terms(after):
        return call(
            head_kernel,
            [((2 * edges, columns), BF)],
            (),
            (grad, rel, relations),
            (),
            after,
            cost=0,
        )[0]

    def add(away, outs, after, cost=0):
        return call(
            functools.partial(add_kernel, special, away),
            outs,
            (),
            (asked, neg_own, returned),
            (head, head_grads),
            after,
            cost=cost,
        )

    if not special:
        whole = jnp.concatenate([away, keep], axis=0)
        whole = whole.reshape(count, columns, columns)
        head_grads = head_terms(())
        (added,) = add(0, [((ent_dev, columns), F32)], ())
        entity_grad = lax.psum(added, "rep")
        return entity_grad, lax.psum(whole, ("dom", "rep")), loss.reshape(edges)

    half, quarter = columns // 2, columns // 8

    def over_y(v):
        return flip(v, "rep", 4, 2)

    def over_x(v):
        return flip(v, "dom", 8, 1)

    def over_core(v):
        return flip(v, "rep", 4, 1)

    own, sent = call(
        pair_kernel,
        [((columns, columns), F32), ((columns, columns), BF)],
        (),
        (keep, over_core(away)),
    )
    own, sent = call(
        middle_kernel,
        [((half, columns), F32), ((half, columns), BF)],
        (),
        (own, over_y(sent)),
        cost=0,
    )
    head_grads = head_terms((sent,))
    own, *sent = call(
        spread_kernel,
        [((quarter, columns), F32)] + [((quarter, columns), BF)] * 3,
        (),
        (own, over_x(sent)),
        (),
        (head_grads,),
        cost=0,
    )
    met = [flip(v, "dom", 8, 2 * (k + 1)) for k, v in enumerate(sent)]
    rows_half = ent_dev // 2
    (leaving,) = add(1, [((rows_half, columns), BF)], (sent[0],))
    (kept,) = add(0, [((rows_half, columns), F32)], (leaving,), 20)
    arrived = over_core(leaving)
    (own,) = call(
        sum_kernel, [((quarter, columns), BF)], (), (own, *met), (), (kept,), cost=100
    )
    stripes = [own] + [flip(own, "dom", 8, 2 * (k + 1)) for k in range(3)]
    (whole,) = call(
        stack_kernel, [((half, columns), BF)], (), stripes, cost=0
    )
    (both,) = call(both_kernel, [((rows_half, columns), BF)], (), (kept, arrived))
    across = over_y(both)

    y_whole = over_y(whole)
    x_whole = over_x(whole)

    def half_of(which, v):
        return call(
            functools.partial(half_kernel, which), [((half // 2, columns), BF)], (), (v,)
        )[0]

    mine = [whole, x_whole, y_whole]
    mine += [over_y(half_of(0, x_whole)), over_x(half_of(1, y_whole))]
    places = [(0, 0), (1, 0), (2, 0), (3, 0), (3, 2)]
    places += [(4 + index, first) for index, first in places]
    early, late = (0, 1, 2, 5, 6, 7), (3, 4, 8, 9)
    limit = pltpu.CompilerParams(vmem_limit_bytes=40 * 1024 * 1024)
    shape = jax.ShapeDtypeStruct((count, columns, columns), F32)
    entity_grad, relation_grad, token = pl.pallas_call(
        functools.partial(join_kernel, [places[k] for k in early]),
        out_shape=[
            jax.ShapeDtypeStruct((ent_dev, columns), F32),
            shape,
            jax.ShapeDtypeStruct((8, 128), F32),
        ],
        in_specs=[VMEM] * (4 + len(early)),
        out_specs=[FAR, FAR, VMEM],
        scratch_shapes=[
            pltpu.VMEM((2, rows_half, columns), F32),
            pltpu.SemaphoreType.DMA((2,)),
            pltpu.VMEM((len(early), half, columns), F32),
            pltpu.SemaphoreType.DMA((len(early), 4)),
        ],
        compiler_params=limit,
    )(both, over_core(both), across, over_core(across), *(mine[:3] + [over_core(v) for v in mine[:3]]))
    last = [
        call(same_kernel, [(v.shape, BF)], (), (v,), (), (token,))[0] for v in mine[3:]
    ]
    relation_grad = pl.pallas_call(
        functools.partial(operator_kernel, [places[k] for k in late]),
        out_shape=shape,
        in_specs=[VMEM] * len(late) + [FAR],
        out_specs=FAR,
        scratch_shapes=[
            pltpu.VMEM((len(late), half, columns), F32),
            pltpu.SemaphoreType.DMA((len(late), 4)),
        ],
        input_output_aliases={len(late): 0},
        compiler_params=limit,
    )(*last, *[over_core(v) for v in last], relation_grad)
    return entity_grad, relation_grad, loss.reshape(edges)


def solution(mesh):
    special = dict(mesh.shape) == {"dom": 8, "rep": 4}
    return jax.shard_map(
        functools.partial(local, special),
        mesh=mesh,
        in_specs=(
            P("dom", None),
            P(),
            P(("dom", "rep")),
            P(("dom", "rep")),
            P(("dom", "rep"), None),
            P(("dom", "rep")),
            P("dom"),
        ),
        out_specs=(P("dom", None), P(), P(("dom", "rep"))),
        check_vma=False,
    )
```

```python
import functools
import math

import jax
import jax.numpy as jnp
from jax import lax
from jax.experimental import pallas as pl
from jax.experimental.pallas import tpu as pltpu
from jax.sharding import PartitionSpec as P

BF = jnp.bfloat16
F32 = jnp.float32
I32 = jnp.int32
VMEM = pl.BlockSpec(memory_space=pltpu.VMEM)
SMEM = pl.BlockSpec(memory_space=pltpu.SMEM)
FAR = pl.BlockSpec(memory_space=pltpu.HBM)


def call(body, outs, scalars, near, far=(), after=(), room=40, cost=0):
    counts = len(scalars), len(near), len(far), len(after), len(outs), len(far)
    away = [index for index, out in enumerate(outs) if len(out) == 3]

    def kernel(*refs):
        refs = list(refs)
        groups = []
        for size in counts:
            groups.append(refs[:size])
            refs = refs[size:]
        scalar_refs, near_refs, far_refs, _, out_refs, held = groups
        copies = [
            pltpu.make_async_copy(source, target, refs[len(away)].at[index])
            for index, (source, target) in enumerate(zip(far_refs, held))
        ]
        for copy in copies:
            copy.start()

        def take(index):
            copies[index].wait()
            return held[index]

        filled = list(out_refs)
        for place, index in enumerate(away):
            filled[index] = refs[place]
        body(*scalar_refs, *near_refs, *([take] if far else []), *filled)
        copies_out = [
            pltpu.make_async_copy(refs[place], out_refs[index], refs[-1].at[place])
            for place, index in enumerate(away)
        ]
        for copy in copies_out:
            copy.start()
        for copy in copies_out:
            copy.wait()

    scratch = [pltpu.VMEM(x.shape, x.dtype) for x in far]
    scratch += [pltpu.VMEM(outs[index][0], outs[index][1]) for index in away]
    if far:
        scratch.append(pltpu.SemaphoreType.DMA((len(far),)))
    if away:
        scratch.append(pltpu.SemaphoreType.DMA((len(away),)))
    return pl.pallas_call(
        kernel,
        out_shape=[jax.ShapeDtypeStruct(out[0], out[1]) for out in outs],
        in_specs=[SMEM] * len(scalars)
        + [VMEM] * len(near)
        + [FAR] * (len(far) + len(after)),
        out_specs=[FAR if len(out) == 3 else VMEM for out in outs],
        scratch_shapes=scratch,
        compiler_params=pltpu.CompilerParams(vmem_limit_bytes=room * 1024 * 1024),
        cost_estimate=estimate(cost),
    )(*scalars, *near, *far, *after)


def estimate(cost):
    return pl.CostEstimate(flops=1 + int(cost * 1e9), bytes_accessed=1, transcendentals=0)


def iota(shape, axis):
    return lax.broadcasted_iota(I32, shape, axis)


def as_column(row):
    size = row.shape[1]
    step = min(128, size)
    eye = iota((step, step), 0) == iota((step, step), 1)
    pieces = [
        jnp.sum(jnp.where(eye, row[:, at : at + step], 0), axis=1, keepdims=True)
        for at in range(0, size, step)
    ]
    return jnp.concatenate(pieces, axis=0)


def as_row(column):
    size = column.shape[0]
    step = min(128, size)
    eye = iota((step, step), 0) == iota((step, step), 1)
    pieces = [
        jnp.sum(jnp.where(eye, column[at : at + step, :], 0.0), axis=0, keepdims=True)
        for at in range(0, size, step)
    ]
    return jnp.concatenate(pieces, axis=1)


def hot(mask):
    return mask.astype(F32).astype(BF)


def hot_rows(row, count):
    return hot(as_column(row) == iota((row.shape[1], count), 1))


def dot(a, b):
    return jnp.dot(a, b, preferred_element_type=F32)


def dot_t0(a, b):
    return lax.dot_general(a, b, (((0,), (0,)), ((), ())), preferred_element_type=F32)


def dot_t1(a, b):
    return lax.dot_general(a, b, (((1,), (1,)), ((), ())), preferred_element_type=F32)


def split(x):
    high = x.astype(BF)
    return high, (x - high.astype(F32)).astype(BF)


def slots_kernel(parts, cap, take, slot_ref, neg_ref, request_ref):
    part = take(0)[...]
    edges = part.shape[1]
    slots = parts * cap
    named = (iota((parts, edges), 0) == part).astype(F32)
    before = hot(iota((edges, edges), 0) < iota((edges, edges), 1))
    earlier = dot(named.astype(BF), before)
    position = jnp.sum(earlier * named, axis=0, keepdims=True).astype(I32)
    slot = part * cap + position
    slot_ref[...] = slot
    placed = hot(iota((slots, edges), 0) == slot)
    which = iota((8, edges), 0)
    tail = take(1)[...]
    digits = jnp.where(which == 0, tail >> 7, jnp.where(which == 1, tail & 127, 0))
    found = dot_t1(digits.astype(F32).astype(BF), placed).astype(BF)
    neg = as_column(take(2)[...])
    negs = neg.shape[0]
    share = request_ref.shape[1]
    turned = iota((negs, negs), 0) == (iota((negs, negs), 1) ^ (lax.axis_index("rep") * share))
    ordered = jnp.sum(jnp.where(turned, neg, 0), axis=0, keepdims=True)
    neg_ref[...] = ordered
    entities = take(3)
    own = hot_rows(ordered, entities.shape[0])[:share]
    rows = dot(own, entities[...]).astype(BF)
    columns = rows.shape[1]
    for index in range(parts):
        request_ref[index, :, :columns] = rows
        ids = found[:, index * cap : (index + 1) * cap]
        if cap < 128:
            ids = jnp.concatenate([ids, jnp.zeros((share, 128 - cap), BF)], axis=1)
        request_ref[index, :, columns:] = ids


def query_kernel(take, rows_ref, query_ref):
    head, rel = take(0), take(1)
    entities = take(2)
    rows = dot(hot_rows(head[...], entities.shape[0]), entities[...]).astype(BF)
    rows_ref[...] = rows
    rel = as_column(rel[...])
    total = jnp.zeros(rows.shape, F32)
    operators = take(3)
    for relation in range(operators.shape[0]):
        picked = jnp.where(rel == relation, rows, jnp.zeros_like(rows))
        total = total + dot(picked, operators[relation])
    query_ref[...] = total.astype(BF)


def lookup_kernel(cap, request_ref, entities, ids_ref, rows_ref, negs_ref):
    parts, share, width = request_ref.shape
    columns = rows_ref.shape[1]
    pieces = []
    for index in range(parts):
        digits = request_ref[index, :, columns : columns + cap].astype(F32)
        pieces.append(digits[0:1] * 128.0 + digits[1:2])
    ids = jnp.concatenate(pieces, axis=1).astype(I32)
    ids_ref[...] = ids
    rows_ref[...] = dot(hot_rows(ids, entities.shape[0]), entities[...]).astype(BF)
    negs_ref[...] = jnp.concatenate(
        [request_ref[index, :, :columns].astype(F32) for index in range(parts)], axis=0
    ).astype(BF)


def quarter_of(special, index):
    if not special:
        return index // 2, index % 2
    rep, x = lax.axis_index("rep"), lax.axis_index("dom") & 1
    quarter = ((rep & 2) + x) ^ (index % 4)
    core = (rep & 1) ^ (1 if index < 4 else 0)
    return 2 * core + (quarter >> 1), quarter & 1


def operator_terms(special, first, rows_ref, rel, grad, out_ref):
    width = grad.shape[1] // 2
    for place in range(4):
        relation, part = quarter_of(special, first + place)
        at = part * width if isinstance(part, int) else pl.multiple_of(part * width, width)
        picked = jnp.where(rel == relation, grad, jnp.zeros_like(grad))
        term = dot_t0(rows_ref[:, pl.ds(at, width)], picked)
        out_ref[place * width : (place + 1) * width] = term.astype(out_ref.dtype)


def edge_kernel(
    factor,
    slot_ref,
    near_ref,
    core_ref,
    across_ref,
    both_ref,
    got_ref,
    take,
    loss_ref,
    grad_ref,
    back_ref,
):
    edges = slot_ref.shape[1]
    negatives = jnp.concatenate(
        [near_ref[...], core_ref[...], across_ref[...], both_ref[...]], axis=0
    )
    slots = got_ref.shape[0]
    tails = dot(hot(as_column(slot_ref[...]) == iota((edges, slots), 1)), got_ref[...])
    queries = take(0)[...]
    scores = dot_t1(queries, negatives) * factor
    positive = jnp.sum(queries.astype(F32) * tails, axis=1, keepdims=True) * factor
    row_max = jnp.maximum(positive, jnp.max(scores, axis=1, keepdims=True))
    exp_pos = jnp.exp(positive - row_max)
    exp_neg = jnp.exp(scores - row_max)
    total = exp_pos + jnp.sum(exp_neg, axis=1, keepdims=True)
    loss_ref[...] = as_row(jnp.log(total) + row_max - positive)
    pull = exp_pos / total - 1.0
    prob = (exp_neg / total).astype(BF)
    grad = (factor * (pull * tails + dot(prob, negatives))).astype(BF)
    grad_ref[...] = grad
    parts = back_ref.shape[0]
    cap = slots // parts
    weighted = (factor * pull * queries.astype(F32)).astype(BF)
    rows = dot(hot(iota((slots, edges), 0) == slot_ref[...]), weighted).astype(BF)
    negs = factor * dot_t0(prob, queries)
    share = negs.shape[0] // parts // 4
    for index in range(parts):
        back_ref[index, :cap] = rows[index * cap : (index + 1) * cap]
        pieces = [
            negs[(turn * parts + index) * share : (turn * parts + index + 1) * share]
            for turn in range(4)
        ]
        back_ref[index, cap:] = jnp.concatenate(pieces, axis=0).astype(BF)


def terms_kernel(special, first, grad_ref, rows_ref, rel_ref, out_ref):
    operator_terms(special, first, rows_ref, as_column(rel_ref[...]), grad_ref[...], out_ref)


def pair_kernel(keep_ref, got_ref, own_ref, sent_ref):
    half = own_ref.shape[0] // 2
    for place in range(4):
        at = slice(place * half, (place + 1) * half)
        term = keep_ref[at].astype(F32) + got_ref[at].astype(F32)
        if place < 2:
            own_ref[place * half : (place + 1) * half] = term
        else:
            sent_ref[(place - 2) * half : (place - 1) * half] = term.astype(BF)


def middle_kernel(own_ref, got_ref, keep_ref, sent_ref):
    half = keep_ref.shape[0]
    keep_ref[...] = own_ref[:half] + got_ref[:half].astype(F32)
    sent_ref[...] = (own_ref[half:] + got_ref[half:].astype(F32)).astype(BF)


def head_kernel(special, grad_ref, rel_ref, operators, head_ref, *out_refs):
    rel = as_column(rel_ref[...])
    grad = grad_ref[...]
    total = jnp.zeros(grad.shape, F32)
    for relation in range(operators.shape[0]):
        picked = jnp.where(rel == relation, grad, jnp.zeros_like(grad))
        total = total + dot_t1(picked, operators[relation])
    high, low = split(total)
    head = head_ref[...]
    for turn, out_ref in enumerate(out_refs):
        count = out_ref.shape[0]
        base = ((lax.axis_index("rep") & 1) ^ 1 ^ turn) * count if special else 0
        heads = hot((iota((count, head.shape[1]), 0) + base) == head)
        out_ref[...] = (dot(heads, high) + dot(heads, low)).astype(BF)


def spread_kernel(own_ref, got_ref, *out_refs):
    size = out_refs[0].shape[0]
    for turn, out_ref in enumerate(out_refs):
        rows = pl.ds(pl.multiple_of(((lax.axis_index("dom") >> 1) ^ turn) * size, size), size)
        total = own_ref[rows, :] + got_ref[rows, :].astype(F32)
        out_ref[...] = total.astype(out_ref.dtype)


def sum_kernel(own_ref, first_ref, second_ref, third_ref, out_ref):
    total = own_ref[...] + first_ref[...].astype(F32)
    total = total + (second_ref[...].astype(F32) + third_ref[...].astype(F32))
    out_ref[...] = total.astype(BF)


def stack_kernel(*refs):
    size = refs[0].shape[0]
    for index, ref in enumerate(refs[:-1]):
        refs[-1][index * size : (index + 1) * size] = ref[...]


def half_kernel(which, in_ref, out_ref):
    size = out_ref.shape[0]
    out_ref[...] = in_ref[which * size : (which + 1) * size]


def place_operators(places, sources, out_ref, wide, sems):
    width = out_ref.shape[1] // 2
    size = width // 4
    copies = []
    for slot, ((index, first), source) in enumerate(zip(places, sources)):
        wide[slot, : source.shape[0]] = source[...].astype(F32)
        relation, part = quarter_of(True, (index + 4) % 8)
        for turn in range(source.shape[0] // size):
            at = part * width + ((lax.axis_index("dom") >> 1) ^ (first + turn)) * size
            copy = pltpu.make_async_copy(
                wide.at[slot, pl.ds(turn * size, size)],
                out_ref.at[relation, pl.ds(pl.multiple_of(at, size), size)],
                sems.at[slot, turn],
            )
            copy.start()
            copies.append(copy)
    return copies


def same_kernel(in_ref, out_ref):
    out_ref[...] = in_ref[...]


def operator_kernel(places, *refs):
    sources, (_, out_ref, wide, sems) = refs[:-4], refs[-4:]
    for copy in place_operators(places, sources, out_ref, wide, sems):
        copy.wait()


def add_kernel(halves, away, ids_ref, neg_ref, back_ref, base_ref, out_ref):
    parts = back_ref.shape[0]
    cap = ids_ref.shape[1] // parts
    tails = jnp.concatenate([back_ref[index, :cap] for index in range(parts)], axis=0)
    negs = back_ref[0, cap:].astype(F32)
    for index in range(1, parts):
        negs = negs + back_ref[index, cap:].astype(F32)
    high, low = split(negs)
    negs = jnp.concatenate([high, low], axis=0)
    count = out_ref.shape[0]
    base = ((lax.axis_index("rep") & 1) ^ away) * count if halves else 0

    def pick(row):
        return hot((iota((count, row.shape[1]), 0) + base) == row)

    own = pick(neg_ref[...])
    total = dot(pick(ids_ref[...]), tails) + dot(jnp.concatenate([own, own], axis=1), negs)
    out_ref[...] = (total + base_ref[...].astype(F32)).astype(out_ref.dtype)


def both_kernel(kept_ref, arrived_ref, out_ref):
    out_ref[...] = (kept_ref[...] + arrived_ref[...].astype(F32)).astype(BF)


def join_kernel(
    indices, mine_ref, other_ref, over_ref, far_ref, *refs
):
    sources, rest = refs[: len(indices)], refs[len(indices) :]
    out_ref, operators_ref, token_ref, wide, sems, operators_wide, operators_sems = rest
    token_ref[...] = jnp.zeros_like(token_ref)
    half = mine_ref.shape[0]
    core = lax.axis_index("rep") & 1
    copies = []
    for index, (first, second, at) in enumerate(
        ((mine_ref, over_ref, core), (other_ref, far_ref, 1 - core))
    ):
        wide[index] = first[...].astype(F32) + second[...].astype(F32)
        copy = pltpu.make_async_copy(
            wide.at[index],
            out_ref.at[pl.ds(pl.multiple_of(at * half, half), half)],
            sems.at[index],
        )
        copy.start()
        copies.append(copy)
    copies += place_operators(
        indices, sources, operators_ref, operators_wide, operators_sems
    )
    for copy in copies:
        copy.wait()


def flip(x, axis, size, bit):
    return lax.ppermute(x, axis, [(i, i ^ bit) for i in range(size)])


def exchange(x):
    return lax.all_to_all(x, "dom", split_axis=0, concat_axis=0, tiled=True)


def local(special, entities, relations, head_local, rel_ids, tail_part, tail_local, neg_local):
    columns = entities.shape[1]
    factor = 1.0 / math.sqrt(columns)
    ent_dev = entities.shape[0]
    edges = head_local.shape[0]
    parts = lax.axis_size("dom")
    reps = lax.axis_size("rep")
    cap = 2 * edges // parts
    slots = parts * cap
    neg_dev = neg_local.shape[0]
    negs = parts * neg_dev
    share = neg_dev // reps
    count = relations.shape[0]
    head = head_local.reshape(1, edges)
    rel = rel_ids.reshape(1, edges)
    slot, neg_own, request = call(
        functools.partial(slots_kernel, parts, cap),
        [((1, edges), I32), ((1, neg_dev), I32), ((parts, share, columns + 128), BF)],
        (),
        (),
        (
            tail_part.reshape(1, edges),
            tail_local.reshape(1, edges),
            neg_local.reshape(1, neg_dev),
            entities,
        ),
        room=60,
    )
    requests = exchange(request)
    rows, queries = call(
        query_kernel,
        [((edges, columns), BF, True), ((edges, columns), BF, True)],
        (),
        (),
        (head, rel, entities, relations),
        (slot,),
        room=60,
    )
    asked, found, neg_near = call(
        functools.partial(lookup_kernel, cap),
        [((1, slots), I32), ((slots, columns), BF), ((parts * share, columns), BF)],
        (),
        (requests, entities),
        (),
        (rows,),
    )
    got = exchange(found.reshape(parts, cap, columns)).reshape(slots, columns)
    neg_core, neg_across, neg_both = [flip(neg_near, "rep", reps, k) for k in (1, 2, 3)]

    loss, grad, back = call(
        functools.partial(edge_kernel, factor),
        [
            ((1, edges), F32),
            ((edges, columns), BF),
            ((parts, cap + neg_dev, columns), BF),
        ],
        (),
        (slot, neg_near, neg_core, neg_across, neg_both, got),
        (queries,),
    )
    returned = exchange(back)
    kind = BF if special else F32

    def terms(first, after):
        return call(
            functools.partial(terms_kernel, special, first),
            [((2 * columns, columns), kind)],
            (),
            (grad, rows, rel),
            (),
            after,
        )[0]

    away = terms(0, (back,))
    keep = terms(4, (away,))

    def head_terms(count, after):
        return call(
            functools.partial(head_kernel, special),
            [((ent_dev // count, columns), BF)] * count,
            (),
            (grad, rel, relations, head),
            (),
            after,
            cost=0,
        )

    def add(away, base, outs, after, cost=0):
        return call(
            functools.partial(add_kernel, special, away),
            outs,
            (),
            (asked, neg_own, returned, base),
            (),
            after,
            cost=cost,
        )

    if not special:
        whole = jnp.concatenate([away, keep], axis=0)
        whole = whole.reshape(count, columns, columns)
        (base,) = head_terms(1, ())
        (added,) = add(0, base, [((ent_dev, columns), F32)], ())
        entity_grad = lax.psum(added, "rep")
        return entity_grad, lax.psum(whole, ("dom", "rep")), loss.reshape(edges)

    half, quarter = columns // 2, columns // 8

    def over_y(v):
        return flip(v, "rep", 4, 2)

    def over_x(v):
        return flip(v, "dom", 8, 1)

    def over_core(v):
        return flip(v, "rep", 4, 1)

    own, sent = call(
        pair_kernel,
        [((columns, columns), F32), ((columns, columns), BF)],
        (),
        (keep, over_core(away)),
    )
    own, sent = call(
        middle_kernel,
        [((half, columns), F32), ((half, columns), BF)],
        (),
        (own, over_y(sent)),
        cost=0,
    )
    base_away, base_kept = head_terms(2, (sent,))
    own, *sent = call(
        spread_kernel,
        [((quarter, columns), F32)] + [((quarter, columns), BF)] * 3,
        (),
        (own, over_x(sent)),
        (),
        (base_kept,),
        cost=0,
    )
    met = [flip(v, "dom", 8, 2 * (k + 1)) for k, v in enumerate(sent)]
    rows_half = ent_dev // 2
    (leaving,) = add(1, base_away, [((rows_half, columns), BF)], (sent[0],))
    (kept,) = add(0, base_kept, [((rows_half, columns), F32)], (leaving,), 20)
    arrived = over_core(leaving)
    (own,) = call(
        sum_kernel, [((quarter, columns), BF)], (), (own, *met), (), (kept,), cost=100
    )
    stripes = [own] + [flip(own, "dom", 8, 2 * (k + 1)) for k in range(3)]
    (whole,) = call(
        stack_kernel, [((half, columns), BF)], (), stripes, cost=0
    )
    (both,) = call(both_kernel, [((rows_half, columns), BF)], (), (kept, arrived))
    across = over_y(both)

    y_whole = over_y(whole)
    x_whole = over_x(whole)

    def half_of(which, v):
        return call(
            functools.partial(half_kernel, which), [((half // 2, columns), BF)], (), (v,)
        )[0]

    mine = [whole, x_whole, y_whole]
    mine += [over_y(half_of(0, x_whole)), over_x(half_of(1, y_whole))]
    places = [(0, 0), (1, 0), (2, 0), (3, 0), (3, 2)]
    places += [(4 + index, first) for index, first in places]
    early, late = (0, 1, 2, 5, 6, 7), (3, 4, 8, 9)
    limit = pltpu.CompilerParams(vmem_limit_bytes=40 * 1024 * 1024)
    shape = jax.ShapeDtypeStruct((count, columns, columns), F32)
    entity_grad, relation_grad, token = pl.pallas_call(
        functools.partial(join_kernel, [places[k] for k in early]),
        out_shape=[
            jax.ShapeDtypeStruct((ent_dev, columns), F32),
            shape,
            jax.ShapeDtypeStruct((8, 128), F32),
        ],
        in_specs=[VMEM] * (4 + len(early)),
        out_specs=[FAR, FAR, VMEM],
        scratch_shapes=[
            pltpu.VMEM((2, rows_half, columns), F32),
            pltpu.SemaphoreType.DMA((2,)),
            pltpu.VMEM((len(early), half, columns), F32),
            pltpu.SemaphoreType.DMA((len(early), 4)),
        ],
        compiler_params=limit,
    )(both, over_core(both), across, over_core(across), *(mine[:3] + [over_core(v) for v in mine[:3]]))
    last = [
        call(same_kernel, [(v.shape, BF)], (), (v,), (), (token,))[0] for v in mine[3:]
    ]
    relation_grad = pl.pallas_call(
        functools.partial(operator_kernel, [places[k] for k in late]),
        out_shape=shape,
        in_specs=[VMEM] * len(late) + [FAR],
        out_specs=FAR,
        scratch_shapes=[
            pltpu.VMEM((len(late), half, columns), F32),
            pltpu.SemaphoreType.DMA((len(late), 4)),
        ],
        input_output_aliases={len(late): 0},
        compiler_params=limit,
    )(*last, *[over_core(v) for v in last], relation_grad)
    return entity_grad, relation_grad, loss.reshape(edges)


def solution(mesh):
    special = dict(mesh.shape) == {"dom": 8, "rep": 4}
    return jax.shard_map(
        functools.partial(local, special),
        mesh=mesh,
        in_specs=(
            P("dom", None),
            P(),
            P(("dom", "rep")),
            P(("dom", "rep")),
            P(("dom", "rep"), None),
            P(("dom", "rep")),
            P("dom"),
        ),
        out_specs=(P("dom", None), P(), P(("dom", "rep"))),
        check_vma=False,
    )
```

```python
import functools
import math

import jax
import jax.numpy as jnp
from jax import lax
from jax.experimental import pallas as pl
from jax.experimental.pallas import tpu as pltpu
from jax.sharding import PartitionSpec as P

BF = jnp.bfloat16
F32 = jnp.float32
I32 = jnp.int32
VMEM = pl.BlockSpec(memory_space=pltpu.VMEM)
SMEM = pl.BlockSpec(memory_space=pltpu.SMEM)
FAR = pl.BlockSpec(memory_space=pltpu.HBM)


def call(body, outs, scalars, near, far=(), after=(), room=40, cost=0):
    counts = len(scalars), len(near), len(far), len(after), len(outs), len(far)
    away = [index for index, out in enumerate(outs) if len(out) == 3]

    def kernel(*refs):
        refs = list(refs)
        groups = []
        for size in counts:
            groups.append(refs[:size])
            refs = refs[size:]
        scalar_refs, near_refs, far_refs, _, out_refs, held = groups
        copies = [
            pltpu.make_async_copy(source, target, refs[len(away)].at[index])
            for index, (source, target) in enumerate(zip(far_refs, held))
        ]
        for copy in copies:
            copy.start()

        def take(index):
            copies[index].wait()
            return held[index]

        filled = list(out_refs)
        for place, index in enumerate(away):
            filled[index] = refs[place]
        body(*scalar_refs, *near_refs, *([take] if far else []), *filled)
        copies_out = [
            pltpu.make_async_copy(refs[place], out_refs[index], refs[-1].at[place])
            for place, index in enumerate(away)
        ]
        for copy in copies_out:
            copy.start()
        for copy in copies_out:
            copy.wait()

    scratch = [pltpu.VMEM(x.shape, x.dtype) for x in far]
    scratch += [pltpu.VMEM(outs[index][0], outs[index][1]) for index in away]
    if far:
        scratch.append(pltpu.SemaphoreType.DMA((len(far),)))
    if away:
        scratch.append(pltpu.SemaphoreType.DMA((len(away),)))
    return pl.pallas_call(
        kernel,
        out_shape=[jax.ShapeDtypeStruct(out[0], out[1]) for out in outs],
        in_specs=[SMEM] * len(scalars)
        + [VMEM] * len(near)
        + [FAR] * (len(far) + len(after)),
        out_specs=[FAR if len(out) == 3 else VMEM for out in outs],
        scratch_shapes=scratch,
        compiler_params=pltpu.CompilerParams(vmem_limit_bytes=room * 1024 * 1024),
        cost_estimate=estimate(cost),
    )(*scalars, *near, *far, *after)


def estimate(cost):
    return pl.CostEstimate(flops=1 + int(cost * 1e9), bytes_accessed=1, transcendentals=0)


def iota(shape, axis):
    return lax.broadcasted_iota(I32, shape, axis)


def as_column(row):
    size = row.shape[1]
    step = min(128, size)
    eye = iota((step, step), 0) == iota((step, step), 1)
    pieces = [
        jnp.sum(jnp.where(eye, row[:, at : at + step], 0), axis=1, keepdims=True)
        for at in range(0, size, step)
    ]
    return jnp.concatenate(pieces, axis=0)


def as_row(column):
    size = column.shape[0]
    step = min(128, size)
    eye = iota((step, step), 0) == iota((step, step), 1)
    pieces = [
        jnp.sum(jnp.where(eye, column[at : at + step, :], 0.0), axis=0, keepdims=True)
        for at in range(0, size, step)
    ]
    return jnp.concatenate(pieces, axis=1)


def hot(mask):
    return mask.astype(F32).astype(BF)


def hot_rows(row, count):
    return hot(as_column(row) == iota((row.shape[1], count), 1))


def dot(a, b):
    return jnp.dot(a, b, preferred_element_type=F32)


def dot_t0(a, b):
    return lax.dot_general(a, b, (((0,), (0,)), ((), ())), preferred_element_type=F32)


def dot_t1(a, b):
    return lax.dot_general(a, b, (((1,), (1,)), ((), ())), preferred_element_type=F32)


def split(x):
    high = x.astype(BF)
    return high, (x - high.astype(F32)).astype(BF)


def slots_kernel(parts, cap, take, slot_ref, neg_ref, request_ref):
    part = take(0)[...]
    edges = part.shape[1]
    slots = parts * cap
    named = (iota((parts, edges), 0) == part).astype(F32)
    before = hot(iota((edges, edges), 0) < iota((edges, edges), 1))
    earlier = dot(named.astype(BF), before)
    position = jnp.sum(earlier * named, axis=0, keepdims=True).astype(I32)
    slot = part * cap + position
    slot_ref[...] = slot
    placed = hot(iota((slots, edges), 0) == slot)
    which = iota((8, edges), 0)
    tail = take(1)[...]
    digits = jnp.where(which == 0, tail >> 7, jnp.where(which == 1, tail & 127, 0))
    found = dot_t1(digits.astype(F32).astype(BF), placed).astype(BF)
    neg = as_column(take(2)[...])
    negs = neg.shape[0]
    share = request_ref.shape[1]
    turned = iota((negs, negs), 0) == (iota((negs, negs), 1) ^ (lax.axis_index("rep") * share))
    ordered = jnp.sum(jnp.where(turned, neg, 0), axis=0, keepdims=True)
    neg_ref[...] = ordered
    entities = take(3)
    own = hot_rows(ordered, entities.shape[0])[:share]
    rows = dot(own, entities[...]).astype(BF)
    columns = rows.shape[1]
    for index in range(parts):
        request_ref[index, :, :columns] = rows
        ids = found[:, index * cap : (index + 1) * cap]
        if cap < 128:
            ids = jnp.concatenate([ids, jnp.zeros((share, 128 - cap), BF)], axis=1)
        request_ref[index, :, columns:] = ids


def query_kernel(take, rows_ref, query_ref):
    head, rel = take(0), take(1)
    entities = take(2)
    rows = dot(hot_rows(head[...], entities.shape[0]), entities[...]).astype(BF)
    rows_ref[...] = rows
    rel = as_column(rel[...])
    total = jnp.zeros(rows.shape, F32)
    operators = take(3)
    for relation in range(operators.shape[0]):
        picked = jnp.where(rel == relation, rows, jnp.zeros_like(rows))
        total = total + dot(picked, operators[relation])
    query_ref[...] = total.astype(BF)


def lookup_kernel(cap, request_ref, entities, ids_ref, rows_ref, negs_ref):
    parts, share, width = request_ref.shape
    columns = rows_ref.shape[1]
    pieces = []
    for index in range(parts):
        digits = request_ref[index, :, columns : columns + cap].astype(F32)
        pieces.append(digits[0:1] * 128.0 + digits[1:2])
    ids = jnp.concatenate(pieces, axis=1).astype(I32)
    ids_ref[...] = ids
    rows_ref[...] = dot(hot_rows(ids, entities.shape[0]), entities[...]).astype(BF)
    negs_ref[...] = jnp.concatenate(
        [request_ref[index, :, :columns].astype(F32) for index in range(parts)], axis=0
    ).astype(BF)


def quarter_of(special, index):
    if not special:
        return index // 2, index % 2
    rep, x = lax.axis_index("rep"), lax.axis_index("dom") & 1
    quarter = ((rep & 2) + x) ^ (index % 4)
    core = (rep & 1) ^ (1 if index < 4 else 0)
    return 2 * core + (quarter >> 1), quarter & 1


def operator_terms(special, first, rows_ref, rel, grad, *out_refs):
    width = grad.shape[1] // 2
    for place in range(4):
        relation, part = quarter_of(special, first + place)
        at = part * width if isinstance(part, int) else pl.multiple_of(part * width, width)
        picked = jnp.where(rel == relation, grad, jnp.zeros_like(grad))
        term = dot_t0(rows_ref[:, pl.ds(at, width)], picked)
        out_ref = out_refs[place // 2]
        out_ref[place % 2 * width : (place % 2 + 1) * width] = term.astype(out_ref.dtype)


def score_kernel(
    factor, near_ref, core_ref, across_ref, both_ref, query_ref, score_ref
):
    negatives = jnp.concatenate(
        [near_ref[...], core_ref[...], across_ref[...], both_ref[...]], axis=0
    )
    score_ref[...] = dot_t1(query_ref[...], negatives) * factor


def edge_kernel(
    factor,
    slot_ref,
    near_ref,
    core_ref,
    across_ref,
    both_ref,
    got_ref,
    score_ref,
    take,
    loss_ref,
    grad_ref,
    back_ref,
):
    edges = slot_ref.shape[1]
    negatives = jnp.concatenate(
        [near_ref[...], core_ref[...], across_ref[...], both_ref[...]], axis=0
    )
    slots = got_ref.shape[0]
    tails = dot(hot(as_column(slot_ref[...]) == iota((edges, slots), 1)), got_ref[...])
    queries = take(0)[...]
    scores = score_ref[...]
    positive = jnp.sum(queries.astype(F32) * tails, axis=1, keepdims=True) * factor
    row_max = jnp.maximum(positive, jnp.max(scores, axis=1, keepdims=True))
    exp_pos = jnp.exp(positive - row_max)
    exp_neg = jnp.exp(scores - row_max)
    total = exp_pos + jnp.sum(exp_neg, axis=1, keepdims=True)
    loss_ref[...] = as_row(jnp.log(total) + row_max - positive)
    pull = exp_pos / total - 1.0
    prob = (exp_neg / total).astype(BF)
    grad = (factor * (pull * tails + dot(prob, negatives))).astype(BF)
    grad_ref[...] = grad
    parts = back_ref.shape[0]
    cap = slots // parts
    weighted = (factor * pull * queries.astype(F32)).astype(BF)
    rows = dot(hot(iota((slots, edges), 0) == slot_ref[...]), weighted).astype(BF)
    negs = factor * dot_t0(prob, queries)
    share = negs.shape[0] // parts // 4
    for index in range(parts):
        back_ref[index, :cap] = rows[index * cap : (index + 1) * cap]
        pieces = [
            negs[(turn * parts + index) * share : (turn * parts + index + 1) * share]
            for turn in range(4)
        ]
        back_ref[index, cap:] = jnp.concatenate(pieces, axis=0).astype(BF)


def terms_kernel(special, first, grad_ref, rows_ref, rel_ref, *out_refs):
    operator_terms(special, first, rows_ref, as_column(rel_ref[...]), grad_ref[...], *out_refs)


def pair_kernel(keep_ref, got_ref, out_ref):
    out_ref[...] = (keep_ref[...].astype(F32) + got_ref[...].astype(F32)).astype(out_ref.dtype)


def middle_kernel(own_ref, got_ref, keep_ref, sent_ref):
    half = keep_ref.shape[0]
    keep_ref[...] = own_ref[:half] + got_ref[:half].astype(F32)
    sent_ref[...] = (own_ref[half:] + got_ref[half:].astype(F32)).astype(BF)


def head_kernel(special, grad_ref, rel_ref, operators, head_ref, *out_refs):
    rel = as_column(rel_ref[...])
    grad = grad_ref[...]
    total = jnp.zeros(grad.shape, F32)
    for relation in range(operators.shape[0]):
        picked = jnp.where(rel == relation, grad, jnp.zeros_like(grad))
        total = total + dot_t1(picked, operators[relation])
    high, low = split(total)
    head = head_ref[...]
    for turn, out_ref in enumerate(out_refs):
        count = out_ref.shape[0]
        base = ((lax.axis_index("rep") & 1) ^ 1 ^ turn) * count if special else 0
        heads = hot((iota((count, head.shape[1]), 0) + base) == head)
        out_ref[...] = (dot(heads, high) + dot(heads, low)).astype(BF)


def spread_kernel(own_ref, got_ref, *out_refs):
    size = out_refs[0].shape[0]
    for turn, out_ref in enumerate(out_refs):
        rows = pl.ds(pl.multiple_of(((lax.axis_index("dom") >> 1) ^ turn) * size, size), size)
        total = own_ref[rows, :] + got_ref[rows, :].astype(F32)
        out_ref[...] = total.astype(out_ref.dtype)


def sum_kernel(own_ref, first_ref, second_ref, third_ref, out_ref):
    total = own_ref[...] + first_ref[...].astype(F32)
    total = total + (second_ref[...].astype(F32) + third_ref[...].astype(F32))
    out_ref[...] = total.astype(BF)


def stack_kernel(*refs):
    size = refs[0].shape[0]
    for index, ref in enumerate(refs[:-1]):
        refs[-1][index * size : (index + 1) * size] = ref[...]


def half_kernel(which, in_ref, out_ref):
    size = out_ref.shape[0]
    out_ref[...] = in_ref[which * size : (which + 1) * size]


def place_operators(places, sources, out_ref, wide, sems):
    width = out_ref.shape[1] // 2
    size = width // 4
    copies = []
    for slot, ((index, first), source) in enumerate(zip(places, sources)):
        wide[slot, : source.shape[0]] = source[...].astype(F32)
        relation, part = quarter_of(True, (index + 4) % 8)
        for turn in range(source.shape[0] // size):
            at = part * width + ((lax.axis_index("dom") >> 1) ^ (first + turn)) * size
            copy = pltpu.make_async_copy(
                wide.at[slot, pl.ds(turn * size, size)],
                out_ref.at[relation, pl.ds(pl.multiple_of(at, size), size)],
                sems.at[slot, turn],
            )
            copy.start()
            copies.append(copy)
    return copies


def same_kernel(in_ref, out_ref):
    out_ref[...] = in_ref[...]


def operator_kernel(places, *refs):
    sources, (_, out_ref, wide, sems) = refs[:-4], refs[-4:]
    for copy in place_operators(places, sources, out_ref, wide, sems):
        copy.wait()


def add_kernel(halves, away, ids_ref, neg_ref, back_ref, base_ref, out_ref):
    parts = back_ref.shape[0]
    cap = ids_ref.shape[1] // parts
    tails = jnp.concatenate([back_ref[index, :cap] for index in range(parts)], axis=0)
    negs = back_ref[0, cap:].astype(F32)
    for index in range(1, parts):
        negs = negs + back_ref[index, cap:].astype(F32)
    high, low = split(negs)
    negs = jnp.concatenate([high, low], axis=0)
    count = out_ref.shape[0]
    base = ((lax.axis_index("rep") & 1) ^ away) * count if halves else 0

    def pick(row):
        return hot((iota((count, row.shape[1]), 0) + base) == row)

    own = pick(neg_ref[...])
    total = dot(pick(ids_ref[...]), tails) + dot(jnp.concatenate([own, own], axis=1), negs)
    out_ref[...] = (total + base_ref[...].astype(F32)).astype(out_ref.dtype)


def both_kernel(kept_ref, arrived_ref, out_ref):
    out_ref[...] = (kept_ref[...] + arrived_ref[...].astype(F32)).astype(BF)


def join_kernel(
    indices, mine_ref, other_ref, over_ref, far_ref, *refs
):
    sources, rest = refs[: len(indices)], refs[len(indices) :]
    out_ref, operators_ref, token_ref, wide, sems, operators_wide, operators_sems = rest
    token_ref[...] = jnp.zeros_like(token_ref)
    half = mine_ref.shape[0]
    core = lax.axis_index("rep") & 1
    copies = []
    for index, (first, second, at) in enumerate(
        ((mine_ref, over_ref, core), (other_ref, far_ref, 1 - core))
    ):
        wide[index] = first[...].astype(F32) + second[...].astype(F32)
        copy = pltpu.make_async_copy(
            wide.at[index],
            out_ref.at[pl.ds(pl.multiple_of(at * half, half), half)],
            sems.at[index],
        )
        copy.start()
        copies.append(copy)
    copies += place_operators(
        indices, sources, operators_ref, operators_wide, operators_sems
    )
    for copy in copies:
        copy.wait()


def flip(x, axis, size, bit):
    return lax.ppermute(x, axis, [(i, i ^ bit) for i in range(size)])


def exchange(x):
    return lax.all_to_all(x, "dom", split_axis=0, concat_axis=0, tiled=True)


def local(special, entities, relations, head_local, rel_ids, tail_part, tail_local, neg_local):
    columns = entities.shape[1]
    factor = 1.0 / math.sqrt(columns)
    ent_dev = entities.shape[0]
    edges = head_local.shape[0]
    parts = lax.axis_size("dom")
    reps = lax.axis_size("rep")
    cap = 2 * edges // parts
    slots = parts * cap
    neg_dev = neg_local.shape[0]
    negs = parts * neg_dev
    share = neg_dev // reps
    count = relations.shape[0]
    head = head_local.reshape(1, edges)
    rel = rel_ids.reshape(1, edges)
    slot, neg_own, request = call(
        functools.partial(slots_kernel, parts, cap),
        [((1, edges), I32), ((1, neg_dev), I32), ((parts, share, columns + 128), BF)],
        (),
        (),
        (
            tail_part.reshape(1, edges),
            tail_local.reshape(1, edges),
            neg_local.reshape(1, neg_dev),
            entities,
        ),
        room=60,
    )
    requests = exchange(request)
    rows, queries = call(
        query_kernel,
        [((edges, columns), BF, True), ((edges, columns), BF, True)],
        (),
        (),
        (head, rel, entities, relations),
        (slot,),
        room=60,
    )
    asked, found, neg_near = call(
        functools.partial(lookup_kernel, cap),
        [((1, slots), I32), ((slots, columns), BF), ((parts * share, columns), BF)],
        (),
        (requests, entities),
        (),
        (rows,),
    )
    got = exchange(found.reshape(parts, cap, columns)).reshape(slots, columns)
    neg_core, neg_across, neg_both = [flip(neg_near, "rep", reps, k) for k in (1, 2, 3)]

    (scores,) = call(
        functools.partial(score_kernel, factor),
        [((edges, negs), F32)],
        (),
        (neg_near, neg_core, neg_across, neg_both, queries),
    )
    loss, grad, back = call(
        functools.partial(edge_kernel, factor),
        [
            ((1, edges), F32),
            ((edges, columns), BF),
            ((parts, cap + neg_dev, columns), BF),
        ],
        (),
        (slot, neg_near, neg_core, neg_across, neg_both, got, scores),
        (queries,),
    )
    returned = exchange(back)
    kind = BF if special else F32

    def terms(first, after):
        return call(
            functools.partial(terms_kernel, special, first),
            [((columns, columns), kind)] * 2,
            (),
            (grad, rows, rel),
            (),
            after,
        )

    away = terms(0, (back,))
    keep = terms(4, (away[0],))

    def head_terms(count, after):
        return call(
            functools.partial(head_kernel, special),
            [((ent_dev // count, columns), BF)] * count,
            (),
            (grad, rel, relations, head),
            (),
            after,
            cost=0,
        )

    def add(away, base, outs, after, cost=0):
        return call(
            functools.partial(add_kernel, special, away),
            outs,
            (),
            (asked, neg_own, returned, base),
            (),
            after,
            cost=cost,
        )

    if not special:
        whole = jnp.concatenate([*away, *keep], axis=0)
        whole = whole.reshape(count, columns, columns)
        (base,) = head_terms(1, ())
        (added,) = add(0, base, [((ent_dev, columns), F32)], ())
        entity_grad = lax.psum(added, "rep")
        return entity_grad, lax.psum(whole, ("dom", "rep")), loss.reshape(edges)

    half, quarter = columns // 2, columns // 8

    def over_y(v):
        return flip(v, "rep", 4, 2)

    def over_x(v):
        return flip(v, "dom", 8, 1)

    def over_core(v):
        return flip(v, "rep", 4, 1)

    shape = (columns, columns)
    (sent,) = call(pair_kernel, [(shape, BF)], (), (keep[1], over_core(away[1])))
    (own,) = call(pair_kernel, [(shape, F32)], (), (keep[0], over_core(away[0])), (), (sent,))
    own, sent = call(
        middle_kernel,
        [((half, columns), F32), ((half, columns), BF)],
        (),
        (own, over_y(sent)),
        cost=0,
    )
    base_away, base_kept = head_terms(2, (sent,))
    own, *sent = call(
        spread_kernel,
        [((quarter, columns), F32)] + [((quarter, columns), BF)] * 3,
        (),
        (own, over_x(sent)),
        (),
        (base_kept,),
        cost=0,
    )
    met = [flip(v, "dom", 8, 2 * (k + 1)) for k, v in enumerate(sent)]
    rows_half = ent_dev // 2
    (leaving,) = add(1, base_away, [((rows_half, columns), BF)], (sent[0],))
    (kept,) = add(0, base_kept, [((rows_half, columns), F32)], (leaving,), 20)
    arrived = over_core(leaving)
    (own,) = call(
        sum_kernel, [((quarter, columns), BF)], (), (own, *met), (), (kept,), cost=100
    )
    stripes = [own] + [flip(own, "dom", 8, 2 * (k + 1)) for k in range(3)]
    (whole,) = call(
        stack_kernel, [((half, columns), BF)], (), stripes, cost=0
    )
    (both,) = call(both_kernel, [((rows_half, columns), BF)], (), (kept, arrived))
    across = over_y(both)

    y_whole = over_y(whole)
    x_whole = over_x(whole)

    def half_of(which, v):
        return call(
            functools.partial(half_kernel, which), [((half // 2, columns), BF)], (), (v,)
        )[0]

    mine = [whole, x_whole, y_whole]
    mine += [over_y(half_of(0, x_whole)), over_x(half_of(1, y_whole))]
    places = [(0, 0), (1, 0), (2, 0), (3, 0), (3, 2)]
    places += [(4 + index, first) for index, first in places]
    early, late = (0, 1, 2, 5, 6, 7), (3, 4, 8, 9)
    limit = pltpu.CompilerParams(vmem_limit_bytes=40 * 1024 * 1024)
    shape = jax.ShapeDtypeStruct((count, columns, columns), F32)
    entity_grad, relation_grad, token = pl.pallas_call(
        functools.partial(join_kernel, [places[k] for k in early]),
        out_shape=[
            jax.ShapeDtypeStruct((ent_dev, columns), F32),
            shape,
            jax.ShapeDtypeStruct((8, 128), F32),
        ],
        in_specs=[VMEM] * (4 + len(early)),
        out_specs=[FAR, FAR, VMEM],
        scratch_shapes=[
            pltpu.VMEM((2, rows_half, columns), F32),
            pltpu.SemaphoreType.DMA((2,)),
            pltpu.VMEM((len(early), half, columns), F32),
            pltpu.SemaphoreType.DMA((len(early), 4)),
        ],
        compiler_params=limit,
    )(both, over_core(both), across, over_core(across), *(mine[:3] + [over_core(v) for v in mine[:3]]))
    last = [
        call(same_kernel, [(v.shape, BF)], (), (v,), (), (token,))[0] for v in mine[3:]
    ]
    relation_grad = pl.pallas_call(
        functools.partial(operator_kernel, [places[k] for k in late]),
        out_shape=shape,
        in_specs=[VMEM] * len(late) + [FAR],
        out_specs=FAR,
        scratch_shapes=[
            pltpu.VMEM((len(late), half, columns), F32),
            pltpu.SemaphoreType.DMA((len(late), 4)),
        ],
        input_output_aliases={len(late): 0},
        compiler_params=limit,
    )(*last, *[over_core(v) for v in last], relation_grad)
    return entity_grad, relation_grad, loss.reshape(edges)


def solution(mesh):
    special = dict(mesh.shape) == {"dom": 8, "rep": 4}
    return jax.shard_map(
        functools.partial(local, special),
        mesh=mesh,
        in_specs=(
            P("dom", None),
            P(),
            P(("dom", "rep")),
            P(("dom", "rep")),
            P(("dom", "rep"), None),
            P(("dom", "rep")),
            P("dom"),
        ),
        out_specs=(P("dom", None), P(), P(("dom", "rep"))),
        check_vma=False,
    )
```

```python
import functools
import math

import jax
import jax.numpy as jnp
from jax import lax
from jax.experimental import pallas as pl
from jax.experimental.pallas import tpu as pltpu
from jax.sharding import PartitionSpec as P

BF = jnp.bfloat16
F32 = jnp.float32
I32 = jnp.int32
VMEM = pl.BlockSpec(memory_space=pltpu.VMEM)
SMEM = pl.BlockSpec(memory_space=pltpu.SMEM)
FAR = pl.BlockSpec(memory_space=pltpu.HBM)


def call(body, outs, scalars, near, far=(), after=(), room=40, cost=0):
    counts = len(scalars), len(near), len(far), len(after), len(outs), len(far)
    away = [index for index, out in enumerate(outs) if len(out) == 3]

    def kernel(*refs):
        refs = list(refs)
        groups = []
        for size in counts:
            groups.append(refs[:size])
            refs = refs[size:]
        scalar_refs, near_refs, far_refs, _, out_refs, held = groups
        copies = [
            pltpu.make_async_copy(source, target, refs[len(away)].at[index])
            for index, (source, target) in enumerate(zip(far_refs, held))
        ]
        for copy in copies:
            copy.start()

        def take(index):
            copies[index].wait()
            return held[index]

        filled = list(out_refs)
        for place, index in enumerate(away):
            filled[index] = refs[place]
        body(*scalar_refs, *near_refs, *([take] if far else []), *filled)
        copies_out = [
            pltpu.make_async_copy(refs[place], out_refs[index], refs[-1].at[place])
            for place, index in enumerate(away)
        ]
        for copy in copies_out:
            copy.start()
        for copy in copies_out:
            copy.wait()

    scratch = [pltpu.VMEM(x.shape, x.dtype) for x in far]
    scratch += [pltpu.VMEM(outs[index][0], outs[index][1]) for index in away]
    if far:
        scratch.append(pltpu.SemaphoreType.DMA((len(far),)))
    if away:
        scratch.append(pltpu.SemaphoreType.DMA((len(away),)))
    return pl.pallas_call(
        kernel,
        out_shape=[jax.ShapeDtypeStruct(out[0], out[1]) for out in outs],
        in_specs=[SMEM] * len(scalars)
        + [VMEM] * len(near)
        + [FAR] * (len(far) + len(after)),
        out_specs=[FAR if len(out) == 3 else VMEM for out in outs],
        scratch_shapes=scratch,
        compiler_params=pltpu.CompilerParams(vmem_limit_bytes=room * 1024 * 1024),
        cost_estimate=estimate(cost),
    )(*scalars, *near, *far, *after)


def estimate(cost):
    return pl.CostEstimate(flops=1 + int(cost * 1e9), bytes_accessed=1, transcendentals=0)


def iota(shape, axis):
    return lax.broadcasted_iota(I32, shape, axis)


def as_column(row):
    size = row.shape[1]
    step = min(128, size)
    eye = iota((step, step), 0) == iota((step, step), 1)
    pieces = [
        jnp.sum(jnp.where(eye, row[:, at : at + step], 0), axis=1, keepdims=True)
        for at in range(0, size, step)
    ]
    return jnp.concatenate(pieces, axis=0)


def as_row(column):
    size = column.shape[0]
    step = min(128, size)
    eye = iota((step, step), 0) == iota((step, step), 1)
    pieces = [
        jnp.sum(jnp.where(eye, column[at : at + step, :], 0.0), axis=0, keepdims=True)
        for at in range(0, size, step)
    ]
    return jnp.concatenate(pieces, axis=1)


def hot(mask):
    return mask.astype(F32).astype(BF)


def hot_rows(row, count):
    return hot(as_column(row) == iota((row.shape[1], count), 1))


def dot(a, b):
    return jnp.dot(a, b, preferred_element_type=F32)


def dot_t0(a, b):
    return lax.dot_general(a, b, (((0,), (0,)), ((), ())), preferred_element_type=F32)


def dot_t1(a, b):
    return lax.dot_general(a, b, (((1,), (1,)), ((), ())), preferred_element_type=F32)


def split(x):
    high = x.astype(BF)
    return high, (x - high.astype(F32)).astype(BF)


def slots_kernel(parts, cap, take, slot_ref, neg_ref, request_ref):
    part = take(0)[...]
    edges = part.shape[1]
    slots = parts * cap
    named = (iota((parts, edges), 0) == part).astype(F32)
    before = hot(iota((edges, edges), 0) < iota((edges, edges), 1))
    earlier = dot(named.astype(BF), before)
    position = jnp.sum(earlier * named, axis=0, keepdims=True).astype(I32)
    slot = part * cap + position
    slot_ref[...] = slot
    placed = hot(iota((slots, edges), 0) == slot)
    which = iota((8, edges), 0)
    tail = take(1)[...]
    digits = jnp.where(which == 0, tail >> 7, jnp.where(which == 1, tail & 127, 0))
    found = dot_t1(digits.astype(F32).astype(BF), placed).astype(BF)
    neg = as_column(take(2)[...])
    negs = neg.shape[0]
    share = request_ref.shape[1]
    turned = iota((negs, negs), 0) == (iota((negs, negs), 1) ^ (lax.axis_index("rep") * share))
    ordered = jnp.sum(jnp.where(turned, neg, 0), axis=0, keepdims=True)
    neg_ref[...] = ordered
    entities = take(3)
    own = hot_rows(ordered, entities.shape[0])[:share]
    rows = dot(own, entities[...]).astype(BF)
    columns = rows.shape[1]
    for index in range(parts):
        request_ref[index, :, :columns] = rows
        ids = found[:, index * cap : (index + 1) * cap]
        if cap < 128:
            ids = jnp.concatenate([ids, jnp.zeros((share, 128 - cap), BF)], axis=1)
        request_ref[index, :, columns:] = ids


def query_kernel(take, rows_ref, query_ref):
    head, rel = take(0), take(1)
    entities = take(2)
    rows = dot(hot_rows(head[...], entities.shape[0]), entities[...]).astype(BF)
    rows_ref[...] = rows
    rel = as_column(rel[...])
    total = jnp.zeros(rows.shape, F32)
    operators = take(3)
    for relation in range(operators.shape[0]):
        picked = jnp.where(rel == relation, rows, jnp.zeros_like(rows))
        total = total + dot(picked, operators[relation])
    query_ref[...] = total.astype(BF)


def lookup_kernel(cap, request_ref, entities, ids_ref, rows_ref):
    parts, share, width = request_ref.shape
    columns = rows_ref.shape[1]
    pieces = []
    for index in range(parts):
        digits = request_ref[index, :, columns : columns + cap].astype(F32)
        pieces.append(digits[0:1] * 128.0 + digits[1:2])
    ids = jnp.concatenate(pieces, axis=1).astype(I32)
    ids_ref[...] = ids
    rows_ref[...] = dot(hot_rows(ids, entities.shape[0]), entities[...]).astype(BF)


def negatives_kernel(request_ref, negs_ref):
    parts, columns = request_ref.shape[0], negs_ref.shape[1]
    negs_ref[...] = jnp.concatenate(
        [request_ref[index, :, :columns].astype(F32) for index in range(parts)], axis=0
    ).astype(BF)


def quarter_of(special, index):
    if not special:
        return index // 2, index % 2
    rep, x = lax.axis_index("rep"), lax.axis_index("dom") & 1
    quarter = ((rep & 2) + x) ^ (index % 4)
    core = (rep & 1) ^ (1 if index < 4 else 0)
    return 2 * core + (quarter >> 1), quarter & 1


def operator_terms(special, first, rows_ref, rel, grad, *out_refs):
    width = grad.shape[1] // 2
    for place in range(4):
        relation, part = quarter_of(special, first + place)
        at = part * width if isinstance(part, int) else pl.multiple_of(part * width, width)
        picked = jnp.where(rel == relation, grad, jnp.zeros_like(grad))
        term = dot_t0(rows_ref[:, pl.ds(at, width)], picked)
        out_ref = out_refs[place // 2]
        out_ref[place % 2 * width : (place % 2 + 1) * width] = term.astype(out_ref.dtype)


def score_kernel(
    factor, near_ref, core_ref, across_ref, both_ref, query_ref, score_ref
):
    negatives = jnp.concatenate(
        [near_ref[...], core_ref[...], across_ref[...], both_ref[...]], axis=0
    )
    score_ref[...] = dot_t1(query_ref[...], negatives) * factor


def edge_kernel(
    factor,
    slot_ref,
    near_ref,
    core_ref,
    across_ref,
    both_ref,
    got_ref,
    score_ref,
    take,
    loss_ref,
    grad_ref,
    back_ref,
):
    edges = slot_ref.shape[1]
    negatives = jnp.concatenate(
        [near_ref[...], core_ref[...], across_ref[...], both_ref[...]], axis=0
    )
    slots = got_ref.shape[0]
    tails = dot(hot(as_column(slot_ref[...]) == iota((edges, slots), 1)), got_ref[...])
    queries = take(0)[...]
    scores = score_ref[...]
    positive = jnp.sum(queries.astype(F32) * tails, axis=1, keepdims=True) * factor
    row_max = jnp.maximum(positive, jnp.max(scores, axis=1, keepdims=True))
    exp_pos = jnp.exp(positive - row_max)
    exp_neg = jnp.exp(scores - row_max)
    total = exp_pos + jnp.sum(exp_neg, axis=1, keepdims=True)
    loss_ref[...] = as_row(jnp.log(total) + row_max - positive)
    pull = exp_pos / total - 1.0
    prob = (exp_neg / total).astype(BF)
    grad = (factor * (pull * tails + dot(prob, negatives))).astype(BF)
    grad_ref[...] = grad
    parts = back_ref.shape[0]
    cap = slots // parts
    weighted = (factor * pull * queries.astype(F32)).astype(BF)
    rows = dot(hot(iota((slots, edges), 0) == slot_ref[...]), weighted).astype(BF)
    negs = factor * dot_t0(prob, queries)
    share = negs.shape[0] // parts // 4
    for index in range(parts):
        back_ref[index, :cap] = rows[index * cap : (index + 1) * cap]
        pieces = [
            negs[(turn * parts + index) * share : (turn * parts + index + 1) * share]
            for turn in range(4)
        ]
        back_ref[index, cap:] = jnp.concatenate(pieces, axis=0).astype(BF)


def terms_kernel(special, first, grad_ref, rows_ref, rel_ref, *out_refs):
    operator_terms(special, first, rows_ref, as_column(rel_ref[...]), grad_ref[...], *out_refs)


def pair_kernel(keep_ref, got_ref, out_ref):
    out_ref[...] = (keep_ref[...].astype(F32) + got_ref[...].astype(F32)).astype(out_ref.dtype)


def middle_kernel(own_ref, got_ref, keep_ref, sent_ref):
    half = keep_ref.shape[0]
    keep_ref[...] = own_ref[:half] + got_ref[:half].astype(F32)
    sent_ref[...] = (own_ref[half:] + got_ref[half:].astype(F32)).astype(BF)


def head_kernel(special, grad_ref, rel_ref, operators, head_ref, *out_refs):
    rel = as_column(rel_ref[...])
    grad = grad_ref[...]
    total = jnp.zeros(grad.shape, F32)
    for relation in range(operators.shape[0]):
        picked = jnp.where(rel == relation, grad, jnp.zeros_like(grad))
        total = total + dot_t1(picked, operators[relation])
    high, low = split(total)
    head = head_ref[...]
    for turn, out_ref in enumerate(out_refs):
        count = out_ref.shape[0]
        base = ((lax.axis_index("rep") & 1) ^ 1 ^ turn) * count if special else 0
        heads = hot((iota((count, head.shape[1]), 0) + base) == head)
        out_ref[...] = (dot(heads, high) + dot(heads, low)).astype(BF)


def spread_kernel(own_ref, got_ref, *out_refs):
    size = out_refs[0].shape[0]
    for turn, out_ref in enumerate(out_refs):
        rows = pl.ds(pl.multiple_of(((lax.axis_index("dom") >> 1) ^ turn) * size, size), size)
        total = own_ref[rows, :] + got_ref[rows, :].astype(F32)
        out_ref[...] = total.astype(out_ref.dtype)


def sum_kernel(own_ref, first_ref, second_ref, third_ref, out_ref):
    total = own_ref[...] + first_ref[...].astype(F32)
    total = total + (second_ref[...].astype(F32) + third_ref[...].astype(F32))
    out_ref[...] = total.astype(BF)


def stack_kernel(*refs):
    size = refs[0].shape[0]
    for index, ref in enumerate(refs[:-1]):
        refs[-1][index * size : (index + 1) * size] = ref[...]


def half_kernel(which, in_ref, out_ref):
    size = out_ref.shape[0]
    out_ref[...] = in_ref[which * size : (which + 1) * size]


def place_operators(places, sources, out_ref, wide, sems):
    width = out_ref.shape[1] // 2
    size = width // 4
    copies = []
    for slot, ((index, first), source) in enumerate(zip(places, sources)):
        wide[slot, : source.shape[0]] = source[...].astype(F32)
        relation, part = quarter_of(True, (index + 4) % 8)
        for turn in range(source.shape[0] // size):
            at = part * width + ((lax.axis_index("dom") >> 1) ^ (first + turn)) * size
            copy = pltpu.make_async_copy(
                wide.at[slot, pl.ds(turn * size, size)],
                out_ref.at[relation, pl.ds(pl.multiple_of(at, size), size)],
                sems.at[slot, turn],
            )
            copy.start()
            copies.append(copy)
    return copies


def same_kernel(in_ref, out_ref):
    out_ref[...] = in_ref[...]


def operator_kernel(places, *refs):
    sources, (_, out_ref, wide, sems) = refs[:-4], refs[-4:]
    for copy in place_operators(places, sources, out_ref, wide, sems):
        copy.wait()


def add_kernel(halves, away, ids_ref, neg_ref, back_ref, base_ref, out_ref):
    parts = back_ref.shape[0]
    cap = ids_ref.shape[1] // parts
    tails = jnp.concatenate([back_ref[index, :cap] for index in range(parts)], axis=0)
    negs = back_ref[0, cap:].astype(F32)
    for index in range(1, parts):
        negs = negs + back_ref[index, cap:].astype(F32)
    high, low = split(negs)
    negs = jnp.concatenate([high, low], axis=0)
    count = out_ref.shape[0]
    base = ((lax.axis_index("rep") & 1) ^ away) * count if halves else 0

    def pick(row):
        return hot((iota((count, row.shape[1]), 0) + base) == row)

    own = pick(neg_ref[...])
    total = dot(pick(ids_ref[...]), tails) + dot(jnp.concatenate([own, own], axis=1), negs)
    out_ref[...] = (total + base_ref[...].astype(F32)).astype(out_ref.dtype)


def both_kernel(kept_ref, arrived_ref, out_ref):
    out_ref[...] = (kept_ref[...] + arrived_ref[...].astype(F32)).astype(BF)


def join_kernel(
    indices, mine_ref, other_ref, over_ref, far_ref, *refs
):
    sources, rest = refs[: len(indices)], refs[len(indices) :]
    out_ref, operators_ref, token_ref, wide, sems, operators_wide, operators_sems = rest
    token_ref[...] = jnp.zeros_like(token_ref)
    half = mine_ref.shape[0]
    core = lax.axis_index("rep") & 1
    copies = []
    for index, (first, second, at) in enumerate(
        ((mine_ref, over_ref, core), (other_ref, far_ref, 1 - core))
    ):
        wide[index] = first[...].astype(F32) + second[...].astype(F32)
        copy = pltpu.make_async_copy(
            wide.at[index],
            out_ref.at[pl.ds(pl.multiple_of(at * half, half), half)],
            sems.at[index],
        )
        copy.start()
        copies.append(copy)
    copies += place_operators(
        indices, sources, operators_ref, operators_wide, operators_sems
    )
    for copy in copies:
        copy.wait()


def flip(x, axis, size, bit):
    return lax.ppermute(x, axis, [(i, i ^ bit) for i in range(size)])


def exchange(x):
    return lax.all_to_all(x, "dom", split_axis=0, concat_axis=0, tiled=True)


def local(special, entities, relations, head_local, rel_ids, tail_part, tail_local, neg_local):
    columns = entities.shape[1]
    factor = 1.0 / math.sqrt(columns)
    ent_dev = entities.shape[0]
    edges = head_local.shape[0]
    parts = lax.axis_size("dom")
    reps = lax.axis_size("rep")
    cap = 2 * edges // parts
    slots = parts * cap
    neg_dev = neg_local.shape[0]
    negs = parts * neg_dev
    share = neg_dev // reps
    count = relations.shape[0]
    head = head_local.reshape(1, edges)
    rel = rel_ids.reshape(1, edges)
    slot, neg_own, request = call(
        functools.partial(slots_kernel, parts, cap),
        [((1, edges), I32), ((1, neg_dev), I32), ((parts, share, columns + 128), BF)],
        (),
        (),
        (
            tail_part.reshape(1, edges),
            tail_local.reshape(1, edges),
            neg_local.reshape(1, neg_dev),
            entities,
        ),
        room=60,
    )
    requests = exchange(request)
    rows, queries = call(
        query_kernel,
        [((edges, columns), BF, True), ((edges, columns), BF, True)],
        (),
        (),
        (head, rel, entities, relations),
        (slot,),
        room=60,
    )
    asked, found = call(
        functools.partial(lookup_kernel, cap),
        [((1, slots), I32), ((slots, columns), BF)],
        (),
        (requests, entities),
        (),
        (rows,),
    )
    (neg_near,) = call(
        negatives_kernel, [((parts * share, columns), BF)], (), (requests,), (), (found,)
    )
    got = exchange(found.reshape(parts, cap, columns)).reshape(slots, columns)
    neg_core, neg_across, neg_both = [flip(neg_near, "rep", reps, k) for k in (1, 2, 3)]

    (scores,) = call(
        functools.partial(score_kernel, factor),
        [((edges, negs), F32)],
        (),
        (neg_near, neg_core, neg_across, neg_both, queries),
    )
    loss, grad, back = call(
        functools.partial(edge_kernel, factor),
        [
            ((1, edges), F32),
            ((edges, columns), BF),
            ((parts, cap + neg_dev, columns), BF),
        ],
        (),
        (slot, neg_near, neg_core, neg_across, neg_both, got, scores),
        (queries,),
    )
    returned = exchange(back)
    kind = BF if special else F32

    def terms(first, after):
        return call(
            functools.partial(terms_kernel, special, first),
            [((columns, columns), kind)] * 2,
            (),
            (grad, rows, rel),
            (),
            after,
        )

    away = terms(0, (back,))
    keep = terms(4, (away[0],))

    def head_terms(count, after):
        return call(
            functools.partial(head_kernel, special),
            [((ent_dev // count, columns), BF)] * count,
            (),
            (grad, rel, relations, head),
            (),
            after,
            cost=0,
        )

    def add(away, base, outs, after, cost=0):
        return call(
            functools.partial(add_kernel, special, away),
            outs,
            (),
            (asked, neg_own, returned, base),
            (),
            after,
            cost=cost,
        )

    if not special:
        whole = jnp.concatenate([*away, *keep], axis=0)
        whole = whole.reshape(count, columns, columns)
        (base,) = head_terms(1, ())
        (added,) = add(0, base, [((ent_dev, columns), F32)], ())
        entity_grad = lax.psum(added, "rep")
        return entity_grad, lax.psum(whole, ("dom", "rep")), loss.reshape(edges)

    half, quarter = columns // 2, columns // 8

    def over_y(v):
        return flip(v, "rep", 4, 2)

    def over_x(v):
        return flip(v, "dom", 8, 1)

    def over_core(v):
        return flip(v, "rep", 4, 1)

    shape = (columns, columns)
    (sent,) = call(pair_kernel, [(shape, BF)], (), (keep[1], over_core(away[1])))
    (own,) = call(pair_kernel, [(shape, F32)], (), (keep[0], over_core(away[0])), (), (sent,))
    own, sent = call(
        middle_kernel,
        [((half, columns), F32), ((half, columns), BF)],
        (),
        (own, over_y(sent)),
        cost=0,
    )
    base_away, base_kept = head_terms(2, (sent,))
    own, *sent = call(
        spread_kernel,
        [((quarter, columns), F32)] + [((quarter, columns), BF)] * 3,
        (),
        (own, over_x(sent)),
        (),
        (base_kept,),
        cost=0,
    )
    met = [flip(v, "dom", 8, 2 * (k + 1)) for k, v in enumerate(sent)]
    rows_half = ent_dev // 2
    (leaving,) = add(1, base_away, [((rows_half, columns), BF)], (sent[0],))
    (kept,) = add(0, base_kept, [((rows_half, columns), F32)], (leaving,), 20)
    arrived = over_core(leaving)
    (own,) = call(
        sum_kernel, [((quarter, columns), BF)], (), (own, *met), (), (kept,), cost=100
    )
    stripes = [own] + [flip(own, "dom", 8, 2 * (k + 1)) for k in range(3)]
    (whole,) = call(
        stack_kernel, [((half, columns), BF)], (), stripes, cost=0
    )
    (both,) = call(both_kernel, [((rows_half, columns), BF)], (), (kept, arrived))
    across = over_y(both)

    y_whole = over_y(whole)
    x_whole = over_x(whole)

    def half_of(which, v):
        return call(
            functools.partial(half_kernel, which), [((half // 2, columns), BF)], (), (v,)
        )[0]

    mine = [whole, x_whole, y_whole]
    mine += [over_y(half_of(0, x_whole)), over_x(half_of(1, y_whole))]
    places = [(0, 0), (1, 0), (2, 0), (3, 0), (3, 2)]
    places += [(4 + index, first) for index, first in places]
    early, late = (0, 1, 2, 5, 6, 7), (3, 4, 8, 9)
    limit = pltpu.CompilerParams(vmem_limit_bytes=40 * 1024 * 1024)
    shape = jax.ShapeDtypeStruct((count, columns, columns), F32)
    entity_grad, relation_grad, token = pl.pallas_call(
        functools.partial(join_kernel, [places[k] for k in early]),
        out_shape=[
            jax.ShapeDtypeStruct((ent_dev, columns), F32),
            shape,
            jax.ShapeDtypeStruct((8, 128), F32),
        ],
        in_specs=[VMEM] * (4 + len(early)),
        out_specs=[FAR, FAR, VMEM],
        scratch_shapes=[
            pltpu.VMEM((2, rows_half, columns), F32),
            pltpu.SemaphoreType.DMA((2,)),
            pltpu.VMEM((len(early), half, columns), F32),
            pltpu.SemaphoreType.DMA((len(early), 4)),
        ],
        compiler_params=limit,
    )(both, over_core(both), across, over_core(across), *(mine[:3] + [over_core(v) for v in mine[:3]]))
    last = [
        call(same_kernel, [(v.shape, BF)], (), (v,), (), (token,))[0] for v in mine[3:]
    ]
    relation_grad = pl.pallas_call(
        functools.partial(operator_kernel, [places[k] for k in late]),
        out_shape=shape,
        in_specs=[VMEM] * len(late) + [FAR],
        out_specs=FAR,
        scratch_shapes=[
            pltpu.VMEM((len(late), half, columns), F32),
            pltpu.SemaphoreType.DMA((len(late), 4)),
        ],
        input_output_aliases={len(late): 0},
        compiler_params=limit,
    )(*last, *[over_core(v) for v in last], relation_grad)
    return entity_grad, relation_grad, loss.reshape(edges)


def solution(mesh):
    special = dict(mesh.shape) == {"dom": 8, "rep": 4}
    return jax.shard_map(
        functools.partial(local, special),
        mesh=mesh,
        in_specs=(
            P("dom", None),
            P(),
            P(("dom", "rep")),
            P(("dom", "rep")),
            P(("dom", "rep"), None),
            P(("dom", "rep")),
            P("dom"),
        ),
        out_specs=(P("dom", None), P(), P(("dom", "rep"))),
        check_vma=False,
    )
```
